512 devices in a mesh: row: 32 (over z_hi, y, core), res: 16 (over x, z_lo).
Axes of the slice: x: 4, y: 4, z: 16 (z_hi: 4, z_lo: 4; z = z_hi * 4 + z_lo), core: 2. Of those that a mesh axis runs over, the one named last changes fastest.
Arguments:
- queries: bfloat16 [128, 1024, 384], P('row', 'res'), may hold values from -64 to 64
- keys: bfloat16 [128, 1024, 384], P('row', 'res'), may hold values from -4 to 4
- values: bfloat16 [128, 1024, 384], P('row', 'res'), may hold values from -36 to 36
- out_weight: bfloat16 [384, 768], replicated, may hold values from -0.3125 to 0.3125
- grad_out: bfloat16 [128, 1024, 768], P('row', 'res'), may hold values from -24 to 24
Outputs:
- mixed_out: bfloat16 [128, 1024, 768], P('row', 'res')
- grad_query: bfloat16 [128, 1024, 384], P('row', 'res')
- grad_key: bfloat16 [128, 1024, 384], P('row', 'res')
- grad_value: bfloat16 [128, 1024, 384], P('row', 'res')
The draws below stay inside these ranges and needn't reach their ends.
All inputs are finite; a program needn't handle non-finite values.
Results may differ from the reference program's by a relative error of at most 0.013.
Values may be sent and summed in bfloat16 or wider, within the bound.
No kernel may reach another device: no remote copies, remote signals or barrier semaphores. Data moves between devices by JAX's collectives and lax.ppermute only.
A program may use at most 64 MiB of HBM per device.

```python
import math
import jax
import jax.numpy as jnp
from jax import lax

D = 768
HEADS = 6
HD = 64
SEQS = 128
L = 1024
HH = 384


def base_keys(key):
    return jax.random.truncated_normal(key, -4.0, 4.0, (SEQS, L, HH), jnp.float32)


def draw_keys(key, part):
    field = base_keys(key)
    return field.astype(jnp.bfloat16)


def draw_queries(key, part):
    own_key = jax.random.fold_in(key, 23)
    field = jax.random.truncated_normal(own_key, -4.0, 4.0, (SEQS, L, HH), jnp.float32)
    return field.astype(jnp.bfloat16)


def levels(stream_key, dims, cuts, smallest, top_value):
    loudness = 1.0
    for position, shards_of in cuts:
        draws = jax.random.uniform(jax.random.fold_in(jax.random.fold_in(stream_key, 6), position), (shards_of,), jnp.float32, smallest / len(cuts), top_value / len(cuts))
        loudness = loudness * jnp.repeat(jnp.exp(draws), dims[position] // shards_of).reshape((-1,) + (1,) * (len(dims) - 1 - position))
    return loudness


def centred(rng, extent, spread, limit, split=(), held_as=jnp.bfloat16):
    values = jax.random.normal(rng, extent, jnp.float32) * spread
    if len(split) > 0:
        values = levels(rng, extent, split, -0.22, 0.18) * values
    return jnp.clip(values, min=-limit, max=limit).astype(held_as)


def setup_inputs(seed: int = 0) -> dict:
    streams_of = jax.random.split(jax.random.key(seed), 6)
    queries = draw_queries(jax.random.fold_in(streams_of[5], 71), 0)
    keys = draw_keys(jax.random.fold_in(streams_of[5], 71), 0)
    values = centred(streams_of[2], (SEQS, L, HH), 6.0, 36.0, ((0, 32), (1, 16)))
    out_weight = centred(streams_of[3], (HH, D), HH ** -0.5, 0.3125)
    grad_out = centred(streams_of[4], (SEQS, L, D), 4.0, 24.0, ((0, 32), (1, 16)))
    return dict(queries=queries, keys=keys, values=values, out_weight=out_weight, grad_out=grad_out)


def split_heads(array):
    return array.astype(jnp.float32).reshape(array.shape[0], array.shape[1], HEADS, HD)

def reference(queries, keys, values, out_weight, grad_out):
    logit_scale = 1.0 / math.sqrt(HD * SEQS)
    query_heads = split_heads(queries)
    key_heads = split_heads(keys)
    value_heads = split_heads(values)
    logits = jnp.einsum('sihd,sjhd->hij', query_heads, key_heads) * logit_scale
    top = lax.optimization_barrier(jnp.max(logits, axis=-1, keepdims=True))
    expo = jnp.exp(logits - top)
    weights = expo / lax.optimization_barrier(jnp.sum(expo, axis=-1, keepdims=True))
    weights16 = weights.astype(jnp.bfloat16)
    weights_wide = weights16.astype(jnp.float32)
    attended = jnp.einsum('hij,sjhd->sihd', weights_wide, value_heads).astype(jnp.bfloat16)
    mixed_out = jnp.dot(attended.reshape(SEQS * L, HH), out_weight, preferred_element_type=jnp.float32)
    mixed_out = mixed_out.astype(jnp.bfloat16).reshape(SEQS, L, D)
    grad_attended = lax.dot_general(grad_out.reshape(SEQS * L, D), out_weight, (((1,), (1,)), ((), ())), preferred_element_type=jnp.float32)
    grad_attended = grad_attended.astype(jnp.bfloat16).reshape(SEQS, L, HH)
    grad_heads = split_heads(grad_attended)
    grad_weights = jnp.einsum('sihd,sjhd->hij', grad_heads, value_heads)
    grad_scores = weights * (grad_weights - lax.optimization_barrier(jnp.sum(weights * grad_weights, axis=-1, keepdims=True)))
    grad_scores = grad_scores.astype(jnp.bfloat16).astype(jnp.float32)
    grad_query = (jnp.einsum('hij,sjhd->sihd', grad_scores, key_heads) * logit_scale).astype(jnp.bfloat16)
    grad_key = (jnp.einsum('hij,sihd->sjhd', grad_scores, query_heads) * logit_scale).astype(jnp.bfloat16)
    grad_value = jnp.einsum('hij,sihd->sjhd', weights_wide, grad_heads).astype(jnp.bfloat16)
    return (mixed_out, grad_query.reshape(SEQS, L, HH), grad_key.reshape(SEQS, L, HH), grad_value.reshape(SEQS, L, HH))
```

```python
import math

import jax
import jax.numpy as jnp
from jax import lax
from jax.experimental import pallas as pl
from jax.experimental.pallas import tpu as pltpu
from jax.sharding import Mesh, PartitionSpec as P

HEADS = 6
PAIRS = 3
F32 = jnp.float32
BF16 = jnp.bfloat16
VMEM = 40 * 1024 * 1024


def params():
    return pltpu.CompilerParams(vmem_limit_bytes=VMEM)


def exchange(blocks, axis):
    return lax.all_to_all(blocks, axis, 0, 0, tiled=True)


def prep_kernel(q_ref, k_ref, v_ref, w_ref, go_ref, kv_ref, qg_ref):
    seqs, res, width = q_ref.shape
    for s in range(seqs):
        ga = lax.dot_general(
            go_ref[s], w_ref[...], (((1,), (1,)), ((), ())), preferred_element_type=F32
        ).astype(BF16)
        for n in range(kv_ref.shape[0]):
            qg_ref[n, 1, s] = ga
    for n in range(kv_ref.shape[0]):
        kv_ref[n, 0] = k_ref[...]
        kv_ref[n, 1] = v_ref[...]
        qg_ref[n, 0] = q_ref[...]


def columns(ref, which):
    n, _, seqs, res, lanes = ref.shape
    return jnp.concatenate([ref[:, which, s].reshape(n * res, lanes) for s in range(seqs)], axis=1)


def head_mask(shape, head):
    lane = lax.broadcasted_iota(jnp.int32, shape, 1)
    return ((lane // 64) % 2) == head


def product_kernel(kv_ref, qg_ref, out_ref):
    for which in range(2):
        left = columns(qg_ref, which)
        right = columns(kv_ref, which)
        for head in range(2):
            own = jnp.where(head_mask(left.shape, head), left, jnp.zeros_like(left))
            full = lax.dot_general(own, right, (((1,), (1,)), ((), ())), preferred_element_type=F32)
            out_ref[head, :, 0, which] = full.reshape(out_ref.shape[1], out_ref.shape[4], out_ref.shape[5])


def stats_kernel(scale, part_ref, e_ref, g_ref, stat_ref):
    total = part_ref[0] + part_ref[1] + part_ref[2] + part_ref[3]
    logits = total[:, 0] * scale
    grads = total[:, 1]
    top = jnp.max(logits, axis=-1, keepdims=True)
    expo = jnp.exp(logits - top)
    e_ref[...] = expo
    g_ref[...] = grads
    norm = jnp.sum(expo, axis=-1, keepdims=True)
    dot = jnp.sum(expo * grads, axis=-1, keepdims=True)
    lane = lax.broadcasted_iota(jnp.int32, stat_ref.shape[1:], 2)
    stat = jnp.where(lane == 0, top, jnp.where(lane == 1, norm, dot))
    for n in range(stat_ref.shape[0]):
        stat_ref[n] = stat


def weights_kernel(own_ref, stat_ref, e_ref, g_ref, out_ref):
    tops = stat_ref[:, :, :, 0:1]
    top = jnp.max(tops, axis=0)
    parts = jnp.exp(tops - top[None])
    norm = jnp.sum(parts * stat_ref[:, :, :, 1:2], axis=0)
    dot = jnp.sum(parts * stat_ref[:, :, :, 2:3], axis=0) / norm
    weights = e_ref[...] * (jnp.exp(own_ref[0, :, :, 0:1] - top) / norm)
    scores = weights * (g_ref[...] - dot)
    for n in range(out_ref.shape[0]):
        out_ref[n, 0] = weights.astype(BF16)
        out_ref[n, 1] = scores.astype(BF16)


def output_kernel(scale, ws_ref, kv_ref, qg_ref, row_ref, col_ref):
    def heads(which):
        return [ws_ref[c, :, :, which, 0].reshape(256, 256) for c in range(2)]

    def product(mats, side, contract):
        both = [
            lax.dot_general(m, side, (((contract,), (0,)), ((), ())), preferred_element_type=F32)
            for m in mats
        ]
        return jnp.where(head_mask(both[0].shape, 0), both[0], both[1])

    def put(ref, which, value):
        n, _, seqs, res, lanes = ref.shape
        value = value.astype(BF16)
        for s in range(seqs):
            ref[:, which, s] = value[:, s * lanes : (s + 1) * lanes].reshape(n, res, lanes)

    weights, scores = heads(0), heads(1)
    put(row_ref, 0, product(weights, columns(kv_ref, 1), 1))
    put(row_ref, 1, product(scores, columns(kv_ref, 0), 1) * scale)
    put(col_ref, 0, product(weights, columns(qg_ref, 1), 0))
    put(col_ref, 1, product(scores, columns(qg_ref, 0), 0) * scale)


def total_of(ref, which, s):
    parts = [ref[n, which, s].astype(F32) for n in range(ref.shape[0])]
    return ((parts[0] + parts[1]) + (parts[2] + parts[3])).astype(BF16)


def finish_kernel(row_ref, col_ref, w_ref, mixed_ref, gq_ref, gk_ref, gv_ref):
    for s in range(mixed_ref.shape[0]):
        attended = total_of(row_ref, 0, s)
        mixed_ref[s] = jnp.dot(attended, w_ref[...], preferred_element_type=F32).astype(BF16)
        gq_ref[s] = total_of(row_ref, 1, s)
        gv_ref[s] = total_of(col_ref, 0, s)
        gk_ref[s] = total_of(col_ref, 1, s)


def on_device(queries, keys, values, out_weight, grad_out):
    seqs, res, width = queries.shape
    model_dim = out_weight.shape[1]
    scale = 1.0 / math.sqrt(width // HEADS * seqs * 32)
    gathered = jax.ShapeDtypeStruct((4, 2, seqs, res, width), BF16)
    kv_send, qg_send = pl.pallas_call(
        prep_kernel, out_shape=(gathered, gathered), compiler_params=params(), name="prep"
    )(queries, keys, values, out_weight, grad_out)
    kv = exchange(kv_send, "x")
    qg = exchange(qg_send, "zl")

    slab = pl.BlockSpec((4, 2, seqs, res, 128), lambda p: (0, 0, 0, 0, p))
    partial = pl.pallas_call(
        product_kernel,
        grid=(PAIRS,),
        in_specs=[slab, slab],
        out_specs=pl.BlockSpec((2, 4, 1, 2, 64, 256), lambda p: (0, 0, p, 0, 0, 0)),
        out_shape=jax.ShapeDtypeStruct((2, 4, PAIRS, 2, 64, 256), F32),
        compiler_params=params(),
        name="products",
    )(kv, qg)
    partial = exchange(partial, "c")
    partial = partial[0] + partial[1]
    partial = exchange(partial, "y")
    partial = jnp.sum(partial, axis=0).reshape(PAIRS, 2, 4, 16, 256)
    partial = exchange(jnp.transpose(partial, (2, 0, 1, 3, 4)), "zh")

    tile = jax.ShapeDtypeStruct((PAIRS, 16, 256), F32)
    e, g, stat = pl.pallas_call(
        lambda *refs: stats_kernel(scale, *refs),
        out_shape=(tile, tile, jax.ShapeDtypeStruct((4, PAIRS, 16, 128), F32)),
        compiler_params=params(),
        name="stats",
    )(partial)
    stats = exchange(stat, "zl")
    ws = pl.pallas_call(
        weights_kernel,
        out_shape=jax.ShapeDtypeStruct((4, 2, PAIRS, 16, 256), BF16),
        compiler_params=params(),
        name="weights",
    )(stat, stats, e, g)
    ws = exchange(ws, "zh")
    ws = exchange(jnp.broadcast_to(ws[None], (4,) + ws.shape), "y")
    ws = exchange(jnp.broadcast_to(ws[None], (2,) + ws.shape), "c")

    row, col = pl.pallas_call(
        lambda *refs: output_kernel(scale, *refs),
        grid=(PAIRS,),
        in_specs=[pl.BlockSpec((2, 4, 4, 2, 1, 16, 256), lambda p: (0, 0, 0, 0, p, 0, 0)), slab, slab],
        out_specs=[slab, slab],
        out_shape=(gathered, gathered),
        compiler_params=params(),
        name="outputs",
    )(ws, kv, qg)
    row = exchange(row, "zl")
    col = exchange(col, "x")
    grad = jax.ShapeDtypeStruct((seqs, res, width), BF16)
    return pl.pallas_call(
        finish_kernel,
        out_shape=(jax.ShapeDtypeStruct((seqs, res, model_dim), BF16), grad, grad, grad),
        compiler_params=params(),
        name="finish",
    )(row, col, out_weight)


def solution(mesh):
    grid = Mesh(mesh.devices.reshape(4, 4, 2, 4, 4), ("zh", "y", "c", "x", "zl"))
    placed = P(("zh", "y", "c"), ("x", "zl"), None)
    return jax.shard_map(
        on_device,
        mesh=grid,
        in_specs=(placed, placed, placed, P(), placed),
        out_specs=(placed, placed, placed, placed),
        check_vma=False,
    )
```

```python
import math

import jax
import jax.numpy as jnp
from jax import lax
from jax.experimental import pallas as pl
from jax.experimental.pallas import tpu as pltpu
from jax.sharding import Mesh, PartitionSpec as P

HEADS = 6
PAIRS = 3
F32 = jnp.float32
BF16 = jnp.bfloat16
VMEM = 40 * 1024 * 1024


def params():
    return pltpu.CompilerParams(vmem_limit_bytes=VMEM)


def exchange(blocks, axis):
    return lax.all_to_all(blocks, axis, 0, 0, tiled=True)


def shift(block, axis, by):
    n = lax.axis_size(axis)
    return lax.ppermute(block, axis, [(i, (i + by) % n) for i in range(n)])


def prep_kernel(q_ref, k_ref, v_ref, w_ref, go_ref, kv_ref, qg_ref):
    kv_ref[0] = k_ref[...]
    kv_ref[1] = v_ref[...]
    for s in range(q_ref.shape[0]):
        ga = lax.dot_general(
            go_ref[s], w_ref[...], (((1,), (1,)), ((), ())), preferred_element_type=F32
        ).astype(BF16)
        for n in range(qg_ref.shape[0]):
            qg_ref[n, 0, s] = q_ref[s]
            qg_ref[n, 1, s] = ga


def columns(refs, which):
    seqs = refs[0].shape[1]
    rows = [jnp.concatenate([ref[which, s] for s in range(seqs)], axis=1) for ref in refs]
    return jnp.concatenate(rows, axis=0)


def head_mask(shape, head):
    lane = lax.broadcasted_iota(jnp.int32, shape, 1)
    return ((lane // 64) % 2) == head


def product_kernel(core_ref, *refs):
    kv_refs, qg_ref, keep_ref, send_ref = refs[:4], refs[4], refs[5], refs[6]
    qg_refs = [qg_ref.at[n] for n in range(4)]
    first = core_ref[0] == 0
    for which in range(2):
        left = columns(qg_refs, which)
        right = columns(kv_refs, which)
        both = []
        for head in range(2):
            own = jnp.where(head_mask(left.shape, head), left, jnp.zeros_like(left))
            both.append(
                lax.dot_general(own, right, (((1,), (1,)), ((), ())), preferred_element_type=F32)
            )
        shape = (keep_ref.shape[0],) + keep_ref.shape[3:]
        keep_ref[:, 0, which] = jnp.where(first, both[0], both[1]).reshape(shape)
        send_ref[:, 0, which] = jnp.where(first, both[1], both[0]).reshape(shape)


def rows_kernel(part_ref, out_ref):
    total = (part_ref[0] + part_ref[1]) + (part_ref[2] + part_ref[3])
    for n in range(16):
        for p in range(PAIRS):
            for which in range(2):
                at = (which * PAIRS + p) * 4
                out_ref[n, at : at + 4] = total[p, which, n * 4 : n * 4 + 4]


def softmax_kernel(scale, part_ref, out_ref):
    tiles = []
    for col in range(4):
        parts = [part_ref[n * 4 + col] for n in range(4)]
        tiles.append((parts[0] + parts[1]) + (parts[2] + parts[3]))
    total = jnp.concatenate(tiles, axis=1)
    logits = total[:12] * scale
    grads = total[12:]
    expo = jnp.exp(logits - jnp.max(logits, axis=-1, keepdims=True))
    weights = expo / jnp.sum(expo, axis=-1, keepdims=True)
    scores = weights * (grads - jnp.sum(weights * grads, axis=-1, keepdims=True))
    pad = jnp.zeros((4, weights.shape[1]), F32)
    full = jnp.concatenate([weights, pad, scores, pad], axis=0).astype(BF16)
    for n in range(16):
        col = n % 4
        out_ref[n] = full[:, col * 256 : (col + 1) * 256]


def unpack_kernel(ws_ref, out_ref, rows_ref):
    for n in range(16):
        block = ws_ref[n].astype(F32)
        for which in range(2):
            for p in range(PAIRS):
                at = which * 16 + p * 4
                rows_ref[which, p, n * 4 : n * 4 + 4] = block[at : at + 4]
    full = rows_ref[...].astype(BF16)
    for n in range(out_ref.shape[0]):
        out_ref[n] = full


def output_kernel(scale, core_ref, mine_ref, other_ref, *refs):
    kv_refs, qg_ref, row_ref, col_refs = refs[:4], refs[4], refs[5], refs[6:10]
    qg_refs = [qg_ref.at[n] for n in range(4)]
    row_refs = [row_ref.at[n] for n in range(4)]
    first = core_ref[0] == 0

    def heads(which):
        mine = mine_ref[:, which, 0].reshape(256, 256)
        other = other_ref[:, which, 0].reshape(256, 256)
        return jnp.where(first, mine, other), jnp.where(first, other, mine)

    def product(mats, side, contract):
        both = [
            lax.dot_general(m, side, (((contract,), (0,)), ((), ())), preferred_element_type=F32)
            for m in mats
        ]
        return jnp.where(head_mask(both[0].shape, 0), both[0], both[1])

    def put(outs, which, value):
        value = value.astype(BF16)
        for n, ref in enumerate(outs):
            _, seqs, res, lanes = ref.shape
            for s in range(seqs):
                ref[which, s] = value[n * res : (n + 1) * res, s * lanes : (s + 1) * lanes]

    weights, scores = heads(0), heads(1)
    put(row_refs, 0, product(weights, columns(kv_refs, 1), 1))
    put(row_refs, 1, product(scores, columns(kv_refs, 0), 1) * scale)
    put(col_refs, 0, product(weights, columns(qg_refs, 1), 0))
    put(col_refs, 1, product(scores, columns(qg_refs, 0), 0) * scale)


def total_of(refs, which, s):
    parts = [ref[which, s].astype(F32) for ref in refs]
    return ((parts[0] + parts[1]) + (parts[2] + parts[3])).astype(BF16)


def finish_kernel(row_ref, *refs):
    col_refs, (w_ref, mixed_ref, gq_ref, gk_ref, gv_ref) = refs[:4], refs[4:]
    row_refs = [row_ref.at[n] for n in range(4)]
    for s in range(mixed_ref.shape[0]):
        attended = total_of(row_refs, 0, s)
        mixed_ref[s] = jnp.dot(attended, w_ref[...], preferred_element_type=F32).astype(BF16)
        gq_ref[s] = total_of(row_refs, 1, s)
        gv_ref[s] = total_of(col_refs, 0, s)
        gk_ref[s] = total_of(col_refs, 1, s)


def on_device(queries, keys, values, out_weight, grad_out):
    seqs, res, width = queries.shape
    model_dim = out_weight.shape[1]
    scale = 1.0 / math.sqrt(width // HEADS * seqs * 32)
    core = lax.axis_index("c").astype(jnp.int32).reshape(1)
    block = jax.ShapeDtypeStruct((2, seqs, res, width), BF16)
    blocks = jax.ShapeDtypeStruct((4, 2, seqs, res, width), BF16)
    smem = pl.BlockSpec(memory_space=pltpu.SMEM)

    kv_own, qg_send = pl.pallas_call(
        prep_kernel, out_shape=(block, blocks), compiler_params=params(), name="prep"
    )(queries, keys, values, out_weight, grad_out)
    qg = exchange(qg_send, "zl")
    kv = [kv_own] + [shift(kv_own, "x", by) for by in (1, 2, 3)]

    slab = pl.BlockSpec((2, seqs, res, 128), lambda p: (0, 0, 0, p))
    slabs = pl.BlockSpec((4, 2, seqs, res, 128), lambda p: (0, 0, 0, 0, p))
    half = jax.ShapeDtypeStruct((4, PAIRS, 2, 64, 256), F32)
    half_slab = pl.BlockSpec((4, 1, 2, 64, 256), lambda p: (0, p, 0, 0, 0))
    keep, send = pl.pallas_call(
        product_kernel,
        grid=(PAIRS,),
        in_specs=[smem] + [slab] * 4 + [slabs],
        out_specs=[half_slab, half_slab],
        out_shape=(half, half),
        compiler_params=params(),
        name="products",
    )(core, *kv, qg)
    partial = exchange(keep + shift(send, "c", 1), "y")
    partial = pl.pallas_call(
        rows_kernel,
        out_shape=jax.ShapeDtypeStruct((16, 8 * PAIRS, 256), F32),
        compiler_params=params(),
        name="rows",
    )(partial)
    partial = exchange(partial, ("zh", "zl"))
    ws = pl.pallas_call(
        lambda *refs: softmax_kernel(scale, *refs),
        out_shape=jax.ShapeDtypeStruct((16, 32, 256), BF16),
        compiler_params=params(),
        name="softmax",
    )(partial)
    ws = exchange(ws, ("zh", "zl"))
    ws = pl.pallas_call(
        unpack_kernel,
        out_shape=jax.ShapeDtypeStruct((4, 2, PAIRS, 64, 256), BF16),
        scratch_shapes=[pltpu.VMEM((2, PAIRS, 64, 256), F32)],
        compiler_params=params(),
        name="unpack",
    )(ws)
    mine = exchange(ws, "y")
    other = shift(mine, "c", 1)

    ws_slab = pl.BlockSpec((4, 2, 1, 64, 256), lambda p: (0, 0, p, 0, 0))
    row, *cols = pl.pallas_call(
        lambda *refs: output_kernel(scale, *refs),
        grid=(PAIRS,),
        in_specs=[smem, ws_slab, ws_slab] + [slab] * 4 + [slabs],
        out_specs=[slabs] + [slab] * 4,
        out_shape=(blocks,) + (block,) * 4,
        compiler_params=params(),
        name="outputs",
    )(core, mine, other, *kv, qg)
    row = exchange(row, "zl")
    cols = [cols[0]] + [shift(cols[by], "x", -by) for by in (1, 2, 3)]
    grad = jax.ShapeDtypeStruct((seqs, res, width), BF16)
    return pl.pallas_call(
        finish_kernel,
        out_shape=(jax.ShapeDtypeStruct((seqs, res, model_dim), BF16), grad, grad, grad),
        compiler_params=params(),
        name="finish",
    )(row, *cols, out_weight)


def solution(mesh):
    grid = Mesh(mesh.devices.reshape(4, 4, 2, 4, 4), ("zh", "y", "c", "x", "zl"))
    placed = P(("zh", "y", "c"), ("x", "zl"), None)
    return jax.shard_map(
        on_device,
        mesh=grid,
        in_specs=(placed, placed, placed, P(), placed),
        out_specs=(placed, placed, placed, placed),
        check_vma=False,
    )
```

```python
import math

import jax
import jax.numpy as jnp
from jax import lax
from jax.experimental import pallas as pl
from jax.experimental.pallas import tpu as pltpu
from jax.sharding import Mesh, PartitionSpec as P

HEADS = 6
PAIRS = 3
F32 = jnp.float32
BF16 = jnp.bfloat16
VMEM = 16 * 1024 * 1024


def params():
    return pltpu.CompilerParams(vmem_limit_bytes=VMEM)


def exchange(blocks, axis):
    return lax.all_to_all(blocks, axis, 0, 0, tiled=True)


def shift(block, axis, by):
    n = lax.axis_size(axis)
    return lax.ppermute(block, axis, [(i, (i + by) % n) for i in range(n)])


def grad_kernel(w_ref, go_ref, out_ref):
    for s in range(go_ref.shape[0]):
        ga = lax.dot_general(
            go_ref[s], w_ref[...], (((1,), (1,)), ((), ())), preferred_element_type=F32
        ).astype(BF16)
        for n in range(out_ref.shape[0]):
            out_ref[n, s] = ga


def columns(refs):
    seqs = refs[0].shape[0]
    rows = [jnp.concatenate([ref[s] for s in range(seqs)], axis=1) for ref in refs]
    return jnp.concatenate(rows, axis=0)


def head_mask(shape, head):
    lane = lax.broadcasted_iota(jnp.int32, shape, 1)
    return ((lane // 64) % 2) == head


def product_kernel(core_ref, own_ref, one_ref, two_ref, three_ref, left_ref, keep_ref, send_ref):
    first = core_ref[0] == 0
    left = columns([left_ref.at[n] for n in range(4)])
    right = columns([own_ref, one_ref, two_ref, three_ref])
    both = []
    for head in range(2):
        own = jnp.where(head_mask(left.shape, head), left, jnp.zeros_like(left))
        both.append(lax.dot_general(own, right, (((1,), (1,)), ((), ())), preferred_element_type=F32))
    shape = (keep_ref.shape[0],) + keep_ref.shape[2:]
    keep_ref[:, 0] = jnp.where(first, both[0], both[1]).reshape(shape)
    send_ref[:, 0] = jnp.where(first, both[1], both[0]).reshape(shape)


def split_kernel(core_ref, keep_ref, got_ref, own_ref, one_ref, two_ref, three_ref):
    for by, ref in enumerate((own_ref, one_ref, two_ref, three_ref)):
        at = lax.rem(core_ref[1] + by, 4)
        ref[...] = keep_ref[at] + got_ref[at]


def rows_kernel(own_ref, one_ref, two_ref, three_ref, grad_ref, out_ref):
    logits = (own_ref[...] + one_ref[...]) + (two_ref[...] + three_ref[...])
    grads = (grad_ref[0] + grad_ref[1]) + (grad_ref[2] + grad_ref[3])
    for n in range(16):
        for p in range(PAIRS):
            out_ref[n, p * 4 : p * 4 + 4] = logits[p, n * 4 : n * 4 + 4]
            out_ref[n, 12 + p * 4 : 16 + p * 4] = grads[p, n * 4 : n * 4 + 4]


def softmax_kernel(scale, part_ref, out_ref):
    tiles = []
    for col in range(4):
        parts = [part_ref[n * 4 + col] for n in range(4)]
        tiles.append((parts[0] + parts[1]) + (parts[2] + parts[3]))
    total = jnp.concatenate(tiles, axis=1)
    logits = total[:12] * scale
    grads = total[12:]
    expo = jnp.exp(logits - jnp.max(logits, axis=-1, keepdims=True))
    weights = expo / jnp.sum(expo, axis=-1, keepdims=True)
    scores = weights * (grads - jnp.sum(weights * grads, axis=-1, keepdims=True))
    full = jnp.concatenate([weights, scores], axis=0)
    for col in range(4):
        at = col * 256
        tile = jnp.concatenate([full[:, at : at + 128], full[:, at + 128 : at + 256]], axis=0).astype(BF16)
        for n in range(col, 16, 4):
            out_ref[n] = tile


def unpack_kernel(ws_ref, out_ref, rows_ref):
    for n in range(16):
        block = ws_ref[n].astype(F32)
        for which in range(2):
            for p in range(PAIRS):
                at = which * 12 + p * 4
                rows_ref[which, p, n * 4 : n * 4 + 4, 0:128] = block[at : at + 4]
                rows_ref[which, p, n * 4 : n * 4 + 4, 128:256] = block[24 + at : 28 + at]
    full = rows_ref[...].astype(BF16)
    for n in range(out_ref.shape[0]):
        out_ref[n] = full


def output_kernel(scale, core_ref, mine_ref, other_ref, own_ref, one_ref, two_ref, three_ref, left_ref, row_ref, *col_refs):
    first = core_ref[0] == 0
    mine = mine_ref[:, 0, 0].reshape(256, 256)
    other = other_ref[:, 0, 0].reshape(256, 256)
    mats = (jnp.where(first, mine, other), jnp.where(first, other, mine))

    def product(side, contract):
        both = [
            lax.dot_general(m, side, (((contract,), (0,)), ((), ())), preferred_element_type=F32)
            for m in mats
        ]
        return (jnp.where(head_mask(both[0].shape, 0), both[0], both[1]) * scale).astype(BF16)

    def put(outs, value):
        for n, ref in enumerate(outs):
            seqs, res, lanes = ref.shape
            for s in range(seqs):
                ref[s] = value[n * res : (n + 1) * res, s * lanes : (s + 1) * lanes]

    put([row_ref.at[n] for n in range(4)], product(columns([own_ref, one_ref, two_ref, three_ref]), 1))
    put(col_refs, product(columns([left_ref.at[n] for n in range(4)]), 0))


def total_of(refs, s):
    parts = [ref[s].astype(F32) for ref in refs]
    return ((parts[0] + parts[1]) + (parts[2] + parts[3])).astype(BF16)


def finish_weights_kernel(w_ref, row_ref, own_ref, one_ref, two_ref, three_ref, mixed_ref, gv_ref):
    for s in range(mixed_ref.shape[0]):
        attended = total_of([row_ref.at[n] for n in range(4)], s)
        mixed_ref[s] = jnp.dot(attended, w_ref[...], preferred_element_type=F32).astype(BF16)
        gv_ref[s] = total_of((own_ref, one_ref, two_ref, three_ref), s)


def finish_scores_kernel(row_ref, own_ref, one_ref, two_ref, three_ref, gq_ref, gk_ref):
    for s in range(gq_ref.shape[0]):
        gq_ref[s] = total_of([row_ref.at[n] for n in range(4)], s)
        gk_ref[s] = total_of((own_ref, one_ref, two_ref, three_ref), s)


def on_device(queries, keys, values, out_weight, grad_out):
    seqs, res, width = queries.shape
    model_dim = out_weight.shape[1]
    scale = 1.0 / math.sqrt(width // HEADS * seqs * 32)
    place = jnp.stack([lax.axis_index("c"), lax.axis_index("y")]).astype(jnp.int32)
    block = jax.ShapeDtypeStruct((seqs, res, width), BF16)
    blocks = jax.ShapeDtypeStruct((4, seqs, res, width), BF16)
    half = jax.ShapeDtypeStruct((4, PAIRS, 64, 256), F32)
    quarter = jax.ShapeDtypeStruct((PAIRS, 64, 256), F32)
    smem = pl.BlockSpec(memory_space=pltpu.SMEM)
    slab = pl.BlockSpec((seqs, res, 128), lambda p: (0, 0, p))
    slabs = pl.BlockSpec((4, seqs, res, 128), lambda p: (0, 0, 0, p))
    half_slab = pl.BlockSpec((4, 1, 64, 256), lambda p: (0, p, 0, 0))

    def products(rights, left, name):
        return pl.pallas_call(
            product_kernel,
            grid=(PAIRS,),
            in_specs=[smem] + [slab] * 4 + [slabs],
            out_specs=[half_slab, half_slab],
            out_shape=(half, half),
            compiler_params=params(),
            name=name,
        )(place, *rights, left)

    left_q = exchange(jnp.broadcast_to(queries[None], blocks.shape), "zl")
    rights_k = [keys] + [shift(keys, "x", by) for by in (1, 2, 3)]
    grads = pl.pallas_call(grad_kernel, out_shape=blocks, compiler_params=params(), name="grad_attended")(
        out_weight, grad_out
    )
    rights_v = [values] + [shift(values, "x", by) for by in (1, 2, 3)]
    grads, left_q, rights_k, rights_v = lax.optimization_barrier((grads, left_q, rights_k, rights_v))
    left_g = exchange(grads, "zl")

    keep, send = products(rights_k, left_q, "logits")
    pieces = pl.pallas_call(
        split_kernel,
        in_specs=[smem] + [pl.BlockSpec(memory_space=pltpu.VMEM)] * 2,
        out_shape=(quarter,) * 4,
        compiler_params=params(),
        name="split",
    )(place, keep, shift(send, "c", 1))
    pieces = [pieces[0]] + [shift(pieces[by], "y", by) for by in (1, 2, 3)]

    left_g, pieces = lax.optimization_barrier((left_g, pieces))
    keep, send = products(rights_v, left_g, "weight_grads")
    partial = exchange(keep + shift(send, "c", 1), "y")
    partial = pl.pallas_call(
        rows_kernel,
        out_shape=jax.ShapeDtypeStruct((16, 8 * PAIRS, 256), F32),
        compiler_params=params(),
        name="rows",
    )(*pieces, partial)
    partial = exchange(partial, ("zh", "zl"))
    ws = pl.pallas_call(
        lambda *refs: softmax_kernel(scale, *refs),
        out_shape=jax.ShapeDtypeStruct((16, 48, 128), BF16),
        compiler_params=params(),
        name="softmax",
    )(partial)
    ws = exchange(ws, ("zh", "zl"))
    ws = pl.pallas_call(
        unpack_kernel,
        out_shape=jax.ShapeDtypeStruct((4, 2, PAIRS, 64, 256), BF16),
        scratch_shapes=[pltpu.VMEM((2, PAIRS, 64, 256), F32)],
        compiler_params=params(),
        name="unpack",
    )(ws)
    mine = exchange(ws, "y")
    other = shift(mine, "c", 1)

    def outputs(which, factor, rights, left, name):
        ws_slab = pl.BlockSpec((4, 1, 1, 64, 256), lambda p: (0, which, p, 0, 0))
        return pl.pallas_call(
            lambda *refs: output_kernel(factor, *refs),
            grid=(PAIRS,),
            in_specs=[smem, ws_slab, ws_slab] + [slab] * 4 + [slabs],
            out_specs=[slabs] + [slab] * 4,
            out_shape=(blocks,) + (block,) * 4,
            compiler_params=params(),
            name=name,
        )(place, mine, other, *rights, left)

    row_w, *cols_w = outputs(0, 1.0, rights_v, left_g, "weights_out")
    row_s, *cols_s = outputs(1, scale, rights_k, left_q, "scores_out")
    row_w = exchange(row_w, "zl")
    cols_w = [cols_w[0]] + [shift(cols_w[by], "x", -by) for by in (1, 2, 3)]
    row_s, row_w, cols_w = lax.optimization_barrier((row_s, row_w, cols_w))
    row_s = exchange(row_s, "zl")
    cols_s = [cols_s[0]] + [shift(cols_s[by], "x", -by) for by in (1, 2, 3)]
    mixed, grad_value = pl.pallas_call(
        finish_weights_kernel,
        out_shape=(jax.ShapeDtypeStruct((seqs, res, model_dim), BF16), block),
        compiler_params=params(),
        name="finish_weights",
    )(out_weight, row_w, *cols_w)
    grad_query, grad_key = pl.pallas_call(
        finish_scores_kernel, out_shape=(block, block), compiler_params=params(), name="finish_scores"
    )(row_s, *cols_s)
    return mixed, grad_query, grad_key, grad_value


def solution(mesh):
    grid = Mesh(mesh.devices.reshape(4, 4, 2, 4, 4), ("zh", "y", "c", "x", "zl"))
    placed = P(("zh", "y", "c"), ("x", "zl"), None)
    return jax.shard_map(
        on_device,
        mesh=grid,
        in_specs=(placed, placed, placed, P(), placed),
        out_specs=(placed, placed, placed, placed),
        check_vma=False,
    )
```

```python
import math

import jax
import jax.numpy as jnp
from jax import lax
from jax.experimental import pallas as pl
from jax.experimental.pallas import tpu as pltpu
from jax.sharding import Mesh, PartitionSpec as P

HEADS = 6
PAIRS = 3
F32 = jnp.float32
BF16 = jnp.bfloat16
VMEM = 16 * 1024 * 1024


def params():
    return pltpu.CompilerParams(vmem_limit_bytes=VMEM)


def exchange(blocks, axis):
    return lax.all_to_all(blocks, axis, 0, 0, tiled=True)


def shift(block, axis, by):
    n = lax.axis_size(axis)
    return lax.ppermute(block, axis, [(i, (i + by) % n) for i in range(n)])


def prep_kernel(q_ref, k_ref, v_ref, kv_ref, send_ref, sems):
    copies = [
        pltpu.make_async_copy(k_ref, kv_ref.at[0], sems.at[0]),
        pltpu.make_async_copy(v_ref, kv_ref.at[1], sems.at[1]),
    ]
    for n in range(4):
        copies.append(pltpu.make_async_copy(q_ref, send_ref.at[n], sems.at[2 + n]))
    for copy in copies:
        copy.start()
    for copy in copies:
        copy.wait()


def grad_kernel(w_ref, go_ref, out_ref):
    for s in range(go_ref.shape[0]):
        ga = lax.dot_general(
            go_ref[s], w_ref[...], (((1,), (1,)), ((), ())), preferred_element_type=F32
        ).astype(BF16)
        for n in range(out_ref.shape[0]):
            out_ref[n, s] = ga


def columns(refs):
    seqs = refs[0].shape[0]
    rows = [jnp.concatenate([ref[s] for s in range(seqs)], axis=1) for ref in refs]
    return jnp.concatenate(rows, axis=0)


def head_mask(shape, head):
    lane = lax.broadcasted_iota(jnp.int32, shape, 1)
    return ((lane // 64) % 2) == head


def product_kernel(core_ref, own_ref, one_ref, two_ref, three_ref, left_ref, keep_ref, send_ref):
    first = core_ref[0] == 0
    left = columns([left_ref.at[n] for n in range(4)])
    right = columns([ref.at[0] for ref in (own_ref, one_ref, two_ref, three_ref)])
    both = []
    for head in range(2):
        own = jnp.where(head_mask(left.shape, head), left, jnp.zeros_like(left))
        both.append(lax.dot_general(own, right, (((1,), (1,)), ((), ())), preferred_element_type=F32))
    shape = (keep_ref.shape[0],) + keep_ref.shape[2:]
    keep_ref[:, 0] = jnp.where(first, both[0], both[1]).reshape(shape)
    send_ref[:, 0] = jnp.where(first, both[1], both[0]).reshape(shape)


def split_kernel(core_ref, keep_ref, got_ref, own_ref, one_ref, two_ref, three_ref):
    for by, ref in enumerate((own_ref, one_ref, two_ref, three_ref)):
        at = lax.rem(core_ref[1] + by, 4)
        ref[...] = keep_ref[at] + got_ref[at]


def rows_kernel(own_ref, one_ref, two_ref, three_ref, grad_ref, out_ref):
    logits = (own_ref[...] + one_ref[...]) + (two_ref[...] + three_ref[...])
    grads = (grad_ref[0] + grad_ref[1]) + (grad_ref[2] + grad_ref[3])
    for n in range(16):
        for p in range(PAIRS):
            out_ref[n, p * 4 : p * 4 + 4] = logits[p, n * 4 : n * 4 + 4]
            out_ref[n, 12 + p * 4 : 16 + p * 4] = grads[p, n * 4 : n * 4 + 4]


def softmax_kernel(scale, part_ref, out_ref):
    tiles = []
    for col in range(4):
        parts = [part_ref[n * 4 + col] for n in range(4)]
        tiles.append((parts[0] + parts[1]) + (parts[2] + parts[3]))
    total = jnp.concatenate(tiles, axis=1)
    logits = total[:12] * scale
    grads = total[12:]
    expo = jnp.exp(logits - jnp.max(logits, axis=-1, keepdims=True))
    weights = expo / jnp.sum(expo, axis=-1, keepdims=True)
    scores = weights * (grads - jnp.sum(weights * grads, axis=-1, keepdims=True))
    full = jnp.concatenate([weights, scores], axis=0)
    for col in range(4):
        at = col * 256
        tile = jnp.concatenate([full[:, at : at + 128], full[:, at + 128 : at + 256]], axis=0).astype(BF16)
        for n in range(col, 16, 4):
            out_ref[n] = tile


def unpack_kernel(ws_ref, out_ref, rows_ref):
    for n in range(16):
        block = ws_ref[n].astype(F32)
        for which in range(2):
            for p in range(PAIRS):
                at = which * 12 + p * 4
                rows_ref[which, p, n * 4 : n * 4 + 4, 0:128] = block[at : at + 4]
                rows_ref[which, p, n * 4 : n * 4 + 4, 128:256] = block[24 + at : 28 + at]
    full = rows_ref[...].astype(BF16)
    for n in range(out_ref.shape[0]):
        out_ref[n] = full


def output_kernel(scale, core_ref, mine_ref, other_ref, *refs):
    kv_refs, q_ref, g_ref, row_ref, col_refs = refs[:4], refs[4], refs[5], refs[6], refs[7:11]
    first = core_ref[0] == 0
    row_refs = [row_ref.at[n] for n in range(4)]

    def heads(which):
        mine = mine_ref[:, which, 0].reshape(256, 256)
        other = other_ref[:, which, 0].reshape(256, 256)
        return jnp.where(first, mine, other), jnp.where(first, other, mine)

    def product(mats, side, contract):
        both = [
            lax.dot_general(m, side, (((contract,), (0,)), ((), ())), preferred_element_type=F32)
            for m in mats
        ]
        return jnp.where(head_mask(both[0].shape, 0), both[0], both[1])

    def put(outs, which, value):
        value = value.astype(BF16)
        for n, ref in enumerate(outs):
            _, seqs, res, lanes = ref.shape
            for s in range(seqs):
                ref[which, s] = value[n * res : (n + 1) * res, s * lanes : (s + 1) * lanes]

    weights, scores = heads(0), heads(1)
    left_q = columns([q_ref.at[n] for n in range(4)])
    left_g = columns([g_ref.at[n] for n in range(4)])
    put(row_refs, 0, product(weights, columns([ref.at[1] for ref in kv_refs]), 1))
    put(row_refs, 1, product(scores, columns([ref.at[0] for ref in kv_refs]), 1) * scale)
    put(col_refs, 0, product(weights, left_g, 0))
    put(col_refs, 1, product(scores, left_q, 0) * scale)


def total_of(refs, which, s):
    parts = [ref[which, s].astype(F32) for ref in refs]
    return ((parts[0] + parts[1]) + (parts[2] + parts[3])).astype(BF16)


def finish_kernel(row_ref, *refs):
    col_refs, (w_ref, mixed_ref, gq_ref, gk_ref, gv_ref) = refs[:4], refs[4:]
    row_refs = [row_ref.at[n] for n in range(4)]
    for s in range(mixed_ref.shape[0]):
        attended = total_of(row_refs, 0, s)
        mixed_ref[s] = jnp.dot(attended, w_ref[...], preferred_element_type=F32).astype(BF16)
        gq_ref[s] = total_of(row_refs, 1, s)
        gv_ref[s] = total_of(col_refs, 0, s)
        gk_ref[s] = total_of(col_refs, 1, s)


def on_device(queries, keys, values, out_weight, grad_out):
    seqs, res, width = queries.shape
    model_dim = out_weight.shape[1]
    scale = 1.0 / math.sqrt(width // HEADS * seqs * 32)
    place = jnp.stack([lax.axis_index("c"), lax.axis_index("y")]).astype(jnp.int32)
    block = jax.ShapeDtypeStruct((seqs, res, width), BF16)
    blocks = jax.ShapeDtypeStruct((4, seqs, res, width), BF16)
    half = jax.ShapeDtypeStruct((4, PAIRS, 64, 256), F32)
    quarter = jax.ShapeDtypeStruct((PAIRS, 64, 256), F32)
    smem = pl.BlockSpec(memory_space=pltpu.SMEM)
    hbm = pl.BlockSpec(memory_space=pltpu.HBM)
    slabs = pl.BlockSpec((4, seqs, res, 128), lambda p: (0, 0, 0, p))
    stack_slab = pl.BlockSpec((2, seqs, res, 128), lambda p: (0, 0, 0, p))
    half_slab = pl.BlockSpec((4, 1, 64, 256), lambda p: (0, p, 0, 0))

    def products(which, rights, left, name):
        slab = pl.BlockSpec((1, seqs, res, 128), lambda p: (which, 0, 0, p))
        return pl.pallas_call(
            product_kernel,
            grid=(PAIRS,),
            in_specs=[smem] + [slab] * 4 + [slabs],
            out_specs=[half_slab, half_slab],
            out_shape=(half, half),
            compiler_params=params(),
            name=name,
        )(place, *rights, left)

    kv_own, q_send = pl.pallas_call(
        prep_kernel,
        in_specs=[hbm] * 3,
        out_specs=[hbm] * 2,
        out_shape=(pltpu.HBM((2, seqs, res, width), BF16), pltpu.HBM((4, seqs, res, width), BF16)),
        scratch_shapes=[pltpu.SemaphoreType.DMA((6,))],
        compiler_params=params(),
        name="prep",
    )(*(pltpu.with_memory_space_constraint(a, pltpu.HBM) for a in (queries, keys, values)))
    left_q = exchange(q_send, "zl")
    rights = [kv_own] + [shift(kv_own, "x", by) for by in (1, 2, 3)]
    grads = pl.pallas_call(
        grad_kernel,
        out_shape=pltpu.HBM((4, seqs, res, width), BF16),
        compiler_params=params(),
        name="grad_attended",
    )(out_weight, grad_out)
    grads, left_q, rights = lax.optimization_barrier((grads, left_q, rights))
    left_g = exchange(grads, "zl")

    keep, send = products(0, rights, left_q, "logits")
    pieces = pl.pallas_call(
        split_kernel,
        in_specs=[smem] + [pl.BlockSpec(memory_space=pltpu.VMEM)] * 2,
        out_shape=(quarter,) * 4,
        compiler_params=params(),
        name="split",
    )(place, keep, shift(send, "c", 1))
    _, left_g = lax.optimization_barrier((pieces, left_g))
    keep, send = products(1, rights, left_g, "weight_grads")
    pieces = [pieces[0]] + [shift(pieces[by], "y", by) for by in (1, 2, 3)]
    send, pieces = lax.optimization_barrier((send, pieces))

    partial = exchange(keep + shift(send, "c", 1), "y")
    partial = pl.pallas_call(
        rows_kernel,
        out_shape=jax.ShapeDtypeStruct((16, 8 * PAIRS, 256), F32),
        compiler_params=params(),
        name="rows",
    )(*pieces, partial)
    partial = exchange(partial, ("zh", "zl"))
    ws = pl.pallas_call(
        lambda *refs: softmax_kernel(scale, *refs),
        out_shape=jax.ShapeDtypeStruct((16, 48, 128), BF16),
        compiler_params=params(),
        name="softmax",
    )(partial)
    ws = exchange(ws, ("zh", "zl"))
    ws = pl.pallas_call(
        unpack_kernel,
        out_shape=jax.ShapeDtypeStruct((4, 2, PAIRS, 64, 256), BF16),
        scratch_shapes=[pltpu.VMEM((2, PAIRS, 64, 256), F32)],
        compiler_params=params(),
        name="unpack",
    )(ws)
    mine = exchange(ws, "y")
    other = shift(mine, "c", 1)

    ws_slab = pl.BlockSpec((4, 2, 1, 64, 256), lambda p: (0, 0, p, 0, 0))
    row, *cols = pl.pallas_call(
        lambda *refs: output_kernel(scale, *refs),
        grid=(PAIRS,),
        in_specs=[smem, ws_slab, ws_slab] + [stack_slab] * 4 + [slabs] * 2,
        out_specs=[pl.BlockSpec((4, 2, seqs, res, 128), lambda p: (0, 0, 0, 0, p))] + [stack_slab] * 4,
        out_shape=(pltpu.HBM((4, 2, seqs, res, width), BF16),)
        + (pltpu.HBM((2, seqs, res, width), BF16),) * 4,
        compiler_params=params(),
        name="outputs",
    )(place, mine, other, *rights, left_q, left_g)
    row = exchange(row, "zl")
    cols = [cols[0]] + [shift(cols[by], "x", -by) for by in (1, 2, 3)]
    return pl.pallas_call(
        finish_kernel,
        out_shape=(jax.ShapeDtypeStruct((seqs, res, model_dim), BF16), block, block, block),
        compiler_params=params(),
        name="finish",
    )(row, *cols, out_weight)


def solution(mesh):
    grid = Mesh(mesh.devices.reshape(4, 4, 2, 4, 4), ("zh", "y", "c", "x", "zl"))
    placed = P(("zh", "y", "c"), ("x", "zl"), None)
    return jax.shard_map(
        on_device,
        mesh=grid,
        in_specs=(placed, placed, placed, P(), placed),
        out_specs=(placed, placed, placed, placed),
        check_vma=False,
    )
```

```python
import math

import jax
import jax.numpy as jnp
from jax import lax
from jax.experimental import pallas as pl
from jax.experimental.pallas import tpu as pltpu
from jax.sharding import Mesh, PartitionSpec as P

HEADS = 6
LOCAL = 3
F32 = jnp.float32
BF16 = jnp.bfloat16
VMEM = 16 * 1024 * 1024


def params():
    return pltpu.CompilerParams(vmem_limit_bytes=VMEM)


def exchange(blocks, axis):
    return lax.all_to_all(blocks, axis, 0, 0, tiled=True)


def shift(block, axis, by):
    n = lax.axis_size(axis)
    return lax.ppermute(block, axis, [(i, (i + by) % n) for i in range(n)])


def gather(block, axis):
    return lax.all_gather(block, axis)


def stack_kernel(q_hbm, k_hbm, v_hbm, w_hbm, go_hbm, out_ref, w_ref, go_ref, sems):
    loads = [
        pltpu.make_async_copy(w_hbm, w_ref, sems.at[0]),
        pltpu.make_async_copy(go_hbm, go_ref, sems.at[1]),
        pltpu.make_async_copy(q_hbm, out_ref.at[0], sems.at[2]),
        pltpu.make_async_copy(k_hbm, out_ref.at[1], sems.at[3]),
        pltpu.make_async_copy(v_hbm, out_ref.at[2], sems.at[4]),
    ]
    for load in loads:
        load.start()
    loads[0].wait()
    loads[1].wait()
    for s in range(go_ref.shape[0]):
        out_ref[3, s] = lax.dot_general(
            go_ref[s], w_ref[...], (((1,), (1,)), ((), ())), preferred_element_type=F32
        ).astype(BF16)
    for load in loads[2:]:
        load.wait()


def merge(first, own, other):
    half = own.shape[1] // 2
    swapped = jnp.concatenate([other[:, half:], other[:, :half]], axis=1)
    low = lax.broadcasted_iota(jnp.int32, own.shape, 1) < half
    return jnp.where(first, jnp.where(low, own, swapped), jnp.where(low, swapped, own))


def trade_kernel(place_ref, own_ref, other_ref, q_ref, g_ref, kv_ref):
    first = place_ref[0] == 0
    for s in range(q_ref.shape[0]):
        q_ref[s] = merge(first, own_ref[0, s], other_ref[0, s])
        g_ref[s] = merge(first, own_ref[3, s], other_ref[3, s])
        for which in range(2):
            block = merge(first, own_ref[1 + which, s], other_ref[1 + which, s])
            for n in range(kv_ref.shape[0]):
                kv_ref[n, which, s] = block


def columns(refs):
    seqs = refs[0].shape[0]
    rows = [jnp.concatenate([ref[s] for s in range(seqs)], axis=1) for ref in refs]
    return jnp.concatenate(rows, axis=0)


def lefts(ref):
    return columns([ref.at[n] for n in range(4)])


def rights(place_ref, ref, which):
    return columns([ref.at[lax.rem(place_ref[1] + 4 - n, 4), which] for n in range(4)])


def odd_chunk(shape):
    return (lax.broadcasted_iota(jnp.int32, shape, 1) // 64) % 2


def product_kernel(place_ref, q0_ref, q1_ref, g0_ref, g1_ref, kv0_ref, kv1_ref, out_ref):
    odd = lax.rem(pl.program_id(0), 2)
    for which, (left0, left1) in enumerate(((q0_ref, q1_ref), (g0_ref, g1_ref))):
        left = []
        for ref, parity in ((left0, odd), (left1, 1 - odd)):
            cols = lefts(ref)
            left.append(jnp.where(odd_chunk(cols.shape) == parity, cols, jnp.zeros_like(cols)))
        left = jnp.concatenate(left, axis=1)
        right = jnp.concatenate([rights(place_ref, kv0_ref, which), rights(place_ref, kv1_ref, which)], axis=1)
        full = lax.dot_general(left, right, (((1,), (1,)), ((), ())), preferred_element_type=F32)
        out_ref[:, 0, which] = full.reshape(out_ref.shape[0], out_ref.shape[3], out_ref.shape[4])


def rows_kernel(part_ref, out_ref):
    total = (part_ref[0] + part_ref[1]) + (part_ref[2] + part_ref[3])
    for n in range(16):
        for t in range(LOCAL):
            for which in range(2):
                at = (which * LOCAL + t) * 4
                out_ref[n, at : at + 4] = total[t, which, n * 4 : n * 4 + 4]


def softmax_kernel(scale, part_ref, out_ref):
    tiles = []
    for col in range(4):
        parts = [part_ref[n * 4 + col] for n in range(4)]
        tiles.append((parts[0] + parts[1]) + (parts[2] + parts[3]))
    total = jnp.concatenate(tiles, axis=1)
    logits = total[:12] * scale
    grads = total[12:]
    expo = jnp.exp(logits - jnp.max(logits, axis=-1, keepdims=True))
    weights = expo / jnp.sum(expo, axis=-1, keepdims=True)
    scores = weights * (grads - jnp.sum(weights * grads, axis=-1, keepdims=True))
    full = jnp.concatenate([weights, scores], axis=0)
    for col in range(4):
        at = col * 256
        tile = jnp.concatenate([full[:, at : at + 128], full[:, at + 128 : at + 256]], axis=0).astype(BF16)
        for n in range(col, 16, 4):
            out_ref[n] = tile


def unpack_kernel(ws_ref, out_ref, rows_ref):
    for n in range(16):
        block = ws_ref[n].astype(F32)
        for which in range(2):
            for t in range(LOCAL):
                at = which * 12 + t * 4
                rows_ref[which, t, n * 4 : n * 4 + 4, 0:128] = block[at : at + 4]
                rows_ref[which, t, n * 4 : n * 4 + 4, 128:256] = block[24 + at : 28 + at]
    full = rows_ref[...].astype(BF16)
    for n in range(out_ref.shape[0]):
        out_ref[n] = full


def output_kernel(scale, place_ref, even_ref, odd_ref, q_ref, g_ref, kv_ref, row_ref, *col_refs):
    row_refs = [row_ref.at[n] for n in range(4)]

    def product(kind, side, contract):
        both = [
            lax.dot_general(
                ref[:, kind, 0].reshape(256, 256), side, (((contract,), (0,)), ((), ())), preferred_element_type=F32
            )
            for ref in (even_ref, odd_ref)
        ]
        return jnp.where(odd_chunk(both[0].shape) == 0, both[0], both[1])

    def put(outs, which, value):
        value = value.astype(BF16)
        for n, ref in enumerate(outs):
            _, seqs, res, lanes = ref.shape
            for s in range(seqs):
                ref[which, s] = value[n * res : (n + 1) * res, s * lanes : (s + 1) * lanes]

    put(row_refs, 0, product(0, rights(place_ref, kv_ref, 1), 1))
    put(row_refs, 1, product(1, rights(place_ref, kv_ref, 0), 1) * scale)
    put(col_refs, 0, product(0, lefts(g_ref), 0))
    put(col_refs, 1, product(1, lefts(q_ref), 0) * scale)


def total_kernel(*refs):
    parts, out_ref = refs[:-1], refs[-1]
    for which in range(out_ref.shape[0]):
        for s in range(out_ref.shape[1]):
            p = [ref[which, s].astype(F32) for ref in parts]
            out_ref[which, s] = ((p[0] + p[1]) + (p[2] + p[3])).astype(BF16)


def total_blocks_kernel(part_ref, out_ref):
    total_kernel(*[part_ref.at[n] for n in range(4)], out_ref)


def finish_kernel(place_ref, row_ref, row_other_ref, col_ref, col_other_ref, w_ref, mixed_ref, gq_ref, gk_ref, gv_ref):
    first = place_ref[0] == 0
    for s in range(mixed_ref.shape[0]):
        attended = merge(first, row_ref[0, s], row_other_ref[0, s])
        mixed_ref[s] = jnp.dot(attended, w_ref[...], preferred_element_type=F32).astype(BF16)
        gq_ref[s] = merge(first, row_ref[1, s], row_other_ref[1, s])
        gv_ref[s] = merge(first, col_ref[0, s], col_other_ref[0, s])
        gk_ref[s] = merge(first, col_ref[1, s], col_other_ref[1, s])


def on_device(queries, keys, values, out_weight, grad_out):
    seqs, res, width = queries.shape
    model_dim = out_weight.shape[1]
    scale = 1.0 / math.sqrt(width // HEADS * seqs * 32)
    place = jnp.stack([lax.axis_index("c"), lax.axis_index("x")]).astype(jnp.int32)
    block = (seqs, res, width)
    smem = pl.BlockSpec(memory_space=pltpu.SMEM)
    vmem = pl.BlockSpec(memory_space=pltpu.VMEM)
    hbm = pl.BlockSpec(memory_space=pltpu.HBM)

    def array(shape, dtype=BF16):
        return jax.ShapeDtypeStruct(shape, dtype)

    args = (queries, keys, values, out_weight, grad_out)
    own = pl.pallas_call(
        stack_kernel,
        in_specs=[hbm] * 5,
        out_specs=vmem,
        out_shape=array((4,) + block),
        scratch_shapes=[
            pltpu.VMEM(out_weight.shape, BF16),
            pltpu.VMEM(grad_out.shape, BF16),
            pltpu.SemaphoreType.DMA((5,)),
        ],
        compiler_params=params(),
        name="stack",
    )(*(pltpu.with_memory_space_constraint(arg, pltpu.HBM) for arg in args))
    q, g, kv = pl.pallas_call(
        trade_kernel,
        in_specs=[smem, vmem, vmem],
        out_shape=(array(block), array(block), array((4, 2) + block)),
        compiler_params=params(),
        name="trade",
    )(place, own, shift(own, "c", 1))
    kv = exchange(kv, "x")
    q = gather(q, "zl")
    g = gather(g, "zl")

    def slab(at):
        return pl.BlockSpec((4, seqs, res, 128), lambda t: (0, 0, 0, at(t)))

    def kv_slab(at):
        return pl.BlockSpec((4, 2, seqs, res, 128), lambda t: (0, 0, 0, 0, at(t)))

    low, high, same = (lambda t: t // 2), (lambda t: (t + 3) // 2), (lambda t: t)
    partial = pl.pallas_call(
        product_kernel,
        grid=(LOCAL,),
        in_specs=[smem, slab(low), slab(high), slab(low), slab(high), kv_slab(low), kv_slab(high)],
        out_specs=pl.BlockSpec((4, 1, 2, 64, 256), lambda t: (0, t, 0, 0, 0)),
        out_shape=array((4, LOCAL, 2, 64, 256), F32),
        compiler_params=params(),
        name="products",
    )(place, q, q, g, g, kv, kv)
    partial = exchange(partial, "y")
    partial = pl.pallas_call(
        rows_kernel, out_shape=array((16, 8 * LOCAL, 256), F32), compiler_params=params(), name="rows"
    )(partial)
    partial = exchange(partial, ("zh", "zl"))
    ws = pl.pallas_call(
        lambda *refs: softmax_kernel(scale, *refs),
        out_shape=array((16, 48, 128)),
        compiler_params=params(),
        name="softmax",
    )(partial)
    ws = exchange(ws, ("zh", "zl"))
    ws = pl.pallas_call(
        unpack_kernel,
        out_shape=array((4, 2, LOCAL, 64, 256)),
        scratch_shapes=[pltpu.VMEM((2, LOCAL, 64, 256), F32)],
        compiler_params=params(),
        name="unpack",
    )(ws)
    ws = exchange(ws, "y")

    def ws_slab(add):
        return pl.BlockSpec((4, 2, 1, 64, 256), lambda p: (0, 0, (2 * p + add) % 3, 0, 0))

    row, *cols = pl.pallas_call(
        lambda *refs: output_kernel(scale, *refs),
        grid=(3,),
        in_specs=[smem, ws_slab(0), ws_slab(1), slab(same), slab(same), kv_slab(same)],
        out_specs=[kv_slab(same)] + [pl.BlockSpec((2, seqs, res, 128), lambda p: (0, 0, 0, p))] * 4,
        out_shape=(pltpu.HBM((4, 2) + block, BF16),) + (pltpu.HBM((2,) + block, BF16),) * 4,
        compiler_params=params(),
        name="outputs",
    )(place, ws, ws, q, g, kv)
    row = exchange(row, "zl")
    cols = [cols[0]] + [shift(cols[by], "x", -by) for by in (1, 2, 3)]
    col = pl.pallas_call(
        total_kernel, out_shape=array((2,) + block), compiler_params=params(), name="total_columns"
    )(*cols)
    col_other = shift(col, "c", 1)
    row = pl.pallas_call(
        total_blocks_kernel, out_shape=array((2,) + block), compiler_params=params(), name="total_rows"
    )(row)
    return pl.pallas_call(
        finish_kernel,
        in_specs=[smem] + [vmem] * 5,
        out_shape=(array((seqs, res, model_dim)), array(block), array(block), array(block)),
        compiler_params=params(),
        name="finish",
    )(place, row, shift(row, "c", 1), col, col_other, out_weight)


def solution(mesh):
    grid = Mesh(mesh.devices.reshape(4, 4, 2, 4, 4), ("zh", "y", "c", "x", "zl"))
    placed = P(("zh", "y", "c"), ("x", "zl"), None)
    return jax.shard_map(
        on_device,
        mesh=grid,
        in_specs=(placed, placed, placed, P(), placed),
        out_specs=(placed, placed, placed, placed),
        check_vma=False,
    )
```

```python
import math

import jax
import jax.numpy as jnp
from jax import lax
from jax.experimental import pallas as pl
from jax.experimental.pallas import tpu as pltpu
from jax.sharding import Mesh, PartitionSpec as P

HEADS = 6
F32 = jnp.float32
BF16 = jnp.bfloat16
VMEM = 16 * 1024 * 1024


def params():
    return pltpu.CompilerParams(vmem_limit_bytes=VMEM)


def exchange(blocks, axis):
    return lax.all_to_all(blocks, axis, 0, 0, tiled=True)


def shift(block, axis, by):
    n = lax.axis_size(axis)
    return lax.ppermute(block, axis, [(i, (i + by) % n) for i in range(n)])


def halves(one, two):
    half = one.shape[1] // 2
    return (
        jnp.concatenate([one[:, :half], two[:, :half]], axis=1),
        jnp.concatenate([one[:, half:], two[:, half:]], axis=1),
    )


def pack_kernel(place_ref, q_hbm, k_hbm, v_hbm, w_hbm, go_hbm, own_ref, send_ref, right_ref, q_ref, k_ref, v_ref, w_ref, go_ref, sems):
    loads = [
        pltpu.make_async_copy(src, dst, sems.at[n])
        for n, (src, dst) in enumerate(
            ((w_hbm, w_ref), (go_hbm, go_ref), (q_hbm, q_ref), (k_hbm, k_ref), (v_hbm, v_ref))
        )
    ]
    for load in loads:
        load.start()
    for load in loads:
        load.wait()
    first = place_ref[0] == 0
    for s in range(q_ref.shape[0]):
        grads = lax.dot_general(
            go_ref[s], w_ref[...], (((1,), (1,)), ((), ())), preferred_element_type=F32
        ).astype(BF16)
        low, high = halves(q_ref[s], grads)
        own_ref[s] = jnp.where(first, low, high)
        send_ref[s] = jnp.where(first, high, low)
        for core, part in enumerate(halves(k_ref[s], v_ref[s])):
            for n in range(right_ref.shape[0]):
                right_ref[n, core, s] = part


def columns(blocks):
    rows = [jnp.concatenate([ref[s] for ref in row for s in range(ref.shape[0])], axis=1) for row in blocks]
    return jnp.concatenate(rows, axis=0)


def lefts(own_ref, other_ref):
    return columns([(own_ref.at[n], other_ref.at[n]) for n in range(4)])


def rights(place_ref, ref):
    core = place_ref[0]
    x = [lax.rem(place_ref[1] + 4 - n, 4) for n in range(4)]
    return columns([(ref.at[x[n], core], ref.at[x[n], 1 - core]) for n in range(4)])


def odd_chunk(shape):
    return (lax.broadcasted_iota(jnp.int32, shape, 1) // 64) % 2 == 1


def product_kernel(place_ref, own_ref, other_ref, right_ref, out_ref):
    left = lefts(own_ref, other_ref)
    right = rights(place_ref, right_ref)
    odd = odd_chunk(left.shape)
    zero = jnp.zeros_like(left)
    for parity, part in enumerate((jnp.where(odd, zero, left), jnp.where(odd, left, zero))):
        full = lax.dot_general(part, right, (((1,), (1,)), ((), ())), preferred_element_type=F32)
        out_ref[:, parity] = full.reshape(out_ref.shape[0], out_ref.shape[2], out_ref.shape[3])


def rows_kernel(part_ref, out_ref):
    total = (part_ref[0] + part_ref[1]) + (part_ref[2] + part_ref[3])
    for n in range(16):
        for j in range(6):
            out_ref[n, j * 4 : j * 4 + 4] = total[j, n * 4 : n * 4 + 4]


def softmax_kernel(scale, part_ref, out_ref):
    tiles = []
    for col in range(4):
        parts = [part_ref[n * 4 + col] for n in range(4)]
        tiles.append((parts[0] + parts[1]) + (parts[2] + parts[3]))
    total = jnp.concatenate(tiles, axis=1)
    logits = total[:12] * scale
    grads = total[12:]
    expo = jnp.exp(logits - jnp.max(logits, axis=-1, keepdims=True))
    weights = expo / jnp.sum(expo, axis=-1, keepdims=True)
    scores = weights * (grads - jnp.sum(weights * grads, axis=-1, keepdims=True))
    full = jnp.concatenate([scores, weights], axis=0)
    for col in range(4):
        at = col * 256
        tile = jnp.concatenate([full[:, at : at + 128], full[:, at + 128 : at + 256]], axis=0).astype(BF16)
        for n in range(col, 16, 4):
            out_ref[n] = tile


def unpack_kernel(mats_ref, out_ref, rows_ref):
    for n in range(16):
        block = mats_ref[n].astype(F32)
        for j in range(6):
            rows_ref[j, n * 4 : n * 4 + 4, 0:128] = block[j * 4 : j * 4 + 4]
            rows_ref[j, n * 4 : n * 4 + 4, 128:256] = block[24 + j * 4 : 28 + j * 4]
    full = rows_ref[...].astype(BF16)
    for n in range(out_ref.shape[0]):
        out_ref[n] = full


def output_kernel(scale, place_ref, mats_ref, own_ref, other_ref, right_ref, row_ref, *col_refs):
    core = place_ref[0]
    seqs, res, lanes = own_ref.shape[1:]
    mats = [mats_ref[:, parity].reshape(256, 256) for parity in range(2)]

    def product(side, contract):
        both = [
            lax.dot_general(m, side, (((contract,), (0,)), ((), ())), preferred_element_type=F32) for m in mats
        ]
        odd = odd_chunk(both[0].shape)
        chunk = 2 * pl.program_id(0) + odd.astype(jnp.int32)
        return (jnp.where(odd, both[1], both[0]) * jnp.where(chunk < 3, scale, 1.0)).astype(BF16)

    def piece(value, n, core_slot, s):
        at = (core_slot * seqs + s) * lanes
        return value[n * res : (n + 1) * res, at : at + lanes]

    row = product(rights(place_ref, right_ref), 1)
    col = product(lefts(own_ref, other_ref), 0)
    for n in range(4):
        for s in range(seqs):
            row_ref[n, core, s] = piece(row, n, 0, s)
            row_ref[n, 1 - core, s] = piece(row, n, 1, s)
            col_refs[n][0, s] = piece(col, n, 0, s)
            col_refs[n][1, s] = piece(col, n, 1, s)


def four(refs, s):
    p = [ref[s].astype(F32) for ref in refs]
    return ((p[0] + p[1]) + (p[2] + p[3])).astype(BF16)


def columns_total_kernel(zero_ref, one_ref, two_ref, three_ref, keep_ref, send_ref):
    refs = (zero_ref, one_ref, two_ref, three_ref)
    for s in range(keep_ref.shape[0]):
        keep_ref[s] = four([ref.at[0] for ref in refs], s)
        send_ref[s] = four([ref.at[1] for ref in refs], s)


def finish_kernel(place_ref, row_ref, col_ref, got_ref, w_ref, mixed_ref, gq_ref, gk_ref, gv_ref):
    first = place_ref[0] == 0
    for s in range(mixed_ref.shape[0]):
        cores = [four([row_ref.at[n, core] for n in range(4)], s) for core in range(2)]
        gq_ref[s], attended = halves(*cores)
        mixed_ref[s] = jnp.dot(attended, w_ref[...], preferred_element_type=F32).astype(BF16)
        low, high = jnp.where(first, col_ref[s], got_ref[s]), jnp.where(first, got_ref[s], col_ref[s])
        gk_ref[s], gv_ref[s] = halves(low, high)


def on_device(queries, keys, values, out_weight, grad_out):
    seqs, res, width = queries.shape
    model_dim = out_weight.shape[1]
    scale = 1.0 / math.sqrt(width // HEADS * seqs * 32)
    place = jnp.stack([lax.axis_index("c"), lax.axis_index("x")]).astype(jnp.int32)
    block = (seqs, res, width)
    smem = pl.BlockSpec(memory_space=pltpu.SMEM)
    vmem = pl.BlockSpec(memory_space=pltpu.VMEM)
    hbm = pl.BlockSpec(memory_space=pltpu.HBM)

    def array(shape, dtype=BF16):
        return jax.ShapeDtypeStruct(shape, dtype)

    args = (queries, keys, values, out_weight, grad_out)
    own, send, right = pl.pallas_call(
        pack_kernel,
        in_specs=[smem] + [hbm] * 5,
        out_specs=[vmem] * 3,
        out_shape=(array(block), array(block), array((4, 2) + block)),
        scratch_shapes=[pltpu.VMEM(a.shape, BF16) for a in (queries, keys, values, out_weight, grad_out)]
        + [pltpu.SemaphoreType.DMA((5,))],
        compiler_params=params(),
        name="pack",
    )(place, *(pltpu.with_memory_space_constraint(arg, pltpu.HBM) for arg in args))
    right = exchange(right.reshape((8,) + block), ("x", "c")).reshape((4, 2) + block)
    other = shift(send, "c", 1)
    own = lax.all_gather(own, "zl")
    other = lax.all_gather(other, "zl")

    left_slab = pl.BlockSpec((4, seqs, res, 128), lambda p: (0, 0, 0, p))
    right_slab = pl.BlockSpec((4, 2, seqs, res, 128), lambda p: (0, 0, 0, 0, p))
    mats_slab = pl.BlockSpec((4, 2, 64, 256), lambda p: (0, p, 0, 0))
    partial = pl.pallas_call(
        product_kernel,
        grid=(3,),
        in_specs=[smem, left_slab, left_slab, right_slab],
        out_specs=mats_slab,
        out_shape=array((4, 6, 64, 256), F32),
        compiler_params=params(),
        name="products",
    )(place, own, other, right)
    partial = exchange(partial, "y")
    partial = pl.pallas_call(
        rows_kernel, out_shape=array((16, 24, 256), F32), compiler_params=params(), name="rows"
    )(partial)
    partial = exchange(partial, ("zh", "zl"))
    mats = pl.pallas_call(
        lambda *refs: softmax_kernel(scale, *refs),
        out_shape=array((16, 48, 128)),
        compiler_params=params(),
        name="softmax",
    )(partial)
    mats = exchange(mats, ("zh", "zl"))
    mats = pl.pallas_call(
        unpack_kernel,
        out_shape=array((4, 6, 64, 256)),
        scratch_shapes=[pltpu.VMEM((6, 64, 256), F32)],
        compiler_params=params(),
        name="unpack",
    )(mats)
    mats = exchange(mats, "y")

    row, *cols = pl.pallas_call(
        lambda *refs: output_kernel(scale, *refs),
        grid=(3,),
        in_specs=[smem, mats_slab, left_slab, left_slab, right_slab],
        out_specs=[right_slab] + [pl.BlockSpec((2, seqs, res, 128), lambda p: (0, 0, 0, p))] * 4,
        out_shape=(pltpu.HBM((4, 2) + block, BF16),) + (pltpu.HBM((2,) + block, BF16),) * 4,
        compiler_params=params(),
        name="outputs",
    )(place, mats, own, other, right)
    row = exchange(row.reshape((8,) + block), ("zl", "c")).reshape((4, 2) + block)
    cols = [cols[0]] + [shift(cols[by], "x", -by) for by in (1, 2, 3)]
    keep, send = pl.pallas_call(
        columns_total_kernel, out_shape=(array(block), array(block)), compiler_params=params(), name="columns_total"
    )(*cols)
    return pl.pallas_call(
        finish_kernel,
        in_specs=[smem] + [vmem] * 4,
        out_shape=(array((seqs, res, model_dim)), array(block), array(block), array(block)),
        compiler_params=params(),
        name="finish",
    )(place, row, keep, shift(send, "c", 1), out_weight)


def solution(mesh):
    grid = Mesh(mesh.devices.reshape(4, 4, 2, 4, 4), ("zh", "y", "c", "x", "zl"))
    placed = P(("zh", "y", "c"), ("x", "zl"), None)
    return jax.shard_map(
        on_device,
        mesh=grid,
        in_specs=(placed, placed, placed, P(), placed),
        out_specs=(placed, placed, placed, placed),
        check_vma=False,
    )
```

```python
import math

import jax
import jax.numpy as jnp
from jax import lax
from jax.experimental import pallas as pl
from jax.experimental.pallas import tpu as pltpu
from jax.sharding import Mesh, PartitionSpec as P

HEADS = 6
F32 = jnp.float32
BF16 = jnp.bfloat16
VMEM = 16 * 1024 * 1024


def params():
    return pltpu.CompilerParams(vmem_limit_bytes=VMEM)


def exchange(blocks, axis):
    return lax.all_to_all(blocks, axis, 0, 0, tiled=True)


def shift(block, axis, by):
    n = lax.axis_size(axis)
    return lax.ppermute(block, axis, [(i, (i + by) % n) for i in range(n)])


def halves(one, two):
    half = one.shape[1] // 2
    return (
        jnp.concatenate([one[:, :half], two[:, :half]], axis=1),
        jnp.concatenate([one[:, half:], two[:, half:]], axis=1),
    )


def pack_kernel(place_ref, q_hbm, k_hbm, v_hbm, w_hbm, go_hbm, own_ref, send_ref, right_ref, q_ref, k_ref, v_ref, w_ref, go_ref, sems):
    loads = [
        pltpu.make_async_copy(src, dst, sems.at[n])
        for n, (src, dst) in enumerate(
            ((k_hbm, k_ref), (v_hbm, v_ref), (w_hbm, w_ref), (go_hbm, go_ref), (q_hbm, q_ref))
        )
    ]
    for load in loads:
        load.start()
    first = place_ref[0] == 0
    loads[0].wait()
    loads[1].wait()
    seqs, res, _ = q_ref.shape
    for s in range(seqs):
        for core, part in enumerate(halves(k_ref[s], v_ref[s])):
            for n in range(right_ref.shape[0]):
                right_ref[n, core, s] = part
    for load in loads[2:]:
        load.wait()
    grads = lax.dot_general(
        go_ref[...].reshape(seqs * res, go_ref.shape[2]),
        w_ref[...],
        (((1,), (1,)), ((), ())),
        preferred_element_type=F32,
    ).astype(BF16)
    for s in range(seqs):
        low, high = halves(q_ref[s], grads[s * res : (s + 1) * res])
        own_ref[s] = jnp.where(first, low, high)
        send_ref[s] = jnp.where(first, high, low)


def slab(blocks, p):
    at = slice(p * 128, p * 128 + 128)
    rows = [
        jnp.concatenate([ref[s, :, at] for ref in row for s in range(ref.shape[0])], axis=1) for row in blocks
    ]
    return jnp.concatenate(rows, axis=0)


def lefts(own_ref, other_ref):
    return [(own_ref.at[n], other_ref.at[n]) for n in range(4)]


def rights(place_ref, ref):
    core = place_ref[0]
    x = [lax.rem(place_ref[1] + 4 - n, 4) for n in range(4)]
    return [(ref.at[x[n], core], ref.at[x[n], 1 - core]) for n in range(4)]


def odd_chunk(shape):
    return (lax.broadcasted_iota(jnp.int32, shape, 1) // 64) % 2 == 1


def product_kernel(place_ref, own_ref, other_ref, right_ref, out_ref):
    for p in range(3):
        left = slab(lefts(own_ref, other_ref), p)
        right = slab(rights(place_ref, right_ref), p)
        odd = odd_chunk(left.shape)
        zero = jnp.zeros_like(left)
        for parity, part in enumerate((jnp.where(odd, zero, left), jnp.where(odd, left, zero))):
            full = lax.dot_general(part, right, (((1,), (1,)), ((), ())), preferred_element_type=F32)
            out_ref[:, 2 * p + parity] = full.reshape(out_ref.shape[0], out_ref.shape[2], out_ref.shape[3])


def rows_kernel(part_ref, out_ref):
    total = (part_ref[0] + part_ref[1]) + (part_ref[2] + part_ref[3])
    for n in range(16):
        for j in range(6):
            out_ref[n, j * 4 : j * 4 + 4] = total[j, n * 4 : n * 4 + 4]


def softmax_kernel(scale, part_ref, out_ref):
    tiles = []
    for col in range(4):
        parts = [part_ref[n * 4 + col] for n in range(4)]
        tiles.append((parts[0] + parts[1]) + (parts[2] + parts[3]))
    total = jnp.concatenate(tiles, axis=1)
    logits = total[:12] * scale
    grads = total[12:]
    expo = jnp.exp(logits - jnp.max(logits, axis=-1, keepdims=True))
    weights = expo / jnp.sum(expo, axis=-1, keepdims=True)
    scores = weights * (grads - jnp.sum(weights * grads, axis=-1, keepdims=True))
    full = jnp.concatenate([scores, weights], axis=0)
    for col in range(4):
        at = col * 256
        tile = jnp.concatenate([full[:, at : at + 128], full[:, at + 128 : at + 256]], axis=0).astype(BF16)
        for n in range(col, 16, 4):
            out_ref[n] = tile


def unpack_kernel(mats_ref, out_ref, rows_ref):
    for n in range(16):
        block = mats_ref[n].astype(F32)
        for j in range(6):
            rows_ref[j, n * 4 : n * 4 + 4, 0:128] = block[j * 4 : j * 4 + 4]
            rows_ref[j, n * 4 : n * 4 + 4, 128:256] = block[24 + j * 4 : 28 + j * 4]
    full = rows_ref[...].astype(BF16)
    for n in range(out_ref.shape[0]):
        out_ref[n] = full


def output_kernel(scale, place_ref, mats_ref, own_ref, other_ref, right_ref, row_hbm, *refs):
    col_hbms, row_ref, col_ref, sems = refs[:4], refs[4], refs[5], refs[6]
    seqs, res = own_ref.shape[1:3]

    def put(ref, value, p):
        for n in range(4):
            for slot in range(2):
                for s in range(seqs):
                    at = (slot * seqs + s) * 128
                    ref[n, slot, s, :, p * 128 : p * 128 + 128] = value[n * res : (n + 1) * res, at : at + 128]

    def product(side, contract, p):
        mats = [mats_ref[:, 2 * p + parity].reshape(256, 256) for parity in range(2)]
        even, odd = (
            lax.dot_general(m, side, (((contract,), (0,)), ((), ())), preferred_element_type=F32) for m in mats
        )
        if 2 * p < 3:
            even = even * scale
        if 2 * p + 1 < 3:
            odd = odd * scale
        return jnp.where(odd_chunk(even.shape), odd, even).astype(BF16)

    for p in range(3):
        put(row_ref, product(slab(rights(place_ref, right_ref), p), 1, p), p)
    row_copy = pltpu.make_async_copy(row_ref, row_hbm, sems.at[4])
    row_copy.start()
    for p in range(3):
        put(col_ref, product(slab(lefts(own_ref, other_ref), p), 0, p), p)
    col_copies = [pltpu.make_async_copy(col_ref.at[n], col_hbms[n], sems.at[n]) for n in range(4)]
    for copy in col_copies:
        copy.start()
    row_copy.wait()
    for copy in col_copies:
        copy.wait()


def four(refs, s):
    p = [ref[s].astype(F32) for ref in refs]
    return ((p[0] + p[1]) + (p[2] + p[3])).astype(BF16)


def total_kernel(zero_ref, one_ref, two_ref, three_ref, keep_ref, send_ref):
    refs = (zero_ref, one_ref, two_ref, three_ref)
    for s in range(keep_ref.shape[0]):
        keep_ref[s] = four([ref.at[0] for ref in refs], s)
        send_ref[s] = four([ref.at[1] for ref in refs], s)


def total_blocks_kernel(part_ref, keep_ref, send_ref):
    total_kernel(*[part_ref.at[n] for n in range(4)], keep_ref, send_ref)


def unpacked(first, keep, got):
    return halves(jnp.where(first, keep, got), jnp.where(first, got, keep))


def finish_columns_kernel(place_ref, keep_ref, got_ref, gk_ref, gv_ref):
    first = place_ref[0] == 0
    for s in range(keep_ref.shape[0]):
        gk_ref[s], gv_ref[s] = unpacked(first, keep_ref[s], got_ref[s])


def finish_rows_kernel(place_ref, keep_ref, got_ref, w_ref, mixed_ref, gq_ref):
    first = place_ref[0] == 0
    for s in range(keep_ref.shape[0]):
        gq_ref[s], attended = unpacked(first, keep_ref[s], got_ref[s])
        mixed_ref[s] = jnp.dot(attended, w_ref[...], preferred_element_type=F32).astype(BF16)


def on_device(queries, keys, values, out_weight, grad_out):
    seqs, res, width = queries.shape
    model_dim = out_weight.shape[1]
    scale = 1.0 / math.sqrt(width // HEADS * seqs * 32)
    place = jnp.stack([lax.axis_index("c"), lax.axis_index("x")]).astype(jnp.int32)
    block = (seqs, res, width)
    smem = pl.BlockSpec(memory_space=pltpu.SMEM)
    vmem = pl.BlockSpec(memory_space=pltpu.VMEM)
    hbm = pl.BlockSpec(memory_space=pltpu.HBM)

    def array(shape, dtype=BF16):
        return jax.ShapeDtypeStruct(shape, dtype)

    args = (queries, keys, values, out_weight, grad_out)
    own, send, right = pl.pallas_call(
        pack_kernel,
        in_specs=[smem] + [hbm] * 5,
        out_specs=[vmem] * 3,
        out_shape=(array(block), array(block), array((4, 2) + block)),
        scratch_shapes=[pltpu.VMEM(a.shape, BF16) for a in (queries, keys, values, out_weight, grad_out)]
        + [pltpu.SemaphoreType.DMA((5,))],
        compiler_params=params(),
        name="pack",
    )(place, *(pltpu.with_memory_space_constraint(arg, pltpu.HBM) for arg in args))
    right = exchange(right.reshape((8,) + block), ("x", "c")).reshape((4, 2) + block)
    other = shift(send, "c", 1)
    own = lax.all_gather(own, "zl")
    other = lax.all_gather(other, "zl")

    partial = pl.pallas_call(
        product_kernel,
        in_specs=[smem] + [vmem] * 3,
        out_shape=array((4, 6, 64, 256), F32),
        compiler_params=params(),
        name="products",
    )(place, own, other, right)
    partial = exchange(partial, "y")
    partial = pl.pallas_call(
        rows_kernel, out_shape=array((16, 24, 256), F32), compiler_params=params(), name="rows"
    )(partial)
    partial = exchange(partial, ("zh", "zl"))
    mats = pl.pallas_call(
        lambda *refs: softmax_kernel(scale, *refs),
        out_shape=array((16, 48, 128)),
        compiler_params=params(),
        name="softmax",
    )(partial)
    mats = exchange(mats, ("zh", "zl"))
    mats = pl.pallas_call(
        unpack_kernel,
        out_shape=array((4, 6, 64, 256)),
        scratch_shapes=[pltpu.VMEM((6, 64, 256), F32)],
        compiler_params=params(),
        name="unpack",
    )(mats)
    mats = exchange(mats, "y")

    row, *cols = pl.pallas_call(
        lambda *refs: output_kernel(scale, *refs),
        in_specs=[smem] + [vmem] * 4,
        out_specs=[hbm] * 5,
        out_shape=(pltpu.HBM((4, 2) + block, BF16),) + (pltpu.HBM((2,) + block, BF16),) * 4,
        scratch_shapes=[pltpu.VMEM((4, 2) + block, BF16)] * 2 + [pltpu.SemaphoreType.DMA((5,))],
        compiler_params=params(),
        name="outputs",
    )(place, mats, own, other, right)
    row = exchange(row, "zl")
    cols = [cols[0]] + [shift(cols[by], "x", -by) for by in (1, 2, 3)]
    keep, send = pl.pallas_call(
        total_kernel, out_shape=(array(block), array(block)), compiler_params=params(), name="total_columns"
    )(*cols)
    grad_key, grad_value = pl.pallas_call(
        finish_columns_kernel,
        in_specs=[smem, vmem, vmem],
        out_shape=(array(block), array(block)),
        compiler_params=params(),
        name="finish_columns",
    )(place, keep, shift(send, "c", 1))
    keep, send = pl.pallas_call(
        total_blocks_kernel, out_shape=(array(block), array(block)), compiler_params=params(), name="total_rows"
    )(row)
    mixed, grad_query = pl.pallas_call(
        finish_rows_kernel,
        in_specs=[smem] + [vmem] * 3,
        out_shape=(array((seqs, res, model_dim)), array(block)),
        compiler_params=params(),
        name="finish_rows",
    )(place, keep, shift(send, "c", 1), out_weight)
    return mixed, grad_query, grad_key, grad_value


def solution(mesh):
    grid = Mesh(mesh.devices.reshape(4, 4, 2, 4, 4), ("zh", "y", "c", "x", "zl"))
    placed = P(("zh", "y", "c"), ("x", "zl"), None)
    return jax.shard_map(
        on_device,
        mesh=grid,
        in_specs=(placed, placed, placed, P(), placed),
        out_specs=(placed, placed, placed, placed),
        check_vma=False,
    )
```

```python
import math

import jax
import jax.numpy as jnp
from jax import lax
from jax.experimental import pallas as pl
from jax.experimental.pallas import tpu as pltpu
from jax.sharding import Mesh, PartitionSpec as P

HEADS = 6
F32 = jnp.float32
BF16 = jnp.bfloat16
VMEM = 16 * 1024 * 1024


def params():
    return pltpu.CompilerParams(vmem_limit_bytes=VMEM)


def exchange(blocks, axis):
    return lax.all_to_all(blocks, axis, 0, 0, tiled=True)


def shift(block, axis, by):
    n = lax.axis_size(axis)
    return lax.ppermute(block, axis, [(i, (i + by) % n) for i in range(n)])


def halves(one, two):
    half = one.shape[1] // 2
    return (
        jnp.concatenate([one[:, :half], two[:, :half]], axis=1),
        jnp.concatenate([one[:, half:], two[:, half:]], axis=1),
    )


def low_lanes(shape):
    return lax.broadcasted_iota(jnp.int32, shape, 1) < shape[1] // 2


def pack_kernel(place_ref, q_hbm, k_hbm, v_hbm, w_hbm, go_hbm, own_ref, send_ref, right_ref, q_ref, k_ref, v_ref, w_ref, go_ref, sems):
    loads = [
        pltpu.make_async_copy(src, dst, sems.at[n])
        for n, (src, dst) in enumerate(
            ((w_hbm, w_ref), (go_hbm, go_ref), (k_hbm, k_ref), (v_hbm, v_ref), (q_hbm, q_ref))
        )
    ]
    for load in loads:
        load.start()
    first = place_ref[0] == 0
    loads[0].wait()
    loads[1].wait()
    seqs, res, _ = q_ref.shape
    grads = lax.dot_general(
        go_ref[...].reshape(seqs * res, go_ref.shape[2]),
        w_ref[...],
        (((1,), (1,)), ((), ())),
        preferred_element_type=F32,
    ).astype(BF16)
    for load in loads[2:]:
        load.wait()
    for s in range(seqs):
        kv = halves(k_ref[s], v_ref[s])
        vk = halves(v_ref[s], k_ref[s])
        for core, part in enumerate((jnp.where(first, kv[0], vk[0]), jnp.where(first, vk[1], kv[1]))):
            for n in range(right_ref.shape[0]):
                right_ref[n, core, s] = part
        q, g = q_ref[s], grads[s * res : (s + 1) * res]
        qg, gq = halves(q, g), halves(g, q)
        own_ref[s] = jnp.where(first, qg[0], qg[1])
        send_ref[s] = jnp.where(first, gq[1], gq[0])


def mix_kernel(own_ref, got_ref, low_ref, high_ref):
    for s in range(own_ref.shape[0]):
        low = low_lanes(own_ref.shape[1:])
        low_ref[s] = jnp.where(low, own_ref[s], got_ref[s])
        high_ref[s] = jnp.where(low, got_ref[s], own_ref[s])


def slab(blocks, p):
    at = slice(p * 128, p * 128 + 128)
    rows = [
        jnp.concatenate([ref[s, :, at] for ref in row for s in range(ref.shape[0])], axis=1) for row in blocks
    ]
    return jnp.concatenate(rows, axis=0)


def lefts(ref):
    return [(ref.at[n],) for n in range(4)]


def rights(place_ref, ref, slot):
    core = place_ref[0] if slot == 0 else 1 - place_ref[0]
    return [(ref.at[lax.rem(place_ref[1] + 4 - n, 4), core],) for n in range(4)]


def odd_chunk(shape):
    return (lax.broadcasted_iota(jnp.int32, shape, 1) // 64) % 2 == 1


def product_kernel(own_first, place_ref, left_ref, right_ref, out_ref):
    own, other = (0, 1) if own_first else (1, 0)
    left = [slab(lefts(left_ref), p) for p in range(3)]
    right = [[slab(rights(place_ref, right_ref, slot), p) for p in range(3)] for slot in range(2)]
    odd = odd_chunk(left[0].shape)
    zero = jnp.zeros_like(left[0])
    for t in range(3):
        ones, others = [], []
        for chunk, slot in ((t, own), (t + 3, other)):
            part = left[chunk // 2]
            ones.append(jnp.where(odd, part, zero) if chunk % 2 else jnp.where(odd, zero, part))
            others.append(right[slot][chunk // 2])
        full = lax.dot_general(
            jnp.concatenate(ones, axis=1),
            jnp.concatenate(others, axis=1),
            (((1,), (1,)), ((), ())),
            preferred_element_type=F32,
        )
        out_ref[:, t] = full.reshape(out_ref.shape[0], out_ref.shape[2], out_ref.shape[3])


def rows_kernel(logit_ref, grad_ref, out_ref):
    for which, ref in enumerate((logit_ref, grad_ref)):
        total = (ref[0] + ref[1]) + (ref[2] + ref[3])
        for n in range(16):
            for t in range(3):
                at = (which * 3 + t) * 4
                out_ref[n, at : at + 4] = total[t, n * 4 : n * 4 + 4]


def softmax_kernel(scale, part_ref, out_ref):
    tiles = []
    for col in range(4):
        parts = [part_ref[n * 4 + col] for n in range(4)]
        tiles.append((parts[0] + parts[1]) + (parts[2] + parts[3]))
    total = jnp.concatenate(tiles, axis=1)
    logits = total[:12] * scale
    grads = total[12:]
    expo = jnp.exp(logits - jnp.max(logits, axis=-1, keepdims=True))
    weights = expo / jnp.sum(expo, axis=-1, keepdims=True)
    scores = weights * (grads - jnp.sum(weights * grads, axis=-1, keepdims=True))
    full = jnp.concatenate([scores, weights], axis=0)
    for col in range(4):
        at = col * 256
        tile = jnp.concatenate([full[:, at : at + 128], full[:, at + 128 : at + 256]], axis=0).astype(BF16)
        for n in range(col, 16, 4):
            out_ref[n] = tile


def unpack_kernel(mats_ref, out_ref, rows_ref):
    for n in range(16):
        block = mats_ref[n].astype(F32)
        for j in range(6):
            rows_ref[j, n * 4 : n * 4 + 4, 0:128] = block[j * 4 : j * 4 + 4]
            rows_ref[j, n * 4 : n * 4 + 4, 128:256] = block[24 + j * 4 : 28 + j * 4]
    full = rows_ref[...].astype(BF16)
    for n in range(out_ref.shape[0]):
        out_ref[n] = full


def product(mats_ref, heads, side, contract):
    even, odd = (
        lax.dot_general(
            mats_ref[:, j].reshape(256, 256), side, (((contract,), (0,)), ((), ())), preferred_element_type=F32
        )
        for j in heads
    )
    return jnp.where(odd_chunk(even.shape), odd, even)


def scaled(value, scale, p, scores):
    chunk = 2 * p + odd_chunk(value.shape).astype(jnp.int32)
    return (value * jnp.where((chunk < 3) == scores, scale, 1.0)).astype(BF16)


def put(refs, value, p):
    for n, ref in enumerate(refs):
        seqs, res, _ = ref.shape
        for s in range(seqs):
            ref[s, :, p * 128 : p * 128 + 128] = value[n * res : (n + 1) * res, s * 128 : s * 128 + 128]


def row_kernel(scale, place_ref, mats_ref, right_ref, row_hbm, row_ref, sems):
    copies = [pltpu.make_async_copy(row_ref.at[:, slot], row_hbm.at[:, slot], sems.at[slot]) for slot in range(2)]
    for slot in range(2):
        for p in range(3):
            heads = [(j + 3 * slot) % 6 for j in (2 * p, 2 * p + 1)]
            value = product(mats_ref, heads, slab(rights(place_ref, right_ref, slot), p), 1)
            put([row_ref.at[n, slot] for n in range(4)], scaled(value, scale, p, slot == 0), p)
        copies[slot].start()
    for copy in copies:
        copy.wait()


def col_kernel(scale, mats_ref, q_ref, g_ref, *refs):
    col_hbms, col_ref, sems = refs[:4], refs[4], refs[5]
    for which, ref in enumerate((q_ref, g_ref)):
        for p in range(3):
            heads = [j % 3 + 3 * which for j in (2 * p, 2 * p + 1)]
            value = product(mats_ref, heads, slab(lefts(ref), p), 0)
            put([col_ref.at[n, which] for n in range(4)], (value * scale if which == 0 else value).astype(BF16), p)
    copies = [pltpu.make_async_copy(col_ref.at[n], col_hbms[n], sems.at[n]) for n in range(4)]
    for copy in copies:
        copy.start()
    for copy in copies:
        copy.wait()


def four(refs, s):
    p = [ref[s].astype(F32) for ref in refs]
    return ((p[0] + p[1]) + (p[2] + p[3])).astype(BF16)


def total_columns_kernel(zero_ref, one_ref, two_ref, three_ref, keep_ref, send_ref):
    refs = (zero_ref, one_ref, two_ref, three_ref)
    low = low_lanes(keep_ref.shape[1:])
    for s in range(keep_ref.shape[0]):
        keys = four([ref.at[0] for ref in refs], s)
        values = four([ref.at[1] for ref in refs], s)
        keep_ref[s] = jnp.where(low, keys, values)
        send_ref[s] = jnp.where(low, values, keys)


def total_rows_kernel(row_ref, keep_ref, send_ref):
    for s in range(keep_ref.shape[0]):
        keep_ref[s] = four([row_ref.at[n, 0] for n in range(4)], s)
        send_ref[s] = four([row_ref.at[n, 1] for n in range(4)], s)


def unpacked(first, keep, got):
    low = low_lanes(keep.shape)
    one, two = jnp.where(low, keep, got), jnp.where(low, got, keep)
    half = keep.shape[1] // 2
    turned = [jnp.concatenate([a[:, half:], a[:, :half]], axis=1) for a in (one, two)]
    return jnp.where(first, one, turned[0]), jnp.where(first, turned[1], two)


def finish_columns_kernel(place_ref, keep_ref, got_ref, gk_ref, gv_ref):
    first = place_ref[0] == 0
    for s in range(keep_ref.shape[0]):
        gk_ref[s], gv_ref[s] = unpacked(first, keep_ref[s], got_ref[s])


def finish_rows_kernel(place_ref, keep_ref, got_ref, w_ref, mixed_ref, gq_ref):
    seqs, res, width = keep_ref.shape
    keep, got = keep_ref[...].reshape(seqs * res, width), got_ref[...].reshape(seqs * res, width)
    grad_query, attended = unpacked(place_ref[0] == 0, keep, got)
    gq_ref[...] = grad_query.reshape(seqs, res, width)
    mixed = jnp.dot(attended, w_ref[...], preferred_element_type=F32).astype(BF16)
    mixed_ref[...] = mixed.reshape(mixed_ref.shape)


def on_device(queries, keys, values, out_weight, grad_out):
    seqs, res, width = queries.shape
    model_dim = out_weight.shape[1]
    scale = 1.0 / math.sqrt(width // HEADS * seqs * 32)
    place = jnp.stack([lax.axis_index("c"), lax.axis_index("x")]).astype(jnp.int32)
    block = (seqs, res, width)
    smem = pl.BlockSpec(memory_space=pltpu.SMEM)
    vmem = pl.BlockSpec(memory_space=pltpu.VMEM)
    hbm = pl.BlockSpec(memory_space=pltpu.HBM)

    def array(shape, dtype=BF16):
        return jax.ShapeDtypeStruct(shape, dtype)

    args = (queries, keys, values, out_weight, grad_out)
    own, send, right = pl.pallas_call(
        pack_kernel,
        in_specs=[smem] + [hbm] * 5,
        out_specs=[vmem] * 3,
        out_shape=(array(block), array(block), array((4, 2) + block)),
        scratch_shapes=[pltpu.VMEM(a.shape, BF16) for a in (queries, keys, values, out_weight, grad_out)]
        + [pltpu.SemaphoreType.DMA((5,))],
        compiler_params=params(),
        name="pack",
    )(place, *(pltpu.with_memory_space_constraint(arg, pltpu.HBM) for arg in args))
    right = exchange(right.reshape((8,) + block), ("x", "c")).reshape((4, 2) + block)
    left_q, left_g = pl.pallas_call(
        mix_kernel, out_shape=(array(block), array(block)), compiler_params=params(), name="mix"
    )(own, shift(send, "c", 1))

    def products(own_first, left, name):
        return pl.pallas_call(
            lambda *refs: product_kernel(own_first, *refs),
            in_specs=[smem] + [vmem] * 2,
            out_shape=array((4, 3, 64, 256), F32),
            compiler_params=params(),
            name=name,
        )(place, left, right)

    left_q = lax.all_gather(left_q, "zl")
    logits = products(True, left_q, "logits")
    left_g, logits = lax.optimization_barrier((left_g, logits))
    logits = exchange(logits, "y")
    left_g = lax.all_gather(left_g, "zl")
    weight_grads = exchange(products(False, left_g, "weight_grads"), "y")
    partial = pl.pallas_call(
        rows_kernel, out_shape=array((16, 24, 256), F32), compiler_params=params(), name="rows"
    )(logits, weight_grads)
    partial = exchange(partial, ("zh", "zl"))
    mats = pl.pallas_call(
        lambda *refs: softmax_kernel(scale, *refs),
        out_shape=array((16, 48, 128)),
        compiler_params=params(),
        name="softmax",
    )(partial)
    mats = exchange(mats, ("zh", "zl"))
    mats = pl.pallas_call(
        unpack_kernel,
        out_shape=array((4, 6, 64, 256)),
        scratch_shapes=[pltpu.VMEM((6, 64, 256), F32)],
        compiler_params=params(),
        name="unpack",
    )(mats)
    mats = exchange(mats, "y")

    (row,) = pl.pallas_call(
        lambda *refs: row_kernel(scale, *refs),
        in_specs=[smem] + [vmem] * 2,
        out_specs=[hbm],
        out_shape=(pltpu.HBM((4, 2) + block, BF16),),
        scratch_shapes=[pltpu.VMEM((4, 2) + block, BF16), pltpu.SemaphoreType.DMA((2,))],
        compiler_params=params(),
        name="row_products",
    )(place, mats, right)
    cols = pl.pallas_call(
        lambda *refs: col_kernel(scale, *refs),
        in_specs=[vmem] * 3,
        out_specs=[hbm] * 4,
        out_shape=(pltpu.HBM((2,) + block, BF16),) * 4,
        scratch_shapes=[pltpu.VMEM((4, 2) + block, BF16), pltpu.SemaphoreType.DMA((4,))],
        compiler_params=params(),
        name="col_products",
    )(mats, left_q, left_g)
    row = exchange(row, "zl")
    cols = [cols[0]] + [shift(cols[by], "x", -by) for by in (1, 2, 3)]
    keep, send = pl.pallas_call(
        total_columns_kernel, out_shape=(array(block), array(block)), compiler_params=params(), name="total_columns"
    )(*cols)
    grad_key, grad_value = pl.pallas_call(
        finish_columns_kernel,
        in_specs=[smem, vmem, vmem],
        out_shape=(array(block), array(block)),
        compiler_params=params(),
        name="finish_columns",
    )(place, keep, shift(send, "c", 1))
    keep, send = pl.pallas_call(
        total_rows_kernel, out_shape=(array(block), array(block)), compiler_params=params(), name="total_rows"
    )(row)
    mixed, grad_query = pl.pallas_call(
        finish_rows_kernel,
        in_specs=[smem] + [vmem] * 3,
        out_shape=(array((seqs, res, model_dim)), array(block)),
        compiler_params=params(),
        name="finish_rows",
    )(place, keep, shift(send, "c", 1), out_weight)
    return mixed, grad_query, grad_key, grad_value


def solution(mesh):
    grid = Mesh(mesh.devices.reshape(4, 4, 2, 4, 4), ("zh", "y", "c", "x", "zl"))
    placed = P(("zh", "y", "c"), ("x", "zl"), None)
    return jax.shard_map(
        on_device,
        mesh=grid,
        in_specs=(placed, placed, placed, P(), placed),
        out_specs=(placed, placed, placed, placed),
        check_vma=False,
    )
```

```python
import math

import jax
import jax.numpy as jnp
from jax import lax
from jax.experimental import pallas as pl
from jax.experimental.pallas import tpu as pltpu
from jax.sharding import Mesh, PartitionSpec as P

HEADS = 6
F32 = jnp.float32
BF16 = jnp.bfloat16
VMEM = 16 * 1024 * 1024


def params():
    return pltpu.CompilerParams(vmem_limit_bytes=VMEM)


def exchange(blocks, axis):
    return lax.all_to_all(blocks, axis, 0, 0, tiled=True)


def shift(block, axis, by):
    n = lax.axis_size(axis)
    return lax.ppermute(block, axis, [(i, (i + by) % n) for i in range(n)])


def halves(one, two):
    half = one.shape[1] // 2
    return (
        jnp.concatenate([one[:, :half], two[:, :half]], axis=1),
        jnp.concatenate([one[:, half:], two[:, half:]], axis=1),
    )


def low_lanes(shape):
    return lax.broadcasted_iota(jnp.int32, shape, 1) < shape[1] // 2


def pack_kernel(place_ref, q_hbm, k_hbm, v_hbm, w_hbm, go_hbm, own_ref, send_ref, right_ref, q_ref, k_ref, v_ref, w_ref, go_ref, sems):
    loads = [
        pltpu.make_async_copy(src, dst, sems.at[n])
        for n, (src, dst) in enumerate(
            ((w_hbm, w_ref), (go_hbm, go_ref), (k_hbm, k_ref), (v_hbm, v_ref), (q_hbm, q_ref))
        )
    ]
    for load in loads:
        load.start()
    first = place_ref[0] == 0
    loads[0].wait()
    loads[1].wait()
    seqs, res, _ = q_ref.shape
    grads = lax.dot_general(
        go_ref[...].reshape(seqs * res, go_ref.shape[2]),
        w_ref[...],
        (((1,), (1,)), ((), ())),
        preferred_element_type=F32,
    ).astype(BF16)
    for load in loads[2:]:
        load.wait()
    for s in range(seqs):
        kv = halves(k_ref[s], v_ref[s])
        vk = halves(v_ref[s], k_ref[s])
        for core, part in enumerate((jnp.where(first, kv[0], vk[0]), jnp.where(first, vk[1], kv[1]))):
            for n in range(right_ref.shape[0]):
                right_ref[n, core, s] = part
        q, g = q_ref[s], grads[s * res : (s + 1) * res]
        qg, gq = halves(q, g), halves(g, q)
        own_ref[s] = jnp.where(first, qg[0], qg[1])
        send_ref[s] = jnp.where(first, gq[1], gq[0])


def mix_kernel(own_ref, got_ref, low_ref, high_ref):
    for s in range(own_ref.shape[0]):
        low = low_lanes(own_ref.shape[1:])
        low_ref[s] = jnp.where(low, own_ref[s], got_ref[s])
        high_ref[s] = jnp.where(low, got_ref[s], own_ref[s])


def slab(blocks, p):
    at = slice(p * 128, p * 128 + 128)
    rows = [
        jnp.concatenate([ref[s, :, at] for ref in row for s in range(ref.shape[0])], axis=1) for row in blocks
    ]
    return jnp.concatenate(rows, axis=0)


def lefts(ref):
    return [(ref.at[n],) for n in range(4)]


def rights(place_ref, ref, slot):
    core = place_ref[0] if slot == 0 else 1 - place_ref[0]
    return [(ref.at[lax.rem(place_ref[1] + 4 - n, 4), core],) for n in range(4)]


def odd_chunk(shape):
    return (lax.broadcasted_iota(jnp.int32, shape, 1) // 64) % 2 == 1


def tile_products(own_first, place_ref, left_ref, right_ref, out_ref):
    own, other = (0, 1) if own_first else (1, 0)
    left = [slab(lefts(left_ref), p) for p in range(3)]
    right = [[slab(rights(place_ref, right_ref, slot), p) for p in range(3)] for slot in range(2)]
    odd = odd_chunk(left[0].shape)
    zero = jnp.zeros_like(left[0])
    for t in range(3):
        ones, others = [], []
        for chunk, slot in ((t, own), (t + 3, other)):
            part = left[chunk // 2]
            ones.append(jnp.where(odd, part, zero) if chunk % 2 else jnp.where(odd, zero, part))
            others.append(right[slot][chunk // 2])
        full = lax.dot_general(
            jnp.concatenate(ones, axis=1),
            jnp.concatenate(others, axis=1),
            (((1,), (1,)), ((), ())),
            preferred_element_type=F32,
        )
        out_ref[:, t] = full.reshape(out_ref.shape[0], out_ref.shape[2], out_ref.shape[3])


def logits_kernel(place_ref, left_ref, right_ref, out_ref):
    tile_products(True, place_ref, left_ref, right_ref, out_ref)


def weight_grads_kernel(place_ref, left_ref, right_ref, own_hbm, one_hbm, two_hbm, three_hbm, all_ref, sems):
    tile_products(False, place_ref, left_ref, right_ref, all_ref)
    copies = []
    for by, hbm in enumerate((own_hbm, one_hbm, two_hbm, three_hbm)):
        copies.append(pltpu.make_async_copy(all_ref.at[lax.rem(place_ref[2] + by, 4)], hbm, sems.at[by]))
    for copy in copies:
        copy.start()
    for copy in copies:
        copy.wait()


def cut_rows(total, out_ref):
    for n in range(16):
        for t in range(3):
            rows = total[t, n * 4 : n * 4 + 4]
            out_ref[n, t * 4 : t * 4 + 4] = rows[:, :128]
            out_ref[n, 12 + t * 4 : 16 + t * 4] = rows[:, 128:]


def logit_rows_kernel(part_ref, out_ref):
    cut_rows((part_ref[0] + part_ref[1]) + (part_ref[2] + part_ref[3]), out_ref)


def grad_rows_kernel(own_ref, one_ref, two_ref, three_ref, out_ref):
    cut_rows((own_ref[...] + one_ref[...]) + (two_ref[...] + three_ref[...]), out_ref)


def whole_rows(part_ref):
    tiles = []
    for col in range(4):
        parts = [part_ref[n * 4 + col] for n in range(4)]
        total = (parts[0] + parts[1]) + (parts[2] + parts[3])
        tiles += [total[:12], total[12:]]
    return jnp.concatenate(tiles, axis=1)


def deal_rows(value, out_ref):
    for col in range(4):
        at = col * 256
        tile = jnp.concatenate([value[:, at : at + 128], value[:, at + 128 : at + 256]], axis=0).astype(BF16)
        for n in range(col, 16, 4):
            out_ref[n] = tile


def weights_kernel(scale, part_ref, weights_ref, out_ref):
    logits = whole_rows(part_ref) * scale
    expo = jnp.exp(logits - jnp.max(logits, axis=-1, keepdims=True))
    weights = expo / jnp.sum(expo, axis=-1, keepdims=True)
    weights_ref[...] = weights
    deal_rows(weights, out_ref)


def scores_kernel(weights_ref, part_ref, out_ref):
    weights, grads = weights_ref[...], whole_rows(part_ref)
    deal_rows(weights * (grads - jnp.sum(weights * grads, axis=-1, keepdims=True)), out_ref)


def unpack_rows(rows_in_ref, rows_ref):
    for n in range(16):
        block = rows_in_ref[n].astype(F32)
        for t in range(3):
            rows_ref[t, n * 4 : n * 4 + 4, 0:128] = block[t * 4 : t * 4 + 4]
            rows_ref[t, n * 4 : n * 4 + 4, 128:256] = block[12 + t * 4 : 16 + t * 4]
    return rows_ref[...].astype(BF16)


def unpack_kernel(rows_in_ref, out_ref, rows_ref):
    out_ref[...] = unpack_rows(rows_in_ref, rows_ref)


def unpack_copies_kernel(rows_in_ref, out_ref, rows_ref):
    full = unpack_rows(rows_in_ref, rows_ref)
    for n in range(out_ref.shape[0]):
        out_ref[n] = full


def product(mats_ref, heads, side, contract):
    even, odd = (
        lax.dot_general(
            mats_ref[:, j].reshape(256, 256), side, (((contract,), (0,)), ((), ())), preferred_element_type=F32
        )
        for j in heads
    )
    return jnp.where(odd_chunk(even.shape), odd, even)


def put(refs, value, p):
    for n, ref in enumerate(refs):
        seqs, res, _ = ref.shape
        for s in range(seqs):
            ref[s, :, p * 128 : p * 128 + 128] = value[n * res : (n + 1) * res, s * 128 : s * 128 + 128]


def mixed_rights(place_ref, right_ref, low_slot, p):
    low, high = (slab(rights(place_ref, right_ref, slot), p) for slot in (low_slot, 1 - low_slot))
    if p == 1:
        return jnp.where(odd_chunk(low.shape), high, low)
    return low if p == 0 else high


def rows_into(factor, low_slot, place_ref, mats_ref, right_ref, row_ref):
    for p in range(3):
        value = product(mats_ref, [j % 3 for j in (2 * p, 2 * p + 1)], mixed_rights(place_ref, right_ref, low_slot, p), 1)
        put([row_ref.at[n] for n in range(4)], (value if factor is None else value * factor).astype(BF16), p)


def attended_kernel(place_ref, mats_ref, right_ref, own_hbm, one_hbm, two_hbm, three_hbm, row_ref, sems):
    rows_into(None, 1, place_ref, mats_ref, right_ref, row_ref)
    copies = []
    for by, hbm in enumerate((own_hbm, one_hbm, two_hbm, three_hbm)):
        copies.append(pltpu.make_async_copy(row_ref.at[lax.rem(place_ref[3] + by, 4)], hbm, sems.at[by]))
    for copy in copies:
        copy.start()
    for copy in copies:
        copy.wait()


def grad_query_kernel(scale, place_ref, mats_ref, right_ref, row_hbm, row_ref, sem):
    rows_into(scale, 0, place_ref, mats_ref, right_ref, row_ref)
    copy = pltpu.make_async_copy(row_ref, row_hbm, sem)
    copy.start()
    copy.wait()


def col_kernel(factor, mats_ref, left_ref, *refs):
    col_hbms, col_ref, sems = refs[:4], refs[4], refs[5]
    for p in range(3):
        value = product(mats_ref, [j % 3 for j in (2 * p, 2 * p + 1)], slab(lefts(left_ref), p), 0)
        put([col_ref.at[n] for n in range(4)], (value if factor is None else value * factor).astype(BF16), p)
    copies = [pltpu.make_async_copy(col_ref.at[n], col_hbms[n], sems.at[n]) for n in range(4)]
    for copy in copies:
        copy.start()
    for copy in copies:
        copy.wait()


def four(refs, s):
    p = [ref[s].astype(F32) for ref in refs]
    return ((p[0] + p[1]) + (p[2] + p[3])).astype(BF16)


def total_kernel(zero_ref, one_ref, two_ref, three_ref, out_ref):
    for s in range(out_ref.shape[0]):
        out_ref[s] = four((zero_ref, one_ref, two_ref, three_ref), s)


def total_blocks_kernel(part_ref, out_ref):
    total_kernel(*[part_ref.at[n] for n in range(4)], out_ref)


def turned(array):
    half = array.shape[1] // 2
    return jnp.concatenate([array[:, half:], array[:, :half]], axis=1)


def flat(ref):
    return ref[...].reshape(ref.shape[0] * ref.shape[1], ref.shape[2])


def own_first(first, own, got):
    both = jnp.where(low_lanes(own.shape), own, got)
    return jnp.where(first, both, turned(both))


def own_last(first, own, got):
    both = jnp.where(low_lanes(own.shape), got, own)
    return jnp.where(first, turned(both), both)


def finish_mixed_kernel(place_ref, own_ref, got_ref, w_ref, mixed_ref):
    attended = own_last(place_ref[0] == 0, flat(own_ref), flat(got_ref))
    mixed = jnp.dot(attended, w_ref[...], preferred_element_type=F32).astype(BF16)
    mixed_ref[...] = mixed.reshape(mixed_ref.shape)


def finish_last_kernel(place_ref, own_ref, got_ref, out_ref):
    out_ref[...] = own_last(place_ref[0] == 0, flat(own_ref), flat(got_ref)).reshape(out_ref.shape)


def finish_first_kernel(place_ref, own_ref, got_ref, out_ref):
    out_ref[...] = own_first(place_ref[0] == 0, flat(own_ref), flat(got_ref)).reshape(out_ref.shape)


def on_device(queries, keys, values, out_weight, grad_out):
    seqs, res, width = queries.shape
    model_dim = out_weight.shape[1]
    scale = 1.0 / math.sqrt(width // HEADS * seqs * 32)
    place = jnp.stack([lax.axis_index(axis) for axis in ("c", "x", "y", "zl")]).astype(jnp.int32)
    block = (seqs, res, width)
    smem = pl.BlockSpec(memory_space=pltpu.SMEM)
    vmem = pl.BlockSpec(memory_space=pltpu.VMEM)
    hbm = pl.BlockSpec(memory_space=pltpu.HBM)

    def array(shape, dtype=BF16):
        return jax.ShapeDtypeStruct(shape, dtype)

    args = (queries, keys, values, out_weight, grad_out)
    own, send, right = pl.pallas_call(
        pack_kernel,
        in_specs=[smem] + [hbm] * 5,
        out_specs=[vmem] * 3,
        out_shape=(array(block), array(block), array((4, 2) + block)),
        scratch_shapes=[pltpu.VMEM(a.shape, BF16) for a in (queries, keys, values, out_weight, grad_out)]
        + [pltpu.SemaphoreType.DMA((5,))],
        compiler_params=params(),
        name="pack",
    )(place, *(pltpu.with_memory_space_constraint(arg, pltpu.HBM) for arg in args))
    right = exchange(right.reshape((8,) + block), ("x", "c")).reshape((4, 2) + block)
    left_q, left_g = pl.pallas_call(
        mix_kernel, out_shape=(array(block), array(block)), compiler_params=params(), name="mix"
    )(own, shift(send, "c", 1))

    def call(kernel, out_shape, name, *operands, **more):
        specs = [smem if a is place else vmem for a in operands]
        return pl.pallas_call(
            kernel, in_specs=specs, out_shape=out_shape, compiler_params=params(), name=name, **more
        )(*operands)

    dealt_wide, dealt = array((16, 24, 128), F32), pltpu.HBM((16, 24, 128), BF16)
    unpacking = dict(scratch_shapes=[pltpu.VMEM((3, 64, 256), F32)])
    four_hbm = dict(
        out_specs=[hbm] * 4, scratch_shapes=[pltpu.VMEM((4,) + block, BF16), pltpu.SemaphoreType.DMA((4,))]
    )
    four_blocks = (pltpu.HBM(block, BF16),) * 4

    left_q = lax.all_gather(left_q, "zl")
    logits = call(logits_kernel, array((4, 3, 64, 256), F32), "logits", place, left_q, right)
    left_g, logits = lax.optimization_barrier((left_g, logits))
    logits = exchange(logits, "y")
    left_g = lax.all_gather(left_g, "zl")
    logits = call(logit_rows_kernel, dealt_wide, "logit_rows", logits)
    left_g, logits = lax.optimization_barrier((left_g, logits))
    logits = exchange(logits, ("zh", "zl"))
    grads = call(
        weight_grads_kernel,
        (pltpu.HBM((3, 64, 256), F32),) * 4,
        "weight_grads",
        place,
        left_g,
        right,
        out_specs=[hbm] * 4,
        scratch_shapes=[pltpu.VMEM((4, 3, 64, 256), F32), pltpu.SemaphoreType.DMA((4,))],
    )
    logits, _ = lax.optimization_barrier((logits, grads))
    grads = [grads[0]] + [shift(grads[by], "y", by) for by in (1, 2, 3)]
    weights, dealt_weights = call(
        lambda *refs: weights_kernel(scale, *refs), (pltpu.HBM((12, 1024), F32), dealt), "weights", logits
    )
    dealt_weights = exchange(dealt_weights, ("zh", "zl"))
    grads = call(grad_rows_kernel, dealt_wide, "grad_rows", *grads)
    dealt_weights, grads = lax.optimization_barrier((dealt_weights, grads))
    grads = exchange(grads, ("zh", "zl"))
    mats = lax.all_gather(call(unpack_kernel, array((3, 64, 256)), "unpack_weights", dealt_weights, **unpacking), "y")
    rows = call(attended_kernel, four_blocks, "attended", place, mats, right, **four_hbm)
    grads, _ = lax.optimization_barrier((grads, rows))
    rows = [rows[0]] + [shift(rows[by], "zl", by) for by in (1, 2, 3)]
    cols_made = call(lambda *refs: col_kernel(None, *refs), four_blocks, "grad_value", mats, left_g, **four_hbm)
    cols = [cols_made[0]] + [shift(cols_made[by], "x", -by) for by in (1, 2, 3)]

    scores = exchange(call(scores_kernel, dealt, "scores", weights, grads), ("zh", "zl"))
    scores, _, _ = lax.optimization_barrier((scores, cols_made, rows[1]))
    mats = exchange(call(unpack_copies_kernel, array((4, 3, 64, 256)), "unpack_scores", scores, **unpacking), "y")
    (row,) = call(
        lambda *refs: grad_query_kernel(scale, *refs),
        (pltpu.HBM((4,) + block, BF16),),
        "grad_query",
        place,
        mats,
        right,
        out_specs=[hbm],
        scratch_shapes=[pltpu.VMEM((4,) + block, BF16), pltpu.SemaphoreType.DMA],
    )
    row, rows = lax.optimization_barrier((row, rows))
    row = exchange(row, "zl")
    key_cols = call(lambda *refs: col_kernel(scale, *refs), four_blocks, "grad_key", mats, left_q, **four_hbm)
    key_cols = [key_cols[0]] + [shift(key_cols[by], "x", -by) for by in (1, 2, 3)]

    attended = call(total_kernel, array(block), "total_attended", *rows)
    mixed = call(
        finish_mixed_kernel,
        array((seqs, res, model_dim)),
        "finish_mixed",
        place,
        attended,
        shift(attended, "c", 1),
        out_weight,
    )
    value = call(total_kernel, array(block), "total_grad_value", *cols)
    grad_value = call(finish_last_kernel, array(block), "finish_grad_value", place, value, shift(value, "c", 1))
    key = call(total_kernel, array(block), "total_grad_key", *key_cols)
    grad_key = call(finish_first_kernel, array(block), "finish_grad_key", place, key, shift(key, "c", 1))
    query = call(total_blocks_kernel, array(block), "total_grad_query", row)
    grad_query = call(finish_first_kernel, array(block), "finish_grad_query", place, query, shift(query, "c", 1))
    return mixed, grad_query, grad_key, grad_value


def solution(mesh):
    grid = Mesh(mesh.devices.reshape(4, 4, 2, 4, 4), ("zh", "y", "c", "x", "zl"))
    placed = P(("zh", "y", "c"), ("x", "zl"), None)
    return jax.shard_map(
        on_device,
        mesh=grid,
        in_specs=(placed, placed, placed, P(), placed),
        out_specs=(placed, placed, placed, placed),
        check_vma=False,
    )
```

```python
import math

import jax
import jax.numpy as jnp
from jax import lax
from jax.experimental import pallas as pl
from jax.experimental.pallas import tpu as pltpu
from jax.sharding import Mesh, PartitionSpec as P

HEADS = 6
F32 = jnp.float32
BF16 = jnp.bfloat16
VMEM = 16 * 1024 * 1024


def params():
    return pltpu.CompilerParams(vmem_limit_bytes=VMEM)


def exchange(blocks, axis):
    return lax.all_to_all(blocks, axis, 0, 0, tiled=True)


def shift(block, axis, by):
    n = lax.axis_size(axis)
    return lax.ppermute(block, axis, [(i, (i + by) % n) for i in range(n)])


def halves(one, two):
    half = one.shape[1] // 2
    return (
        jnp.concatenate([one[:, :half], two[:, :half]], axis=1),
        jnp.concatenate([one[:, half:], two[:, half:]], axis=1),
    )


def pack_kernel(
    place_ref, q_hbm, k_hbm, v_hbm, w_hbm, go_hbm, own_ref, send_ref, right_hbm, q_ref, k_ref, v_ref, w_ref, go_ref, kv_ref, sems
):
    loads = [
        pltpu.make_async_copy(src, dst, sems.at[n])
        for n, (src, dst) in enumerate(
            ((k_hbm, k_ref), (v_hbm, v_ref), (w_hbm, w_ref), (go_hbm, go_ref), (q_hbm, q_ref))
        )
    ]
    for load in loads:
        load.start()
    first = place_ref[0] == 0
    seqs, res, _ = q_ref.shape
    loads[0].wait()
    loads[1].wait()
    for s in range(seqs):
        kv_ref[0, s], kv_ref[1, s] = halves(k_ref[s], v_ref[s])
    stores = [pltpu.make_async_copy(kv_ref, right_hbm.at[n], sems.at[5 + n]) for n in range(4)]
    for store in stores:
        store.start()
    for load in loads[2:]:
        load.wait()
    grads = lax.dot_general(
        go_ref[...].reshape(seqs * res, go_ref.shape[2]),
        w_ref[...],
        (((1,), (1,)), ((), ())),
        preferred_element_type=F32,
    ).astype(BF16)
    for s in range(seqs):
        low, high = halves(q_ref[s], grads[s * res : (s + 1) * res])
        own_ref[s] = jnp.where(first, low, high)
        send_ref[s] = jnp.where(first, high, low)
    for store in stores:
        store.wait()


def slab(blocks, p):
    at = slice(p * 128, p * 128 + 128)
    rows = [
        jnp.concatenate([ref[s, :, at] for ref in row for s in range(ref.shape[0])], axis=1) for row in blocks
    ]
    return jnp.concatenate(rows, axis=0)


def lefts(own_ref, other_ref):
    return [(own_ref.at[n], other_ref.at[n]) for n in range(4)]


def rights(place_ref, ref):
    core = place_ref[0]
    x = [lax.rem(place_ref[1] + 4 - n, 4) for n in range(4)]
    return [(ref.at[x[n], core], ref.at[x[n], 1 - core]) for n in range(4)]


def odd_chunk(shape):
    return (lax.broadcasted_iota(jnp.int32, shape, 1) // 64) % 2 == 1


def product_kernel(place_ref, own_ref, other_ref, right_ref, out_ref):
    for p in range(3):
        left = slab(lefts(own_ref, other_ref), p)
        right = slab(rights(place_ref, right_ref), p)
        odd = odd_chunk(left.shape)
        zero = jnp.zeros_like(left)
        for parity, part in enumerate((jnp.where(odd, zero, left), jnp.where(odd, left, zero))):
            full = lax.dot_general(part, right, (((1,), (1,)), ((), ())), preferred_element_type=F32)
            out_ref[:, 2 * p + parity] = full.reshape(out_ref.shape[0], out_ref.shape[2], out_ref.shape[3])


def rows_kernel(part_ref, out_ref):
    total = (part_ref[0] + part_ref[1]) + (part_ref[2] + part_ref[3])
    for n in range(16):
        for j in range(6):
            out_ref[n, j * 4 : j * 4 + 4] = total[j, n * 4 : n * 4 + 4]


def softmax_kernel(scale, part_ref, out_ref):
    tiles = []
    for col in range(4):
        parts = [part_ref[n * 4 + col] for n in range(4)]
        tiles.append((parts[0] + parts[1]) + (parts[2] + parts[3]))
    total = jnp.concatenate(tiles, axis=1)
    logits = total[:12] * scale
    grads = total[12:]
    expo = jnp.exp(logits - jnp.max(logits, axis=-1, keepdims=True))
    weights = expo / jnp.sum(expo, axis=-1, keepdims=True)
    scores = weights * (grads - jnp.sum(weights * grads, axis=-1, keepdims=True))
    full = jnp.concatenate([scores, weights], axis=0)
    for col in range(4):
        at = col * 256
        tile = jnp.concatenate([full[:, at : at + 128], full[:, at + 128 : at + 256]], axis=0).astype(BF16)
        for n in range(col, 16, 4):
            out_ref[n] = tile


def unpack_kernel(mats_ref, out_ref, rows_ref):
    for n in range(16):
        block = mats_ref[n].astype(F32)
        for j in range(6):
            rows_ref[j, n * 4 : n * 4 + 4, 0:128] = block[j * 4 : j * 4 + 4]
            rows_ref[j, n * 4 : n * 4 + 4, 128:256] = block[24 + j * 4 : 28 + j * 4]
    full = rows_ref[...].astype(BF16)
    for n in range(out_ref.shape[0]):
        out_ref[n] = full


def product(mats_ref, p, side, contract, scale):
    even, odd = (
        lax.dot_general(
            mats_ref[:, j].reshape(256, 256), side, (((contract,), (0,)), ((), ())), preferred_element_type=F32
        )
        for j in (2 * p, 2 * p + 1)
    )
    if 2 * p < 3:
        even = even * scale
    if 2 * p + 1 < 3:
        odd = odd * scale
    return jnp.where(odd_chunk(even.shape), odd, even).astype(BF16)


def put(refs, value, p):
    for n, ref in enumerate(refs):
        seqs, res, _ = ref.shape
        for s in range(seqs):
            ref[s, :, p * 128 : p * 128 + 128] = value[n * res : (n + 1) * res, s * 128 : s * 128 + 128]


def row_kernel(scale, place_ref, mats_ref, right_ref, row_hbm, mats_hbm, row_ref, sems):
    handed = pltpu.make_async_copy(mats_ref, mats_hbm, sems.at[2])
    handed.start()
    copies = [pltpu.make_async_copy(row_ref.at[:, slot], row_hbm.at[:, slot], sems.at[slot]) for slot in range(2)]
    blocks = rights(place_ref, right_ref)
    for slot in range(2):
        for p in range(3):
            side = slab([(pair[slot],) for pair in blocks], p)
            put([row_ref.at[n, slot] for n in range(4)], product(mats_ref, p, side, 1, scale), p)
        copies[slot].start()
    handed.wait()
    for copy in copies:
        copy.wait()


def col_kernel(scale, mats_ref, own_ref, other_ref, *refs):
    col_hbms, col_ref, sems = refs[:4], refs[4], refs[5]
    for slot, ref in enumerate((own_ref, other_ref)):
        for p in range(3):
            side = slab([(ref.at[n],) for n in range(4)], p)
            put([col_ref.at[n, slot] for n in range(4)], product(mats_ref, p, side, 0, scale), p)
    copies = [pltpu.make_async_copy(col_ref.at[n], col_hbms[n], sems.at[n]) for n in range(4)]
    for copy in copies:
        copy.start()
    for copy in copies:
        copy.wait()


def four(refs, s):
    p = [ref[s].astype(F32) for ref in refs]
    return ((p[0] + p[1]) + (p[2] + p[3])).astype(BF16)


def total_kernel(zero_ref, one_ref, two_ref, three_ref, keep_ref, send_ref):
    refs = (zero_ref, one_ref, two_ref, three_ref)
    for s in range(keep_ref.shape[0]):
        keep_ref[s] = four([ref.at[0] for ref in refs], s)
        send_ref[s] = four([ref.at[1] for ref in refs], s)


def total_blocks_kernel(part_ref, keep_ref, send_ref):
    total_kernel(*[part_ref.at[n] for n in range(4)], keep_ref, send_ref)


def unpacked(first, keep, got):
    return halves(jnp.where(first, keep, got), jnp.where(first, got, keep))


def finish_columns_kernel(place_ref, keep_ref, got_ref, gk_ref, gv_ref):
    first = place_ref[0] == 0
    for s in range(keep_ref.shape[0]):
        gk_ref[s], gv_ref[s] = unpacked(first, keep_ref[s], got_ref[s])


def finish_rows_kernel(place_ref, keep_ref, got_ref, w_ref, mixed_ref, gq_ref):
    seqs, res, width = keep_ref.shape
    keep, got = keep_ref[...].reshape(seqs * res, width), got_ref[...].reshape(seqs * res, width)
    grad_query, attended = unpacked(place_ref[0] == 0, keep, got)
    gq_ref[...] = grad_query.reshape(seqs, res, width)
    mixed = jnp.dot(attended, w_ref[...], preferred_element_type=F32).astype(BF16)
    mixed_ref[...] = mixed.reshape(mixed_ref.shape)


def on_device(queries, keys, values, out_weight, grad_out):
    seqs, res, width = queries.shape
    model_dim = out_weight.shape[1]
    scale = 1.0 / math.sqrt(width // HEADS * seqs * 32)
    place = jnp.stack([lax.axis_index("c"), lax.axis_index("x")]).astype(jnp.int32)
    block = (seqs, res, width)
    smem = pl.BlockSpec(memory_space=pltpu.SMEM)
    vmem = pl.BlockSpec(memory_space=pltpu.VMEM)
    hbm = pl.BlockSpec(memory_space=pltpu.HBM)

    def array(shape, dtype=BF16):
        return jax.ShapeDtypeStruct(shape, dtype)

    args = (queries, keys, values, out_weight, grad_out)
    own, send, right = pl.pallas_call(
        pack_kernel,
        in_specs=[smem] + [hbm] * 5,
        out_specs=[vmem, vmem, hbm],
        out_shape=(array(block), array(block), pltpu.HBM((4, 2) + block, BF16)),
        scratch_shapes=[pltpu.VMEM(a.shape, BF16) for a in (queries, keys, values, out_weight, grad_out)]
        + [pltpu.VMEM((2,) + block, BF16), pltpu.SemaphoreType.DMA((9,))],
        compiler_params=params(),
        name="pack",
    )(place, *(pltpu.with_memory_space_constraint(arg, pltpu.HBM) for arg in args))
    right = exchange(right.reshape((8,) + block), ("x", "c")).reshape((4, 2) + block)
    other = shift(send, "c", 1)
    own = lax.all_gather(own, "zl")
    other = lax.all_gather(other, "zl")

    partial = pl.pallas_call(
        product_kernel,
        in_specs=[smem] + [vmem] * 3,
        out_shape=array((4, 6, 64, 256), F32),
        compiler_params=params(),
        name="products",
    )(place, own, other, right)
    partial = exchange(partial, "y")
    partial = pl.pallas_call(
        rows_kernel, out_shape=array((16, 24, 256), F32), compiler_params=params(), name="rows"
    )(partial)
    partial = exchange(partial, ("zh", "zl"))
    mats = pl.pallas_call(
        lambda *refs: softmax_kernel(scale, *refs),
        out_shape=array((16, 48, 128)),
        compiler_params=params(),
        name="softmax",
    )(partial)
    mats = exchange(mats, ("zh", "zl"))
    mats = pl.pallas_call(
        unpack_kernel,
        out_shape=array((4, 6, 64, 256)),
        scratch_shapes=[pltpu.VMEM((6, 64, 256), F32)],
        compiler_params=params(),
        name="unpack",
    )(mats)
    mats = exchange(mats, "y")

    row, mats = pl.pallas_call(
        lambda *refs: row_kernel(scale, *refs),
        in_specs=[smem] + [vmem] * 2,
        out_specs=[hbm] * 2,
        out_shape=(pltpu.HBM((4, 2) + block, BF16), pltpu.HBM(mats.shape, BF16)),
        scratch_shapes=[pltpu.VMEM((4, 2) + block, BF16), pltpu.SemaphoreType.DMA((3,))],
        compiler_params=params(),
        name="row_products",
    )(place, mats, right)
    cols = pl.pallas_call(
        lambda *refs: col_kernel(scale, *refs),
        in_specs=[vmem] * 3,
        out_specs=[hbm] * 4,
        out_shape=(pltpu.HBM((2,) + block, BF16),) * 4,
        scratch_shapes=[pltpu.VMEM((4, 2) + block, BF16), pltpu.SemaphoreType.DMA((4,))],
        compiler_params=params(),
        name="col_products",
    )(mats, own, other)
    row = exchange(row, "zl")
    cols = [cols[0]] + [shift(cols[by], "x", -by) for by in (1, 2, 3)]
    keep, send = pl.pallas_call(
        total_kernel, out_shape=(array(block), array(block)), compiler_params=params(), name="total_columns"
    )(*cols)
    grad_key, grad_value = pl.pallas_call(
        finish_columns_kernel,
        in_specs=[smem, vmem, vmem],
        out_shape=(array(block), array(block)),
        compiler_params=params(),
        name="finish_columns",
    )(place, keep, shift(send, "c", 1))
    row, grad_key, grad_value = lax.optimization_barrier((row, grad_key, grad_value))
    keep, send = pl.pallas_call(
        total_blocks_kernel, out_shape=(array(block), array(block)), compiler_params=params(), name="total_rows"
    )(row)
    mixed, grad_query = pl.pallas_call(
        finish_rows_kernel,
        in_specs=[smem] + [vmem] * 3,
        out_shape=(array((seqs, res, model_dim)), array(block)),
        compiler_params=params(),
        name="finish_rows",
    )(place, keep, shift(send, "c", 1), out_weight)
    return mixed, grad_query, grad_key, grad_value


def solution(mesh):
    grid = Mesh(mesh.devices.reshape(4, 4, 2, 4, 4), ("zh", "y", "c", "x", "zl"))
    placed = P(("zh", "y", "c"), ("x", "zl"), None)
    return jax.shard_map(
        on_device,
        mesh=grid,
        in_specs=(placed, placed, placed, P(), placed),
        out_specs=(placed, placed, placed, placed),
        check_vma=False,
    )
```

```python
import math

import jax
import jax.numpy as jnp
from jax import lax
from jax.experimental import pallas as pl
from jax.experimental.pallas import tpu as pltpu
from jax.sharding import Mesh, PartitionSpec as P

HEADS = 6
F32 = jnp.float32
BF16 = jnp.bfloat16
VMEM = 16 * 1024 * 1024


def params():
    return pltpu.CompilerParams(vmem_limit_bytes=VMEM)


def exchange(blocks, axis):
    return lax.all_to_all(blocks, axis, 0, 0, tiled=True)


def shift(block, axis, by):
    n = lax.axis_size(axis)
    return lax.ppermute(block, axis, [(i, (i + by) % n) for i in range(n)])


def halves(one, two):
    half = one.shape[1] // 2
    return (
        jnp.concatenate([one[:, :half], two[:, :half]], axis=1),
        jnp.concatenate([one[:, half:], two[:, half:]], axis=1),
    )


def pack_kernel(
    place_ref, q_hbm, k_hbm, v_hbm, w_hbm, go_hbm, own_ref, send_ref, right_hbm, q_ref, k_ref, v_ref, w_ref, go_ref, kv_ref, sems
):
    loads = [
        pltpu.make_async_copy(src, dst, sems.at[n])
        for n, (src, dst) in enumerate(
            ((k_hbm, k_ref), (v_hbm, v_ref), (w_hbm, w_ref), (go_hbm, go_ref), (q_hbm, q_ref))
        )
    ]
    for load in loads:
        load.start()
    first = place_ref[0] == 0
    seqs, res, _ = q_ref.shape
    loads[0].wait()
    loads[1].wait()
    for s in range(seqs):
        kv_ref[0, s], kv_ref[1, s] = halves(k_ref[s], v_ref[s])
    stores = [pltpu.make_async_copy(kv_ref, right_hbm.at[n], sems.at[5 + n]) for n in range(4)]
    for store in stores:
        store.start()
    for load in loads[2:]:
        load.wait()
    grads = lax.dot_general(
        go_ref[...].reshape(seqs * res, go_ref.shape[2]),
        w_ref[...],
        (((1,), (1,)), ((), ())),
        preferred_element_type=F32,
    ).astype(BF16)
    for s in range(seqs):
        low, high = halves(q_ref[s], grads[s * res : (s + 1) * res])
        own_ref[s] = jnp.where(first, low, high)
        send_ref[s] = jnp.where(first, high, low)
    for store in stores:
        store.wait()


def slab(blocks, p):
    at = slice(p * 128, p * 128 + 128)
    rows = [
        jnp.concatenate([ref[s, :, at] for ref in row for s in range(ref.shape[0])], axis=1) for row in blocks
    ]
    return jnp.concatenate(rows, axis=0)


def lefts(own_ref, other_ref):
    return [(own_ref.at[n], other_ref.at[n]) for n in range(4)]


def rights(place_ref, ref):
    core = place_ref[0]
    x = [lax.rem(place_ref[1] + 4 - n, 4) for n in range(4)]
    return [(ref.at[x[n], core], ref.at[x[n], 1 - core]) for n in range(4)]


def odd_chunk(shape):
    return (lax.broadcasted_iota(jnp.int32, shape, 1) // 64) % 2 == 1


def product_kernel(place_ref, own_ref, other_ref, right_ref, out_ref):
    for p in range(3):
        left = slab(lefts(own_ref, other_ref), p)
        right = slab(rights(place_ref, right_ref), p)
        odd = odd_chunk(left.shape)
        zero = jnp.zeros_like(left)
        for parity, part in enumerate((jnp.where(odd, zero, left), jnp.where(odd, left, zero))):
            full = lax.dot_general(part, right, (((1,), (1,)), ((), ())), preferred_element_type=F32)
            out_ref[:, 2 * p + parity] = full.reshape(out_ref.shape[0], out_ref.shape[2], out_ref.shape[3])


def rows_kernel(part_ref, out_ref):
    total = (part_ref[0] + part_ref[1]) + (part_ref[2] + part_ref[3])
    for n in range(16):
        for j in range(6):
            out_ref[n, j * 4 : j * 4 + 4] = total[j, n * 4 : n * 4 + 4]


def softmax_kernel(scale, part_ref, out_ref):
    tiles = []
    for col in range(4):
        parts = [part_ref[n * 4 + col] for n in range(4)]
        tiles.append((parts[0] + parts[1]) + (parts[2] + parts[3]))
    total = jnp.concatenate(tiles, axis=1)
    logits = total[:12] * scale
    grads = total[12:]
    expo = jnp.exp(logits - jnp.max(logits, axis=-1, keepdims=True))
    weights = expo / jnp.sum(expo, axis=-1, keepdims=True)
    scores = weights * (grads - jnp.sum(weights * grads, axis=-1, keepdims=True))
    full = jnp.concatenate([scores, weights], axis=0)
    for col in range(4):
        at = col * 256
        tile = jnp.concatenate([full[:, at : at + 128], full[:, at + 128 : at + 256]], axis=0).astype(BF16)
        for n in range(col, 16, 4):
            out_ref[n] = tile


def unpack_kernel(mats_ref, out_ref, rows_ref):
    for n in range(16):
        block = mats_ref[n].astype(F32)
        for j in range(6):
            rows_ref[j, n * 4 : n * 4 + 4, 0:128] = block[j * 4 : j * 4 + 4]
            rows_ref[j, n * 4 : n * 4 + 4, 128:256] = block[24 + j * 4 : 28 + j * 4]
    full = rows_ref[...].astype(BF16)
    for n in range(out_ref.shape[0]):
        out_ref[n] = full


def product(mats_ref, p, side, contract, scale):
    even, odd = (
        lax.dot_general(
            mats_ref[:, j].reshape(256, 256), side, (((contract,), (0,)), ((), ())), preferred_element_type=F32
        )
        for j in (2 * p, 2 * p + 1)
    )
    if 2 * p < 3:
        even = even * scale
    if 2 * p + 1 < 3:
        odd = odd * scale
    return jnp.where(odd_chunk(even.shape), odd, even).astype(BF16)


def put(refs, value, p):
    for n, ref in enumerate(refs):
        seqs, res, _ = ref.shape
        for s in range(seqs):
            ref[s, :, p * 128 : p * 128 + 128] = value[n * res : (n + 1) * res, s * 128 : s * 128 + 128]


def row_kernel(scale, place_ref, mats_ref, right_ref, row_hbm, mats_hbm, row_ref, sems):
    handed = pltpu.make_async_copy(mats_ref, mats_hbm, sems.at[2])
    handed.start()
    copies = [pltpu.make_async_copy(row_ref.at[:, slot], row_hbm.at[:, slot], sems.at[slot]) for slot in range(2)]
    blocks = rights(place_ref, right_ref)
    for slot in range(2):
        for p in range(3):
            side = slab([(pair[slot],) for pair in blocks], p)
            put([row_ref.at[n, slot] for n in range(4)], product(mats_ref, p, side, 1, scale), p)
        copies[slot].start()
    handed.wait()
    for copy in copies:
        copy.wait()


def col_kernel(scale, mats_ref, own_ref, other_ref, own_hbm, down_hbm, far_low_hbm, far_high_hbm, up_hbm, col_ref, sems):
    for slot, ref in enumerate((own_ref, other_ref)):
        for p in range(3):
            side = slab([(ref.at[n],) for n in range(4)], p)
            put([col_ref.at[n, slot] for n in range(4)], product(mats_ref, p, side, 0, scale), p)
    copies = [
        pltpu.make_async_copy(src, dst, sems.at[n])
        for n, (src, dst) in enumerate(
            (
                (col_ref.at[2, 0], far_low_hbm),
                (col_ref.at[2, 1], far_high_hbm),
                (col_ref.at[0], own_hbm),
                (col_ref.at[1], down_hbm),
                (col_ref.at[3], up_hbm),
            )
        )
    ]
    for copy in copies:
        copy.start()
    for copy in copies:
        copy.wait()


def four(refs, s):
    p = [ref[s].astype(F32) for ref in refs]
    return ((p[0] + p[1]) + (p[2] + p[3])).astype(BF16)


def relay_kernel(down_ref, up_ref, down_got_ref, up_got_ref, down_hbm, up_hbm, down_sum, up_sum, sems):
    copies = [
        pltpu.make_async_copy(down_ref.at[0], down_hbm.at[0], sems.at[0]),
        pltpu.make_async_copy(up_ref.at[1], up_hbm.at[1], sems.at[1]),
        pltpu.make_async_copy(down_sum, down_hbm.at[1], sems.at[2]),
        pltpu.make_async_copy(up_sum, up_hbm.at[0], sems.at[3]),
    ]
    copies[0].start()
    copies[1].start()
    for s in range(down_sum.shape[0]):
        down_sum[s] = (down_ref[1, s].astype(F32) + down_got_ref[s].astype(F32)).astype(BF16)
        up_sum[s] = (up_ref[0, s].astype(F32) + up_got_ref[s].astype(F32)).astype(BF16)
    copies[2].start()
    copies[3].start()
    for copy in copies:
        copy.wait()


def total_columns_kernel(own_ref, down_ref, up_ref, keep_ref, send_ref):
    for slot, out_ref in enumerate((keep_ref, send_ref)):
        for s in range(out_ref.shape[0]):
            own, down, up = (ref[slot, s].astype(F32) for ref in (own_ref, down_ref, up_ref))
            out_ref[s] = (own + down + up).astype(BF16)


def total_blocks_kernel(part_ref, keep_ref, send_ref):
    for slot, out_ref in enumerate((keep_ref, send_ref)):
        for s in range(out_ref.shape[0]):
            out_ref[s] = four([part_ref.at[n, slot] for n in range(4)], s)


def unpacked(first, keep, got):
    return halves(jnp.where(first, keep, got), jnp.where(first, got, keep))


def finish_columns_kernel(place_ref, keep_ref, got_ref, gk_ref, gv_ref):
    first = place_ref[0] == 0
    for s in range(keep_ref.shape[0]):
        gk_ref[s], gv_ref[s] = unpacked(first, keep_ref[s], got_ref[s])


def finish_rows_kernel(place_ref, keep_ref, got_ref, w_ref, mixed_ref, gq_ref):
    seqs, res, width = keep_ref.shape
    keep, got = keep_ref[...].reshape(seqs * res, width), got_ref[...].reshape(seqs * res, width)
    grad_query, attended = unpacked(place_ref[0] == 0, keep, got)
    gq_ref[...] = grad_query.reshape(seqs, res, width)
    mixed = jnp.dot(attended, w_ref[...], preferred_element_type=F32).astype(BF16)
    mixed_ref[...] = mixed.reshape(mixed_ref.shape)


def on_device(queries, keys, values, out_weight, grad_out):
    seqs, res, width = queries.shape
    model_dim = out_weight.shape[1]
    scale = 1.0 / math.sqrt(width // HEADS * seqs * 32)
    place = jnp.stack([lax.axis_index("c"), lax.axis_index("x")]).astype(jnp.int32)
    block = (seqs, res, width)
    smem = pl.BlockSpec(memory_space=pltpu.SMEM)
    vmem = pl.BlockSpec(memory_space=pltpu.VMEM)
    hbm = pl.BlockSpec(memory_space=pltpu.HBM)

    def array(shape, dtype=BF16):
        return jax.ShapeDtypeStruct(shape, dtype)

    args = (queries, keys, values, out_weight, grad_out)
    own, send, right = pl.pallas_call(
        pack_kernel,
        in_specs=[smem] + [hbm] * 5,
        out_specs=[vmem, vmem, hbm],
        out_shape=(array(block), array(block), pltpu.HBM((4, 2) + block, BF16)),
        scratch_shapes=[pltpu.VMEM(a.shape, BF16) for a in (queries, keys, values, out_weight, grad_out)]
        + [pltpu.VMEM((2,) + block, BF16), pltpu.SemaphoreType.DMA((9,))],
        compiler_params=params(),
        name="pack",
    )(place, *(pltpu.with_memory_space_constraint(arg, pltpu.HBM) for arg in args))
    right = exchange(right.reshape((8,) + block), ("x", "c")).reshape((4, 2) + block)
    other = shift(send, "c", 1)
    own = lax.all_gather(own, "zl")
    other = lax.all_gather(other, "zl")

    partial = pl.pallas_call(
        product_kernel,
        in_specs=[smem] + [vmem] * 3,
        out_shape=array((4, 6, 64, 256), F32),
        compiler_params=params(),
        name="products",
    )(place, own, other, right)
    partial = exchange(partial, "y")
    partial = pl.pallas_call(
        rows_kernel, out_shape=array((16, 24, 256), F32), compiler_params=params(), name="rows"
    )(partial)
    partial = exchange(partial, ("zh", "zl"))
    mats = pl.pallas_call(
        lambda *refs: softmax_kernel(scale, *refs),
        out_shape=array((16, 48, 128)),
        compiler_params=params(),
        name="softmax",
    )(partial)
    mats = exchange(mats, ("zh", "zl"))
    mats = pl.pallas_call(
        unpack_kernel,
        out_shape=array((4, 6, 64, 256)),
        scratch_shapes=[pltpu.VMEM((6, 64, 256), F32)],
        compiler_params=params(),
        name="unpack",
    )(mats)
    mats = exchange(mats, "y")

    row, mats = pl.pallas_call(
        lambda *refs: row_kernel(scale, *refs),
        in_specs=[smem] + [vmem] * 2,
        out_specs=[hbm] * 2,
        out_shape=(pltpu.HBM((4, 2) + block, BF16), pltpu.HBM(mats.shape, BF16)),
        scratch_shapes=[pltpu.VMEM((4, 2) + block, BF16), pltpu.SemaphoreType.DMA((3,))],
        compiler_params=params(),
        name="row_products",
    )(place, mats, right)
    pair = pltpu.HBM((2,) + block, BF16)
    single = pltpu.HBM(block, BF16)
    col, down, far_low, far_high, up = pl.pallas_call(
        lambda *refs: col_kernel(scale, *refs),
        in_specs=[vmem] * 3,
        out_specs=[hbm] * 5,
        out_shape=(pair, pair, single, single, pair),
        scratch_shapes=[pltpu.VMEM((4, 2) + block, BF16), pltpu.SemaphoreType.DMA((5,))],
        compiler_params=params(),
        name="col_products",
    )(mats, own, other)
    row = exchange(row, "zl")
    down, up = pl.pallas_call(
        relay_kernel,
        in_specs=[vmem] * 4,
        out_specs=[hbm] * 2,
        out_shape=(pair, pair),
        scratch_shapes=[pltpu.VMEM(block, BF16)] * 2 + [pltpu.SemaphoreType.DMA((4,))],
        compiler_params=params(),
        name="relay",
    )(down, up, shift(far_high, "x", -1), shift(far_low, "x", 1))
    keep, send = pl.pallas_call(
        total_columns_kernel, out_shape=(array(block), array(block)), compiler_params=params(), name="total_columns"
    )(col, shift(down, "x", -1), shift(up, "x", 1))
    grad_key, grad_value = pl.pallas_call(
        finish_columns_kernel,
        in_specs=[smem, vmem, vmem],
        out_shape=(array(block), array(block)),
        compiler_params=params(),
        name="finish_columns",
    )(place, keep, shift(send, "c", 1))
    keep, send = pl.pallas_call(
        total_blocks_kernel, out_shape=(array(block), array(block)), compiler_params=params(), name="total_rows"
    )(row)
    mixed, grad_query = pl.pallas_call(
        finish_rows_kernel,
        in_specs=[smem] + [vmem] * 3,
        out_shape=(array((seqs, res, model_dim)), array(block)),
        compiler_params=params(),
        name="finish_rows",
    )(place, keep, shift(send, "c", 1), out_weight)
    return mixed, grad_query, grad_key, grad_value


def solution(mesh):
    grid = Mesh(mesh.devices.reshape(4, 4, 2, 4, 4), ("zh", "y", "c", "x", "zl"))
    placed = P(("zh", "y", "c"), ("x", "zl"), None)
    return jax.shard_map(
        on_device,
        mesh=grid,
        in_specs=(placed, placed, placed, P(), placed),
        out_specs=(placed, placed, placed, placed),
        check_vma=False,
    )
```

```python
import math

import jax
import jax.numpy as jnp
from jax import lax
from jax.experimental import pallas as pl
from jax.experimental.pallas import tpu as pltpu
from jax.sharding import Mesh, PartitionSpec as P

HEADS = 6
F32 = jnp.float32
BF16 = jnp.bfloat16
VMEM = 16 * 1024 * 1024


def params():
    return pltpu.CompilerParams(vmem_limit_bytes=VMEM)


def exchange(blocks, axis):
    return lax.all_to_all(blocks, axis, 0, 0, tiled=True)


def shift(block, axis, by):
    n = lax.axis_size(axis)
    return lax.ppermute(block, axis, [(i, (i + by) % n) for i in range(n)])


def halves(one, two):
    half = one.shape[1] // 2
    return (
        jnp.concatenate([one[:, :half], two[:, :half]], axis=1),
        jnp.concatenate([one[:, half:], two[:, half:]], axis=1),
    )


def pack_kernel(
    place_ref, q_hbm, k_hbm, v_hbm, w_hbm, go_hbm, own_ref, send_ref, right_hbm, q_ref, k_ref, v_ref, w_ref, go_ref, kv_ref, sems
):
    loads = [
        pltpu.make_async_copy(src, dst, sems.at[n])
        for n, (src, dst) in enumerate(
            ((k_hbm, k_ref), (v_hbm, v_ref), (w_hbm, w_ref), (go_hbm, go_ref), (q_hbm, q_ref))
        )
    ]
    for load in loads:
        load.start()
    first = place_ref[0] == 0
    seqs, res, _ = q_ref.shape
    loads[0].wait()
    loads[1].wait()
    for s in range(seqs):
        kv_ref[0, s], kv_ref[1, s] = halves(k_ref[s], v_ref[s])
    stores = [pltpu.make_async_copy(kv_ref, right_hbm.at[n], sems.at[5 + n]) for n in range(4)]
    for store in stores:
        store.start()
    for load in loads[2:]:
        load.wait()
    grads = lax.dot_general(
        go_ref[...].reshape(seqs * res, go_ref.shape[2]),
        w_ref[...],
        (((1,), (1,)), ((), ())),
        preferred_element_type=F32,
    ).astype(BF16)
    for s in range(seqs):
        low, high = halves(q_ref[s], grads[s * res : (s + 1) * res])
        own_ref[s] = jnp.where(first, low, high)
        send_ref[s] = jnp.where(first, high, low)
    for store in stores:
        store.wait()


def slab(blocks, p):
    at = slice(p * 128, p * 128 + 128)
    rows = [
        jnp.concatenate([ref[s, :, at] for ref in row for s in range(ref.shape[0])], axis=1) for row in blocks
    ]
    return jnp.concatenate(rows, axis=0)


def lefts(own_ref, other_ref):
    return [(own_ref.at[n], other_ref.at[n]) for n in range(4)]


def rights(place_ref, ref):
    core = place_ref[0]
    x = [lax.rem(place_ref[1] + 4 - n, 4) for n in range(4)]
    return [(ref.at[x[n], core], ref.at[x[n], 1 - core]) for n in range(4)]


def odd_chunk(shape):
    return (lax.broadcasted_iota(jnp.int32, shape, 1) // 64) % 2 == 1


def product_kernel(place_ref, own_ref, other_ref, right_ref, out_ref):
    for p in range(3):
        left = slab(lefts(own_ref, other_ref), p)
        right = slab(rights(place_ref, right_ref), p)
        odd = odd_chunk(left.shape)
        zero = jnp.zeros_like(left)
        for parity, part in enumerate((jnp.where(odd, zero, left), jnp.where(odd, left, zero))):
            full = lax.dot_general(part, right, (((1,), (1,)), ((), ())), preferred_element_type=F32)
            out_ref[:, 2 * p + parity] = full.reshape(out_ref.shape[0], out_ref.shape[2], out_ref.shape[3])


def rows_kernel(part_ref, out_ref):
    total = (part_ref[0] + part_ref[1]) + (part_ref[2] + part_ref[3])
    for n in range(16):
        for j in range(6):
            out_ref[n, j * 4 : j * 4 + 4] = total[j, n * 4 : n * 4 + 4]


def softmax_kernel(scale, part_ref, out_ref):
    tiles = []
    for col in range(4):
        parts = [part_ref[n * 4 + col] for n in range(4)]
        tiles.append((parts[0] + parts[1]) + (parts[2] + parts[3]))
    total = jnp.concatenate(tiles, axis=1)
    logits = total[:12] * scale
    grads = total[12:]
    expo = jnp.exp(logits - jnp.max(logits, axis=-1, keepdims=True))
    weights = expo / jnp.sum(expo, axis=-1, keepdims=True)
    scores = weights * (grads - jnp.sum(weights * grads, axis=-1, keepdims=True))
    full = jnp.concatenate([scores, weights], axis=0)
    for col in range(4):
        at = col * 256
        tile = jnp.concatenate([full[:, at : at + 128], full[:, at + 128 : at + 256]], axis=0).astype(BF16)
        for n in range(col, 16, 4):
            out_ref[n] = tile


def unpack_kernel(mats_ref, out_ref, rows_ref):
    for n in range(16):
        block = mats_ref[n].astype(F32)
        for j in range(6):
            rows_ref[j, n * 4 : n * 4 + 4, 0:128] = block[j * 4 : j * 4 + 4]
            rows_ref[j, n * 4 : n * 4 + 4, 128:256] = block[24 + j * 4 : 28 + j * 4]
    full = rows_ref[...].astype(BF16)
    for n in range(out_ref.shape[0]):
        out_ref[n] = full


def product(mats_ref, p, side, contract, scale):
    even, odd = (
        lax.dot_general(
            mats_ref[:, j].reshape(256, 256), side, (((contract,), (0,)), ((), ())), preferred_element_type=F32
        )
        for j in (2 * p, 2 * p + 1)
    )
    if 2 * p < 3:
        even = even * scale
    if 2 * p + 1 < 3:
        odd = odd * scale
    return jnp.where(odd_chunk(even.shape), odd, even).astype(BF16)


def put(refs, value, p):
    for n, ref in enumerate(refs):
        seqs, res, _ = ref.shape
        for s in range(seqs):
            ref[s, :, p * 128 : p * 128 + 128] = value[n * res : (n + 1) * res, s * 128 : s * 128 + 128]


def row_kernel(scale, place_ref, mats_ref, right_ref, row_hbm, mats_hbm, row_ref, sems):
    handed = pltpu.make_async_copy(mats_ref, mats_hbm, sems.at[2])
    handed.start()
    copies = [pltpu.make_async_copy(row_ref.at[:, slot], row_hbm.at[:, slot], sems.at[slot]) for slot in range(2)]
    blocks = rights(place_ref, right_ref)
    for slot in range(2):
        for p in range(3):
            side = slab([(pair[slot],) for pair in blocks], p)
            put([row_ref.at[n, slot] for n in range(4)], product(mats_ref, p, side, 1, scale), p)
        copies[slot].start()
    handed.wait()
    for copy in copies:
        copy.wait()


def col_kernel(scale, mats_ref, own_ref, other_ref, *refs):
    col_hbms, col_ref, sems = refs[:4], refs[4], refs[5]
    for slot, ref in enumerate((own_ref, other_ref)):
        for p in range(3):
            side = slab([(ref.at[n],) for n in range(4)], p)
            put([col_ref.at[n, slot] for n in range(4)], product(mats_ref, p, side, 0, scale), p)
    copies = [pltpu.make_async_copy(col_ref.at[n], col_hbms[n], sems.at[n]) for n in range(4)]
    for copy in copies:
        copy.start()
    for copy in copies:
        copy.wait()


def four(refs, s):
    p = [ref[s].astype(F32) for ref in refs]
    return ((p[0] + p[1]) + (p[2] + p[3])).astype(BF16)


def total_kernel(zero_ref, one_ref, two_ref, three_ref, keep_ref, send_ref):
    refs = (zero_ref, one_ref, two_ref, three_ref)
    for s in range(keep_ref.shape[0]):
        keep_ref[s] = four([ref.at[0] for ref in refs], s)
        send_ref[s] = four([ref.at[1] for ref in refs], s)


def total_blocks_kernel(part_ref, keep_ref, send_ref):
    total_kernel(*[part_ref.at[n] for n in range(4)], keep_ref, send_ref)


def unpacked(first, keep, got):
    return halves(jnp.where(first, keep, got), jnp.where(first, got, keep))


def finish_columns_kernel(place_ref, keep_ref, got_ref, gk_ref, gv_ref):
    first = place_ref[0] == 0
    for s in range(keep_ref.shape[0]):
        gk_ref[s], gv_ref[s] = unpacked(first, keep_ref[s], got_ref[s])


def finish_rows_kernel(place_ref, keep_ref, got_ref, w_ref, mixed_ref, gq_ref):
    seqs, res, width = keep_ref.shape
    keep, got = keep_ref[...].reshape(seqs * res, width), got_ref[...].reshape(seqs * res, width)
    grad_query, attended = unpacked(place_ref[0] == 0, keep, got)
    gq_ref[...] = grad_query.reshape(seqs, res, width)
    mixed = jnp.dot(attended, w_ref[...], preferred_element_type=F32).astype(BF16)
    mixed_ref[...] = mixed.reshape(mixed_ref.shape)


def on_device(queries, keys, values, out_weight, grad_out):
    seqs, res, width = queries.shape
    model_dim = out_weight.shape[1]
    scale = 1.0 / math.sqrt(width // HEADS * seqs * 32)
    place = jnp.stack([lax.axis_index("c"), lax.axis_index("x")]).astype(jnp.int32)
    block = (seqs, res, width)
    smem = pl.BlockSpec(memory_space=pltpu.SMEM)
    vmem = pl.BlockSpec(memory_space=pltpu.VMEM)
    hbm = pl.BlockSpec(memory_space=pltpu.HBM)

    def array(shape, dtype=BF16):
        return jax.ShapeDtypeStruct(shape, dtype)

    args = (queries, keys, values, out_weight, grad_out)
    own, send, right = pl.pallas_call(
        pack_kernel,
        in_specs=[smem] + [hbm] * 5,
        out_specs=[vmem, vmem, hbm],
        out_shape=(array(block), array(block), pltpu.HBM((4, 2) + block, BF16)),
        scratch_shapes=[pltpu.VMEM(a.shape, BF16) for a in (queries, keys, values, out_weight, grad_out)]
        + [pltpu.VMEM((2,) + block, BF16), pltpu.SemaphoreType.DMA((9,))],
        compiler_params=params(),
        name="pack",
    )(place, *(pltpu.with_memory_space_constraint(arg, pltpu.HBM) for arg in args))
    right = exchange(right.reshape((8,) + block), ("x", "c")).reshape((4, 2) + block)
    other = shift(send, "c", 1)
    own = lax.all_gather(own, "zl")
    other = lax.all_gather(other, "zl")

    partial = pl.pallas_call(
        product_kernel,
        in_specs=[smem] + [vmem] * 3,
        out_shape=array((4, 6, 64, 256), F32),
        compiler_params=params(),
        name="products",
    )(place, own, other, right)
    partial = exchange(partial, "y")
    partial = pl.pallas_call(
        rows_kernel, out_shape=array((16, 24, 256), F32), compiler_params=params(), name="rows"
    )(partial)
    partial = exchange(partial, ("zh", "zl"))
    mats = pl.pallas_call(
        lambda *refs: softmax_kernel(scale, *refs),
        out_shape=array((16, 48, 128)),
        compiler_params=params(),
        name="softmax",
    )(partial)
    mats = exchange(mats, ("zh", "zl"))
    mats = pl.pallas_call(
        unpack_kernel,
        out_shape=array((4, 6, 64, 256)),
        scratch_shapes=[pltpu.VMEM((6, 64, 256), F32)],
        compiler_params=params(),
        name="unpack",
    )(mats)
    mats = exchange(mats, "y")

    row, mats = pl.pallas_call(
        lambda *refs: row_kernel(scale, *refs),
        in_specs=[smem] + [vmem] * 2,
        out_specs=[hbm] * 2,
        out_shape=(pltpu.HBM((4, 2) + block, BF16), pltpu.HBM(mats.shape, BF16)),
        scratch_shapes=[pltpu.VMEM((4, 2) + block, BF16), pltpu.SemaphoreType.DMA((3,))],
        compiler_params=params(),
        name="row_products",
    )(place, mats, right)
    cols = pl.pallas_call(
        lambda *refs: col_kernel(scale, *refs),
        in_specs=[vmem] * 3,
        out_specs=[hbm] * 4,
        out_shape=(pltpu.HBM((2,) + block, BF16),) * 4,
        scratch_shapes=[pltpu.VMEM((4, 2) + block, BF16), pltpu.SemaphoreType.DMA((4,))],
        compiler_params=params(),
        name="col_products",
    )(mats, own, other)
    row = exchange(row, "zl")
    cols = [cols[0]] + [shift(cols[by], "x", -by) for by in (1, 2, 3)]
    keep, send = pl.pallas_call(
        total_kernel, out_shape=(array(block), array(block)), compiler_params=params(), name="total_columns"
    )(*cols)
    grad_key, grad_value = pl.pallas_call(
        finish_columns_kernel,
        in_specs=[smem, vmem, vmem],
        out_shape=(array(block), array(block)),
        compiler_params=params(),
        name="finish_columns",
    )(place, keep, shift(send, "c", 1))
    keep, send = pl.pallas_call(
        total_blocks_kernel, out_shape=(array(block), array(block)), compiler_params=params(), name="total_rows"
    )(row)
    mixed, grad_query = pl.pallas_call(
        finish_rows_kernel,
        in_specs=[smem] + [vmem] * 3,
        out_shape=(array((seqs, res, model_dim)), array(block)),
        compiler_params=params(),
        name="finish_rows",
    )(place, keep, shift(send, "c", 1), out_weight)
    return mixed, grad_query, grad_key, grad_value


def solution(mesh):
    grid = Mesh(mesh.devices.reshape(4, 4, 2, 4, 4), ("zh", "y", "c", "x", "zl"))
    placed = P(("zh", "y", "c"), ("x", "zl"), None)
    return jax.shard_map(
        on_device,
        mesh=grid,
        in_specs=(placed, placed, placed, P(), placed),
        out_specs=(placed, placed, placed, placed),
        check_vma=False,
    )
```

```python
import math

import jax
import jax.numpy as jnp
from jax import lax
from jax.experimental import pallas as pl
from jax.experimental.pallas import tpu as pltpu
from jax.sharding import Mesh, PartitionSpec as P

HEADS = 6
F32 = jnp.float32
BF16 = jnp.bfloat16
VMEM = 16 * 1024 * 1024


def params():
    return pltpu.CompilerParams(vmem_limit_bytes=VMEM)


def exchange(blocks, axis):
    return lax.all_to_all(blocks, axis, 0, 0, tiled=True)


def shift(block, axis, by):
    n = lax.axis_size(axis)
    return lax.ppermute(block, axis, [(i, (i + by) % n) for i in range(n)])


def halves(one, two):
    half = one.shape[1] // 2
    return (
        jnp.concatenate([one[:, :half], two[:, :half]], axis=1),
        jnp.concatenate([one[:, half:], two[:, half:]], axis=1),
    )


def pack_kernel(
    place_ref, q_hbm, k_hbm, v_hbm, w_hbm, go_hbm, own_ref, send_ref, right_hbm, q_ref, k_ref, v_ref, w_ref, go_ref, kv_ref, sems
):
    loads = [
        pltpu.make_async_copy(src, dst, sems.at[n])
        for n, (src, dst) in enumerate(
            ((k_hbm, k_ref), (v_hbm, v_ref), (w_hbm, w_ref), (go_hbm, go_ref), (q_hbm, q_ref))
        )
    ]
    for load in loads:
        load.start()
    first = place_ref[0] == 0
    seqs, res, _ = q_ref.shape
    loads[0].wait()
    loads[1].wait()
    for s in range(seqs):
        kv_ref[0, s], kv_ref[1, s] = halves(k_ref[s], v_ref[s])
    stores = [pltpu.make_async_copy(kv_ref, right_hbm.at[n], sems.at[5 + n]) for n in range(4)]
    for store in stores:
        store.start()
    for load in loads[2:]:
        load.wait()
    grads = lax.dot_general(
        go_ref[...].reshape(seqs * res, go_ref.shape[2]),
        w_ref[...],
        (((1,), (1,)), ((), ())),
        preferred_element_type=F32,
    ).astype(BF16)
    for s in range(seqs):
        low, high = halves(q_ref[s], grads[s * res : (s + 1) * res])
        own_ref[s] = jnp.where(first, low, high)
        send_ref[s] = jnp.where(first, high, low)
    for store in stores:
        store.wait()


def slab(blocks, p):
    at = slice(p * 128, p * 128 + 128)
    rows = [
        jnp.concatenate([ref[s, :, at] for ref in row for s in range(ref.shape[0])], axis=1) for row in blocks
    ]
    return jnp.concatenate(rows, axis=0)


def lefts(own_ref, other_ref):
    return [(own_ref.at[n], other_ref.at[n]) for n in range(4)]


def rights(place_ref, ref):
    core = place_ref[0]
    x = [lax.rem(place_ref[1] + 4 - n, 4) for n in range(4)]
    return [(ref.at[x[n], core], ref.at[x[n], 1 - core]) for n in range(4)]


def odd_chunk(shape):
    return (lax.broadcasted_iota(jnp.int32, shape, 1) // 64) % 2 == 1


def two_terms(value):
    high = value.astype(BF16)
    return high, (value - high.astype(F32)).astype(BF16)


def product_kernel(place_ref, own_ref, other_ref, right_ref, out_ref):
    for p in range(3):
        left = slab(lefts(own_ref, other_ref), p)
        right = slab(rights(place_ref, right_ref), p)
        odd = odd_chunk(left.shape)
        zero = jnp.zeros_like(left)
        for parity, part in enumerate((jnp.where(odd, zero, left), jnp.where(odd, left, zero))):
            full = lax.dot_general(part, right, (((1,), (1,)), ((), ())), preferred_element_type=F32)
            chunk = 2 * p + parity
            for at, term in zip((chunk, chunk + 3) if chunk < 3 else (chunk + 3,), two_terms(full)):
                out_ref[:, at] = term.reshape(out_ref.shape[0], out_ref.shape[2], out_ref.shape[3])


def rows_kernel(part_ref, out_ref, rows_ref):
    def added(j):
        p = [part_ref[n, j].astype(F32) for n in range(4)]
        return (p[0] + p[1]) + (p[2] + p[3])

    for t in range(3):
        terms = [term.astype(F32) for term in two_terms(added(t) + added(t + 3))] + [added(t + 6)]
        for kind, term in enumerate(terms):
            for n in range(16):
                at = (kind * 3 + t) * 4
                rows_ref[n, at : at + 4] = term[n * 4 : n * 4 + 4, :128]
                rows_ref[n, 36 + at : 40 + at] = term[n * 4 : n * 4 + 4, 128:]
    for n in range(16):
        out_ref[n] = rows_ref[n].astype(BF16)


def softmax_kernel(scale, part_ref, out_ref):
    logits, grads = [], []
    for col in range(4):
        parts = [part_ref[n * 4 + col].astype(F32) for n in range(4)]
        total = (parts[0] + parts[1]) + (parts[2] + parts[3])
        for at in (0, 36):
            logits.append(total[at : at + 12] + total[at + 12 : at + 24])
            grads.append(total[at + 24 : at + 36])
    logits = jnp.concatenate(logits, axis=1) * scale
    grads = jnp.concatenate(grads, axis=1)
    expo = jnp.exp(logits - jnp.max(logits, axis=-1, keepdims=True))
    weights = expo / jnp.sum(expo, axis=-1, keepdims=True)
    scores = weights * (grads - jnp.sum(weights * grads, axis=-1, keepdims=True))
    full = jnp.concatenate([scores, weights], axis=0)
    for col in range(4):
        at = col * 256
        tile = jnp.concatenate([full[:, at : at + 128], full[:, at + 128 : at + 256]], axis=0).astype(BF16)
        for n in range(col, 16, 4):
            out_ref[n] = tile


def unpack_kernel(mats_ref, out_ref, rows_ref):
    for n in range(16):
        block = mats_ref[n].astype(F32)
        for j in range(6):
            rows_ref[j, n * 4 : n * 4 + 4, 0:128] = block[j * 4 : j * 4 + 4]
            rows_ref[j, n * 4 : n * 4 + 4, 128:256] = block[24 + j * 4 : 28 + j * 4]
    full = rows_ref[...].astype(BF16)
    for n in range(out_ref.shape[0]):
        out_ref[n] = full


def product(mats_ref, p, side, contract, scale):
    even, odd = (
        lax.dot_general(
            mats_ref[:, j].reshape(256, 256), side, (((contract,), (0,)), ((), ())), preferred_element_type=F32
        )
        for j in (2 * p, 2 * p + 1)
    )
    if 2 * p < 3:
        even = even * scale
    if 2 * p + 1 < 3:
        odd = odd * scale
    return jnp.where(odd_chunk(even.shape), odd, even).astype(BF16)


def put(refs, value, p):
    for n, ref in enumerate(refs):
        seqs, res, _ = ref.shape
        for s in range(seqs):
            ref[s, :, p * 128 : p * 128 + 128] = value[n * res : (n + 1) * res, s * 128 : s * 128 + 128]


def row_kernel(scale, place_ref, mats_ref, right_ref, row_hbm, mats_hbm, row_ref, sems):
    handed = pltpu.make_async_copy(mats_ref, mats_hbm, sems.at[2])
    handed.start()
    copies = [pltpu.make_async_copy(row_ref.at[:, slot], row_hbm.at[:, slot], sems.at[slot]) for slot in range(2)]
    blocks = rights(place_ref, right_ref)
    for slot in range(2):
        for p in range(3):
            side = slab([(pair[slot],) for pair in blocks], p)
            put([row_ref.at[n, slot] for n in range(4)], product(mats_ref, p, side, 1, scale), p)
        copies[slot].start()
    handed.wait()
    for copy in copies:
        copy.wait()


def col_kernel(scale, mats_ref, own_ref, other_ref, *refs):
    col_hbms, col_ref, sems = refs[:4], refs[4], refs[5]
    for slot, ref in enumerate((own_ref, other_ref)):
        for p in range(3):
            side = slab([(ref.at[n],) for n in range(4)], p)
            put([col_ref.at[n, slot] for n in range(4)], product(mats_ref, p, side, 0, scale), p)
    copies = [pltpu.make_async_copy(col_ref.at[n], col_hbms[n], sems.at[n]) for n in range(4)]
    for copy in copies:
        copy.start()
    for copy in copies:
        copy.wait()


def four(refs, s):
    p = [ref[s].astype(F32) for ref in refs]
    return ((p[0] + p[1]) + (p[2] + p[3])).astype(BF16)


def total_kernel(zero_ref, one_ref, two_ref, three_ref, keep_ref, send_ref):
    refs = (zero_ref, one_ref, two_ref, three_ref)
    for s in range(keep_ref.shape[0]):
        keep_ref[s] = four([ref.at[0] for ref in refs], s)
        send_ref[s] = four([ref.at[1] for ref in refs], s)


def total_blocks_kernel(part_ref, keep_ref, send_ref):
    total_kernel(*[part_ref.at[n] for n in range(4)], keep_ref, send_ref)


def unpacked(first, keep, got):
    return halves(jnp.where(first, keep, got), jnp.where(first, got, keep))


def finish_columns_kernel(place_ref, keep_ref, got_ref, gk_ref, gv_ref):
    first = place_ref[0] == 0
    for s in range(keep_ref.shape[0]):
        gk_ref[s], gv_ref[s] = unpacked(first, keep_ref[s], got_ref[s])


def finish_rows_kernel(place_ref, keep_ref, got_ref, w_ref, mixed_ref, gq_ref):
    seqs, res, width = keep_ref.shape
    keep, got = keep_ref[...].reshape(seqs * res, width), got_ref[...].reshape(seqs * res, width)
    grad_query, attended = unpacked(place_ref[0] == 0, keep, got)
    gq_ref[...] = grad_query.reshape(seqs, res, width)
    mixed = jnp.dot(attended, w_ref[...], preferred_element_type=F32).astype(BF16)
    mixed_ref[...] = mixed.reshape(mixed_ref.shape)


def on_device(queries, keys, values, out_weight, grad_out):
    seqs, res, width = queries.shape
    model_dim = out_weight.shape[1]
    scale = 1.0 / math.sqrt(width // HEADS * seqs * 32)
    place = jnp.stack([lax.axis_index("c"), lax.axis_index("x")]).astype(jnp.int32)
    block = (seqs, res, width)
    smem = pl.BlockSpec(memory_space=pltpu.SMEM)
    vmem = pl.BlockSpec(memory_space=pltpu.VMEM)
    hbm = pl.BlockSpec(memory_space=pltpu.HBM)

    def array(shape, dtype=BF16):
        return jax.ShapeDtypeStruct(shape, dtype)

    args = (queries, keys, values, out_weight, grad_out)
    own, send, right = pl.pallas_call(
        pack_kernel,
        in_specs=[smem] + [hbm] * 5,
        out_specs=[vmem, vmem, hbm],
        out_shape=(array(block), array(block), pltpu.HBM((4, 2) + block, BF16)),
        scratch_shapes=[pltpu.VMEM(a.shape, BF16) for a in (queries, keys, values, out_weight, grad_out)]
        + [pltpu.VMEM((2,) + block, BF16), pltpu.SemaphoreType.DMA((9,))],
        compiler_params=params(),
        name="pack",
    )(place, *(pltpu.with_memory_space_constraint(arg, pltpu.HBM) for arg in args))
    right = exchange(right.reshape((8,) + block), ("x", "c")).reshape((4, 2) + block)
    other = shift(send, "c", 1)
    own = lax.all_gather(own, "zl")
    other = lax.all_gather(other, "zl")

    partial = pl.pallas_call(
        product_kernel,
        in_specs=[smem] + [vmem] * 3,
        out_shape=array((4, 9, 64, 256)),
        compiler_params=params(),
        name="products",
    )(place, own, other, right)
    partial = exchange(partial, "y")
    partial = pl.pallas_call(
        rows_kernel,
        out_shape=array((16, 72, 128)),
        scratch_shapes=[pltpu.VMEM((16, 72, 128), F32)],
        compiler_params=params(),
        name="rows",
    )(partial)
    partial = exchange(partial, ("zh", "zl"))
    mats = pl.pallas_call(
        lambda *refs: softmax_kernel(scale, *refs),
        out_shape=array((16, 48, 128)),
        compiler_params=params(),
        name="softmax",
    )(partial)
    mats = exchange(mats, ("zh", "zl"))
    mats = pl.pallas_call(
        unpack_kernel,
        out_shape=array((4, 6, 64, 256)),
        scratch_shapes=[pltpu.VMEM((6, 64, 256), F32)],
        compiler_params=params(),
        name="unpack",
    )(mats)
    mats = exchange(mats, "y")

    row, mats = pl.pallas_call(
        lambda *refs: row_kernel(scale, *refs),
        in_specs=[smem] + [vmem] * 2,
        out_specs=[hbm] * 2,
        out_shape=(pltpu.HBM((4, 2) + block, BF16), pltpu.HBM(mats.shape, BF16)),
        scratch_shapes=[pltpu.VMEM((4, 2) + block, BF16), pltpu.SemaphoreType.DMA((3,))],
        compiler_params=params(),
        name="row_products",
    )(place, mats, right)
    cols = pl.pallas_call(
        lambda *refs: col_kernel(scale, *refs),
        in_specs=[vmem] * 3,
        out_specs=[hbm] * 4,
        out_shape=(pltpu.HBM((2,) + block, BF16),) * 4,
        scratch_shapes=[pltpu.VMEM((4, 2) + block, BF16), pltpu.SemaphoreType.DMA((4,))],
        compiler_params=params(),
        name="col_products",
    )(mats, own, other)
    row = exchange(row, "zl")
    cols = [cols[0]] + [shift(cols[by], "x", -by) for by in (1, 2, 3)]
    keep, send = pl.pallas_call(
        total_kernel, out_shape=(array(block), array(block)), compiler_params=params(), name="total_columns"
    )(*cols)
    grad_key, grad_value = pl.pallas_call(
        finish_columns_kernel,
        in_specs=[smem, vmem, vmem],
        out_shape=(array(block), array(block)),
        compiler_params=params(),
        name="finish_columns",
    )(place, keep, shift(send, "c", 1))
    keep, send = pl.pallas_call(
        total_blocks_kernel, out_shape=(array(block), array(block)), compiler_params=params(), name="total_rows"
    )(row)
    mixed, grad_query = pl.pallas_call(
        finish_rows_kernel,
        in_specs=[smem] + [vmem] * 3,
        out_shape=(array((seqs, res, model_dim)), array(block)),
        compiler_params=params(),
        name="finish_rows",
    )(place, keep, shift(send, "c", 1), out_weight)
    return mixed, grad_query, grad_key, grad_value


def solution(mesh):
    grid = Mesh(mesh.devices.reshape(4, 4, 2, 4, 4), ("zh", "y", "c", "x", "zl"))
    placed = P(("zh", "y", "c"), ("x", "zl"), None)
    return jax.shard_map(
        on_device,
        mesh=grid,
        in_specs=(placed, placed, placed, P(), placed),
        out_specs=(placed, placed, placed, placed),
        check_vma=False,
    )
```

```python
import math

import jax
import jax.numpy as jnp
from jax import lax
from jax.experimental import pallas as pl
from jax.experimental.pallas import tpu as pltpu
from jax.sharding import Mesh, PartitionSpec as P

HEADS = 6
F32 = jnp.float32
BF16 = jnp.bfloat16
VMEM = 16 * 1024 * 1024


def params():
    return pltpu.CompilerParams(vmem_limit_bytes=VMEM)


def exchange(blocks, axis):
    return lax.all_to_all(blocks, axis, 0, 0, tiled=True)


def shift(block, axis, by):
    n = lax.axis_size(axis)
    return lax.ppermute(block, axis, [(i, (i + by) % n) for i in range(n)])


def halves(one, two):
    half = one.shape[1] // 2
    return (
        jnp.concatenate([one[:, :half], two[:, :half]], axis=1),
        jnp.concatenate([one[:, half:], two[:, half:]], axis=1),
    )


def pack_kernel(
    place_ref, q_hbm, k_hbm, v_hbm, w_hbm, go_hbm, own_ref, send_ref, right_hbm, q_ref, k_ref, v_ref, w_ref, go_ref, kv_ref, sems
):
    loads = [
        pltpu.make_async_copy(src, dst, sems.at[n])
        for n, (src, dst) in enumerate(
            ((k_hbm, k_ref), (v_hbm, v_ref), (w_hbm, w_ref), (go_hbm, go_ref), (q_hbm, q_ref))
        )
    ]
    for load in loads:
        load.start()
    first = place_ref[0] == 0
    seqs, res, _ = q_ref.shape
    loads[0].wait()
    loads[1].wait()
    for s in range(seqs):
        kv_ref[0, s], kv_ref[1, s] = halves(k_ref[s], v_ref[s])
    stores = [pltpu.make_async_copy(kv_ref, right_hbm.at[n], sems.at[5 + n]) for n in range(4)]
    for store in stores:
        store.start()
    for load in loads[2:]:
        load.wait()
    grads = lax.dot_general(
        go_ref[...].reshape(seqs * res, go_ref.shape[2]),
        w_ref[...],
        (((1,), (1,)), ((), ())),
        preferred_element_type=F32,
    ).astype(BF16)
    for s in range(seqs):
        low, high = halves(q_ref[s], grads[s * res : (s + 1) * res])
        own_ref[s] = jnp.where(first, low, high)
        send_ref[s] = jnp.where(first, high, low)
    for store in stores:
        store.wait()


def slab(blocks, p):
    at = slice(p * 128, p * 128 + 128)
    rows = [
        jnp.concatenate([ref[s, :, at] for ref in row for s in range(ref.shape[0])], axis=1) for row in blocks
    ]
    return jnp.concatenate(rows, axis=0)


def lefts(own_ref, other_ref):
    return [(own_ref.at[n], other_ref.at[n]) for n in range(4)]


def rights(place_ref, ref):
    core = place_ref[0]
    x = [lax.rem(place_ref[1] + 4 - n, 4) for n in range(4)]
    return [(ref.at[x[n], core], ref.at[x[n], 1 - core]) for n in range(4)]


def odd_chunk(shape):
    return (lax.broadcasted_iota(jnp.int32, shape, 1) // 64) % 2 == 1


def two_terms(value):
    high = value.astype(BF16)
    return high, (value - high.astype(F32)).astype(BF16)


def centred(value):
    mean = jnp.sum(value, axis=1, keepdims=True) * (1.0 / value.shape[1])
    terms = [term.astype(F32) for term in two_terms(mean)]
    return terms, (value - (terms[0] + terms[1])).astype(BF16)


def lanes_of(shape):
    return lax.broadcasted_iota(jnp.int32, shape, 1)


def product_kernel(place_ref, own_ref, other_ref, right_ref, out_ref):
    means = jnp.zeros((256, 128), F32)

    def put_slab(at, value):
        out_ref[:, at] = value.reshape(out_ref.shape[0], out_ref.shape[2], out_ref.shape[3])

    for p in range(3):
        left = slab(lefts(own_ref, other_ref), p)
        right = slab(rights(place_ref, right_ref), p)
        odd = odd_chunk(left.shape)
        zero = jnp.zeros_like(left)
        for parity, part in enumerate((jnp.where(odd, zero, left), jnp.where(odd, left, zero))):
            full = lax.dot_general(part, right, (((1,), (1,)), ((), ())), preferred_element_type=F32)
            chunk = 2 * p + parity
            if chunk < 3:
                terms = zip((chunk, chunk + 3), two_terms(full))
            else:
                mean, rest = centred(full)
                terms = ((chunk + 3, rest),)
                for n, term in enumerate(mean):
                    means = jnp.where(lanes_of(means.shape) == 2 * (chunk - 3) + n, term, means)
            for at, term in terms:
                put_slab(2 * at, term[:, :128])
                put_slab(2 * at + 1, term[:, 128:])
    put_slab(18, means.astype(BF16))


def rows_kernel(part_ref, out_ref, rows_ref):
    def added(at):
        p = [part_ref[n, at].astype(F32) for n in range(4)]
        return (p[0] + p[1]) + (p[2] + p[3])

    def both(j):
        return jnp.concatenate([added(2 * j), added(2 * j + 1)], axis=1)

    sums = added(18)
    lanes = lanes_of(sums.shape)
    inner = lax.broadcasted_iota(jnp.int32, sums.shape, 0) % 4
    spread = [jnp.zeros_like(sums), jnp.zeros_like(sums)]
    for t in range(3):
        mean, rest = centred(both(t + 6) + (sums[:, 2 * t : 2 * t + 1] + sums[:, 2 * t + 1 : 2 * t + 2]))
        spread = [jnp.where(lanes == t * 4 + inner, term, rows) for term, rows in zip(mean, spread)]
        terms = [term.astype(F32) for term in two_terms(both(t) + both(t + 3))] + [rest.astype(F32)]
        for kind, term in enumerate(terms):
            for n in range(16):
                at = (kind * 3 + t) * 4
                rows_ref[n, at : at + 4] = term[n * 4 : n * 4 + 4, :128]
                rows_ref[n, 36 + at : 40 + at] = term[n * 4 : n * 4 + 4, 128:]
    for n in range(16):
        for kind in range(2):
            rows_ref[n, 72 + kind * 4 : 76 + kind * 4] = spread[kind][n * 4 : n * 4 + 4]
        out_ref[n] = rows_ref[n].astype(BF16)


def softmax_kernel(scale, part_ref, out_ref):
    logits, grads = [], []
    for col in range(4):
        parts = [part_ref[n * 4 + col].astype(F32) for n in range(4)]
        total = (parts[0] + parts[1]) + (parts[2] + parts[3])
        means = jnp.broadcast_to(jnp.sum(total[72:80], axis=0, keepdims=True), (12, 128))
        here = lanes_of(means.shape) == lax.broadcasted_iota(jnp.int32, means.shape, 0)
        mean = jnp.sum(jnp.where(here, means, 0.0), axis=1, keepdims=True)
        for at in (0, 36):
            logits.append(total[at : at + 12] + total[at + 12 : at + 24])
            grads.append(total[at + 24 : at + 36] + mean)
    logits = jnp.concatenate(logits, axis=1) * scale
    grads = jnp.concatenate(grads, axis=1)
    expo = jnp.exp(logits - jnp.max(logits, axis=-1, keepdims=True))
    weights = expo / jnp.sum(expo, axis=-1, keepdims=True)
    scores = weights * (grads - jnp.sum(weights * grads, axis=-1, keepdims=True))
    full = jnp.concatenate([scores, weights], axis=0)
    for col in range(4):
        at = col * 256
        tile = jnp.concatenate([full[:, at : at + 128], full[:, at + 128 : at + 256]], axis=0).astype(BF16)
        for n in range(col, 16, 4):
            out_ref[n] = tile


def unpack_kernel(mats_ref, out_ref, rows_ref):
    for n in range(16):
        block = mats_ref[n].astype(F32)
        for j in range(6):
            rows_ref[j, n * 4 : n * 4 + 4, 0:128] = block[j * 4 : j * 4 + 4]
            rows_ref[j, n * 4 : n * 4 + 4, 128:256] = block[24 + j * 4 : 28 + j * 4]
    full = rows_ref[...].astype(BF16)
    for n in range(out_ref.shape[0]):
        out_ref[n] = full


def product(mats_ref, p, side, contract, scale):
    even, odd = (
        lax.dot_general(
            mats_ref[:, j].reshape(256, 256), side, (((contract,), (0,)), ((), ())), preferred_element_type=F32
        )
        for j in (2 * p, 2 * p + 1)
    )
    if 2 * p < 3:
        even = even * scale
    if 2 * p + 1 < 3:
        odd = odd * scale
    return jnp.where(odd_chunk(even.shape), odd, even).astype(BF16)


def put(refs, value, p):
    for n, ref in enumerate(refs):
        seqs, res, _ = ref.shape
        for s in range(seqs):
            ref[s, :, p * 128 : p * 128 + 128] = value[n * res : (n + 1) * res, s * 128 : s * 128 + 128]


def row_kernel(scale, place_ref, mats_ref, right_ref, row_hbm, mats_hbm, row_ref, sems):
    handed = pltpu.make_async_copy(mats_ref, mats_hbm, sems.at[2])
    handed.start()
    copies = [pltpu.make_async_copy(row_ref.at[:, slot], row_hbm.at[:, slot], sems.at[slot]) for slot in range(2)]
    blocks = rights(place_ref, right_ref)
    for slot in range(2):
        for p in range(3):
            side = slab([(pair[slot],) for pair in blocks], p)
            put([row_ref.at[n, slot] for n in range(4)], product(mats_ref, p, side, 1, scale), p)
        copies[slot].start()
    handed.wait()
    for copy in copies:
        copy.wait()


def col_kernel(scale, mats_ref, own_ref, other_ref, *refs):
    col_hbms, col_ref, sems = refs[:4], refs[4], refs[5]
    for slot, ref in enumerate((own_ref, other_ref)):
        for p in range(3):
            side = slab([(ref.at[n],) for n in range(4)], p)
            put([col_ref.at[n, slot] for n in range(4)], product(mats_ref, p, side, 0, scale), p)
    copies = [pltpu.make_async_copy(col_ref.at[n], col_hbms[n], sems.at[n]) for n in range(4)]
    for copy in copies:
        copy.start()
    for copy in copies:
        copy.wait()


def four(refs, s):
    p = [ref[s].astype(F32) for ref in refs]
    return ((p[0] + p[1]) + (p[2] + p[3])).astype(BF16)


def total_kernel(zero_ref, one_ref, two_ref, three_ref, keep_ref, send_ref):
    refs = (zero_ref, one_ref, two_ref, three_ref)
    for s in range(keep_ref.shape[0]):
        keep_ref[s] = four([ref.at[0] for ref in refs], s)
        send_ref[s] = four([ref.at[1] for ref in refs], s)


def total_blocks_kernel(part_ref, keep_ref, send_ref):
    total_kernel(*[part_ref.at[n] for n in range(4)], keep_ref, send_ref)


def unpacked(first, keep, got):
    return halves(jnp.where(first, keep, got), jnp.where(first, got, keep))


def finish_columns_kernel(place_ref, keep_ref, got_ref, gk_ref, gv_ref):
    first = place_ref[0] == 0
    for s in range(keep_ref.shape[0]):
        gk_ref[s], gv_ref[s] = unpacked(first, keep_ref[s], got_ref[s])


def finish_rows_kernel(place_ref, keep_ref, got_ref, w_ref, mixed_ref, gq_ref):
    seqs, res, width = keep_ref.shape
    keep, got = keep_ref[...].reshape(seqs * res, width), got_ref[...].reshape(seqs * res, width)
    grad_query, attended = unpacked(place_ref[0] == 0, keep, got)
    gq_ref[...] = grad_query.reshape(seqs, res, width)
    mixed = jnp.dot(attended, w_ref[...], preferred_element_type=F32).astype(BF16)
    mixed_ref[...] = mixed.reshape(mixed_ref.shape)


def on_device(queries, keys, values, out_weight, grad_out):
    seqs, res, width = queries.shape
    model_dim = out_weight.shape[1]
    scale = 1.0 / math.sqrt(width // HEADS * seqs * 32)
    place = jnp.stack([lax.axis_index("c"), lax.axis_index("x")]).astype(jnp.int32)
    block = (seqs, res, width)
    smem = pl.BlockSpec(memory_space=pltpu.SMEM)
    vmem = pl.BlockSpec(memory_space=pltpu.VMEM)
    hbm = pl.BlockSpec(memory_space=pltpu.HBM)

    def array(shape, dtype=BF16):
        return jax.ShapeDtypeStruct(shape, dtype)

    args = (queries, keys, values, out_weight, grad_out)
    own, send, right = pl.pallas_call(
        pack_kernel,
        in_specs=[smem] + [hbm] * 5,
        out_specs=[vmem, vmem, hbm],
        out_shape=(array(block), array(block), pltpu.HBM((4, 2) + block, BF16)),
        scratch_shapes=[pltpu.VMEM(a.shape, BF16) for a in (queries, keys, values, out_weight, grad_out)]
        + [pltpu.VMEM((2,) + block, BF16), pltpu.SemaphoreType.DMA((9,))],
        compiler_params=params(),
        name="pack",
    )(place, *(pltpu.with_memory_space_constraint(arg, pltpu.HBM) for arg in args))
    right = exchange(right.reshape((8,) + block), ("x", "c")).reshape((4, 2) + block)
    other = shift(send, "c", 1)
    own = lax.all_gather(own, "zl")
    other = lax.all_gather(other, "zl")

    partial = pl.pallas_call(
        product_kernel,
        in_specs=[smem] + [vmem] * 3,
        out_shape=array((4, 19, 64, 128)),
        compiler_params=params(),
        name="products",
    )(place, own, other, right)
    partial = exchange(partial, "y")
    partial = pl.pallas_call(
        rows_kernel,
        out_shape=array((16, 80, 128)),
        scratch_shapes=[pltpu.VMEM((16, 80, 128), F32)],
        compiler_params=params(),
        name="rows",
    )(partial)
    partial = exchange(partial, ("zh", "zl"))
    mats = pl.pallas_call(
        lambda *refs: softmax_kernel(scale, *refs),
        out_shape=array((16, 48, 128)),
        compiler_params=params(),
        name="softmax",
    )(partial)
    mats = exchange(mats, ("zh", "zl"))
    mats = pl.pallas_call(
        unpack_kernel,
        out_shape=array((4, 6, 64, 256)),
        scratch_shapes=[pltpu.VMEM((6, 64, 256), F32)],
        compiler_params=params(),
        name="unpack",
    )(mats)
    mats = exchange(mats, "y")

    row, mats = pl.pallas_call(
        lambda *refs: row_kernel(scale, *refs),
        in_specs=[smem] + [vmem] * 2,
        out_specs=[hbm] * 2,
        out_shape=(pltpu.HBM((4, 2) + block, BF16), pltpu.HBM(mats.shape, BF16)),
        scratch_shapes=[pltpu.VMEM((4, 2) + block, BF16), pltpu.SemaphoreType.DMA((3,))],
        compiler_params=params(),
        name="row_products",
    )(place, mats, right)
    cols = pl.pallas_call(
        lambda *refs: col_kernel(scale, *refs),
        in_specs=[vmem] * 3,
        out_specs=[hbm] * 4,
        out_shape=(pltpu.HBM((2,) + block, BF16),) * 4,
        scratch_shapes=[pltpu.VMEM((4, 2) + block, BF16), pltpu.SemaphoreType.DMA((4,))],
        compiler_params=params(),
        name="col_products",
    )(mats, own, other)
    row = exchange(row, "zl")
    cols = [cols[0]] + [shift(cols[by], "x", -by) for by in (1, 2, 3)]
    keep, send = pl.pallas_call(
        total_kernel, out_shape=(array(block), array(block)), compiler_params=params(), name="total_columns"
    )(*cols)
    grad_key, grad_value = pl.pallas_call(
        finish_columns_kernel,
        in_specs=[smem, vmem, vmem],
        out_shape=(array(block), array(block)),
        compiler_params=params(),
        name="finish_columns",
    )(place, keep, shift(send, "c", 1))
    keep, send = pl.pallas_call(
        total_blocks_kernel, out_shape=(array(block), array(block)), compiler_params=params(), name="total_rows"
    )(row)
    mixed, grad_query = pl.pallas_call(
        finish_rows_kernel,
        in_specs=[smem] + [vmem] * 3,
        out_shape=(array((seqs, res, model_dim)), array(block)),
        compiler_params=params(),
        name="finish_rows",
    )(place, keep, shift(send, "c", 1), out_weight)
    return mixed, grad_query, grad_key, grad_value


def solution(mesh):
    grid = Mesh(mesh.devices.reshape(4, 4, 2, 4, 4), ("zh", "y", "c", "x", "zl"))
    placed = P(("zh", "y", "c"), ("x", "zl"), None)
    return jax.shard_map(
        on_device,
        mesh=grid,
        in_specs=(placed, placed, placed, P(), placed),
        out_specs=(placed, placed, placed, placed),
        check_vma=False,
    )
```

```python
import math

import jax
import jax.numpy as jnp
from jax import lax
from jax.experimental import pallas as pl
from jax.experimental.pallas import tpu as pltpu
from jax.sharding import Mesh, PartitionSpec as P

HEADS = 6
F32 = jnp.float32
BF16 = jnp.bfloat16
VMEM = 16 * 1024 * 1024


def params():
    return pltpu.CompilerParams(vmem_limit_bytes=VMEM)


def exchange(blocks, axis):
    return lax.all_to_all(blocks, axis, 0, 0, tiled=True)


def shift(block, axis, by):
    n = lax.axis_size(axis)
    return lax.ppermute(block, axis, [(i, (i + by) % n) for i in range(n)])


def halves(one, two):
    half = one.shape[1] // 2
    return (
        jnp.concatenate([one[:, :half], two[:, :half]], axis=1),
        jnp.concatenate([one[:, half:], two[:, half:]], axis=1),
    )


def swap(block, axis, bit):
    n = lax.axis_size(axis)
    return lax.ppermute(block, axis, [(i, i ^ bit) for i in range(n)])


def pack_kernel(
    place_ref, q_hbm, k_hbm, v_hbm, w_hbm, go_hbm, own_ref, send_ref, right_hbm, q_ref, k_ref, v_ref, w_ref, go_ref, kv_ref, sems
):
    loads = [
        pltpu.make_async_copy(src, dst, sems.at[n])
        for n, (src, dst) in enumerate(
            ((k_hbm, k_ref), (v_hbm, v_ref), (w_hbm, w_ref), (go_hbm, go_ref), (q_hbm, q_ref))
        )
    ]
    for load in loads:
        load.start()
    first = place_ref[0] == 0
    seqs, res, _ = q_ref.shape
    loads[0].wait()
    loads[1].wait()
    for s in range(seqs):
        kv_ref[0, s], kv_ref[1, s] = halves(k_ref[s], v_ref[s])
    stores = [pltpu.make_async_copy(kv_ref, right_hbm.at[n], sems.at[5 + n]) for n in range(4)]
    for store in stores:
        store.start()
    for load in loads[2:]:
        load.wait()
    grads = lax.dot_general(
        go_ref[...].reshape(seqs * res, go_ref.shape[2]),
        w_ref[...],
        (((1,), (1,)), ((), ())),
        preferred_element_type=F32,
    ).astype(BF16)
    for s in range(seqs):
        low, high = halves(q_ref[s], grads[s * res : (s + 1) * res])
        own_ref[s] = jnp.where(first, low, high)
        send_ref[s] = jnp.where(first, high, low)
    for store in stores:
        store.wait()


def slab(blocks, p):
    at = slice(p * 128, p * 128 + 128)
    rows = [
        jnp.concatenate([ref[s, :, at] for ref in row for s in range(ref.shape[0])], axis=1) for row in blocks
    ]
    return jnp.concatenate(rows, axis=0)


def lefts(own_ref, other_ref):
    return [(own_ref.at[n], other_ref.at[n]) for n in range(4)]


def rights(place_ref, ref):
    core = place_ref[0]
    x = [lax.rem(place_ref[1] + 4 - n, 4) for n in range(4)]
    return [(ref.at[x[n], core], ref.at[x[n], 1 - core]) for n in range(4)]


def odd_chunk(shape):
    return (lax.broadcasted_iota(jnp.int32, shape, 1) // 64) % 2 == 1


def two_terms(value):
    high = value.astype(BF16)
    return high, (value - high.astype(F32)).astype(BF16)


def product_kernel(place_ref, own_ref, other_ref, right_ref, out_ref):
    for p in range(3):
        left = slab(lefts(own_ref, other_ref), p)
        right = slab(rights(place_ref, right_ref), p)
        odd = odd_chunk(left.shape)
        zero = jnp.zeros_like(left)
        for parity, part in enumerate((jnp.where(odd, zero, left), jnp.where(odd, left, zero))):
            full = lax.dot_general(part, right, (((1,), (1,)), ((), ())), preferred_element_type=F32)
            chunk = 2 * p + parity
            for at, term in zip((chunk, chunk + 3) if chunk < 3 else (chunk + 3,), two_terms(full)):
                out_ref[:, at] = term.reshape(out_ref.shape[0], out_ref.shape[2], out_ref.shape[3])


def rows_kernel(part_ref, out_ref, rows_ref):
    def added(j):
        p = [part_ref[n, j].astype(F32) for n in range(4)]
        return (p[0] + p[1]) + (p[2] + p[3])

    for t in range(3):
        terms = [term.astype(F32) for term in two_terms(added(t) + added(t + 3))] + [added(t + 6)]
        for kind, term in enumerate(terms):
            for n in range(16):
                at = (kind * 3 + t) * 4
                rows_ref[n, at : at + 4] = term[n * 4 : n * 4 + 4, :128]
                rows_ref[n, 36 + at : 40 + at] = term[n * 4 : n * 4 + 4, 128:]
    for n in range(16):
        out_ref[n] = rows_ref[n].astype(BF16)


def softmax_kernel(scale, part_ref, out_ref):
    logits, grads = [], []
    for col in range(4):
        parts = [part_ref[n * 4 + col].astype(F32) for n in range(4)]
        total = (parts[0] + parts[1]) + (parts[2] + parts[3])
        for at in (0, 36):
            logits.append(total[at : at + 12] + total[at + 12 : at + 24])
            grads.append(total[at + 24 : at + 36])
    logits = jnp.concatenate(logits, axis=1) * scale
    grads = jnp.concatenate(grads, axis=1)
    expo = jnp.exp(logits - jnp.max(logits, axis=-1, keepdims=True))
    weights = expo / jnp.sum(expo, axis=-1, keepdims=True)
    scores = weights * (grads - jnp.sum(weights * grads, axis=-1, keepdims=True))
    full = jnp.concatenate([scores, weights], axis=0)
    for col in range(4):
        at = col * 256
        tile = jnp.concatenate([full[:, at : at + 128], full[:, at + 128 : at + 256]], axis=0).astype(BF16)
        for n in range(col, 16, 4):
            out_ref[n] = tile


def unpack_kernel(mats_ref, out_ref, rows_ref):
    for n in range(16):
        block = mats_ref[n].astype(F32)
        for j in range(6):
            rows_ref[j, n * 4 : n * 4 + 4, 0:128] = block[j * 4 : j * 4 + 4]
            rows_ref[j, n * 4 : n * 4 + 4, 128:256] = block[24 + j * 4 : 28 + j * 4]
    full = rows_ref[...].astype(BF16)
    for n in range(out_ref.shape[0]):
        out_ref[n] = full


def product(mats_ref, p, side, contract, scale):
    even, odd = (
        lax.dot_general(
            mats_ref[:, j].reshape(256, 256), side, (((contract,), (0,)), ((), ())), preferred_element_type=F32
        )
        for j in (2 * p, 2 * p + 1)
    )
    if 2 * p < 3:
        even = even * scale
    if 2 * p + 1 < 3:
        odd = odd * scale
    return jnp.where(odd_chunk(even.shape), odd, even).astype(BF16)


def put(refs, value, p):
    for n, ref in enumerate(refs):
        seqs, res, _ = ref.shape
        for s in range(seqs):
            ref[s, :, p * 128 : p * 128 + 128] = value[n * res : (n + 1) * res, s * 128 : s * 128 + 128]


def row_kernel(scale, place_ref, mats_ref, right_ref, own_hbm, near_hbm, mine_hbm, cross_hbm, mats_hbm, row_ref, sems):
    handed = pltpu.make_async_copy(mats_ref, mats_hbm, sems.at[0])
    handed.start()
    here = place_ref[2]
    near = here + 1 - 2 * lax.rem(here, 2)
    blocks = rights(place_ref, right_ref)
    copies = [handed]
    for slot in (1, 0):
        for p in range(3):
            side = slab([(pair[slot],) for pair in blocks], p)
            put([row_ref.at[slot, n] for n in range(4)], product(mats_ref, p, side, 1, scale), p)
        if slot == 1:
            moves = (
                (row_ref.at[1, near], near_hbm.at[0]),
                (row_ref.at[1, lax.rem(near + 2, 4)], near_hbm.at[1]),
                (row_ref.at[1, here], mine_hbm),
                (row_ref.at[1, lax.rem(here + 2, 4)], cross_hbm),
            )
        else:
            moves = ((row_ref.at[0], own_hbm),)
        for src, dst in moves:
            copy = pltpu.make_async_copy(src, dst, sems.at[len(copies)])
            copy.start()
            copies.append(copy)
    for copy in copies:
        copy.wait()


def cross_kernel(cross_ref, got_ref, out_ref):
    for s in range(out_ref.shape[0]):
        out_ref[s] = (cross_ref[s].astype(F32) + got_ref[1, s].astype(F32)).astype(BF16)


def other_rows_kernel(mine_ref, got_ref, crossed_ref, out_ref):
    for s in range(out_ref.shape[0]):
        total = mine_ref[s].astype(F32) + got_ref[0, s].astype(F32) + crossed_ref[s].astype(F32)
        out_ref[s] = total.astype(BF16)


def col_kernel(scale, mats_ref, own_ref, other_ref, *refs):
    col_hbms, col_ref, sems = refs[:4], refs[4], refs[5]
    for slot, ref in enumerate((own_ref, other_ref)):
        for p in range(3):
            side = slab([(ref.at[n],) for n in range(4)], p)
            put([col_ref.at[n, slot] for n in range(4)], product(mats_ref, p, side, 0, scale), p)
    copies = [pltpu.make_async_copy(col_ref.at[n], col_hbms[n], sems.at[n]) for n in range(4)]
    for copy in copies:
        copy.start()
    for copy in copies:
        copy.wait()


def four(refs, s):
    p = [ref[s].astype(F32) for ref in refs]
    return ((p[0] + p[1]) + (p[2] + p[3])).astype(BF16)


def total_kernel(zero_ref, one_ref, two_ref, three_ref, keep_ref, send_ref):
    refs = (zero_ref, one_ref, two_ref, three_ref)
    for s in range(keep_ref.shape[0]):
        keep_ref[s] = four([ref.at[0] for ref in refs], s)
        send_ref[s] = four([ref.at[1] for ref in refs], s)


def total_blocks_kernel(part_ref, out_ref):
    for s in range(out_ref.shape[0]):
        out_ref[s] = four([part_ref.at[n] for n in range(4)], s)


def unpacked(first, keep, got):
    return halves(jnp.where(first, keep, got), jnp.where(first, got, keep))


def finish_columns_kernel(place_ref, keep_ref, got_ref, gk_ref, gv_ref):
    first = place_ref[0] == 0
    for s in range(keep_ref.shape[0]):
        gk_ref[s], gv_ref[s] = unpacked(first, keep_ref[s], got_ref[s])


def finish_rows_kernel(place_ref, keep_ref, got_ref, w_ref, mixed_ref, gq_ref):
    seqs, res, width = keep_ref.shape
    keep, got = keep_ref[...].reshape(seqs * res, width), got_ref[...].reshape(seqs * res, width)
    grad_query, attended = unpacked(place_ref[0] == 0, keep, got)
    gq_ref[...] = grad_query.reshape(seqs, res, width)
    mixed = jnp.dot(attended, w_ref[...], preferred_element_type=F32).astype(BF16)
    mixed_ref[...] = mixed.reshape(mixed_ref.shape)


def on_device(queries, keys, values, out_weight, grad_out):
    seqs, res, width = queries.shape
    model_dim = out_weight.shape[1]
    scale = 1.0 / math.sqrt(width // HEADS * seqs * 32)
    place = jnp.stack([lax.axis_index(axis) for axis in ("c", "x", "zl")]).astype(jnp.int32)
    block = (seqs, res, width)
    smem = pl.BlockSpec(memory_space=pltpu.SMEM)
    vmem = pl.BlockSpec(memory_space=pltpu.VMEM)
    hbm = pl.BlockSpec(memory_space=pltpu.HBM)

    def array(shape, dtype=BF16):
        return jax.ShapeDtypeStruct(shape, dtype)

    args = (queries, keys, values, out_weight, grad_out)
    own, send, right = pl.pallas_call(
        pack_kernel,
        in_specs=[smem] + [hbm] * 5,
        out_specs=[vmem, vmem, hbm],
        out_shape=(array(block), array(block), pltpu.HBM((4, 2) + block, BF16)),
        scratch_shapes=[pltpu.VMEM(a.shape, BF16) for a in (queries, keys, values, out_weight, grad_out)]
        + [pltpu.VMEM((2,) + block, BF16), pltpu.SemaphoreType.DMA((9,))],
        compiler_params=params(),
        name="pack",
    )(place, *(pltpu.with_memory_space_constraint(arg, pltpu.HBM) for arg in args))
    right = exchange(right.reshape((8,) + block), ("x", "c")).reshape((4, 2) + block)
    other = shift(send, "c", 1)
    own = lax.all_gather(own, "zl")
    other = lax.all_gather(other, "zl")

    partial = pl.pallas_call(
        product_kernel,
        in_specs=[smem] + [vmem] * 3,
        out_shape=array((4, 9, 64, 256)),
        compiler_params=params(),
        name="products",
    )(place, own, other, right)
    partial = exchange(partial, "y")
    partial = pl.pallas_call(
        rows_kernel,
        out_shape=array((16, 72, 128)),
        scratch_shapes=[pltpu.VMEM((16, 72, 128), F32)],
        compiler_params=params(),
        name="rows",
    )(partial)
    partial = exchange(partial, ("zh", "zl"))
    mats = pl.pallas_call(
        lambda *refs: softmax_kernel(scale, *refs),
        out_shape=array((16, 48, 128)),
        compiler_params=params(),
        name="softmax",
    )(partial)
    mats = exchange(mats, ("zh", "zl"))
    mats = pl.pallas_call(
        unpack_kernel,
        out_shape=array((4, 6, 64, 256)),
        scratch_shapes=[pltpu.VMEM((6, 64, 256), F32)],
        compiler_params=params(),
        name="unpack",
    )(mats)
    mats = exchange(mats, "y")

    pair, single = pltpu.HBM((2,) + block, BF16), pltpu.HBM(block, BF16)
    row, near, mine, cross, mats = pl.pallas_call(
        lambda *refs: row_kernel(scale, *refs),
        in_specs=[smem] + [vmem] * 2,
        out_specs=[hbm] * 5,
        out_shape=(pltpu.HBM((4,) + block, BF16), pair, single, single, pltpu.HBM(mats.shape, BF16)),
        scratch_shapes=[pltpu.VMEM((2, 4) + block, BF16), pltpu.SemaphoreType.DMA((6,))],
        compiler_params=params(),
        name="row_products",
    )(place, mats, right)
    near = swap(near, "zl", 1)
    cols = pl.pallas_call(
        lambda *refs: col_kernel(scale, *refs),
        in_specs=[vmem] * 3,
        out_specs=[hbm] * 4,
        out_shape=(pltpu.HBM((2,) + block, BF16),) * 4,
        scratch_shapes=[pltpu.VMEM((4, 2) + block, BF16), pltpu.SemaphoreType.DMA((4,))],
        compiler_params=params(),
        name="col_products",
    )(mats, own, other)
    row = exchange(row, "zl")
    cols = [cols[0]] + [shift(cols[by], "x", -by) for by in (1, 2, 3)]
    keep, send = pl.pallas_call(
        total_kernel, out_shape=(array(block), array(block)), compiler_params=params(), name="total_columns"
    )(*cols)
    grad_key, grad_value = pl.pallas_call(
        finish_columns_kernel,
        in_specs=[smem, vmem, vmem],
        out_shape=(array(block), array(block)),
        compiler_params=params(),
        name="finish_columns",
    )(place, keep, shift(send, "c", 1))
    cross = pl.pallas_call(cross_kernel, out_shape=array(block), compiler_params=params(), name="cross")(cross, near)
    send = pl.pallas_call(
        other_rows_kernel, out_shape=array(block), compiler_params=params(), name="other_rows"
    )(mine, near, swap(cross, "zl", 2))
    keep = pl.pallas_call(
        total_blocks_kernel, out_shape=array(block), compiler_params=params(), name="total_rows"
    )(row)
    mixed, grad_query = pl.pallas_call(
        finish_rows_kernel,
        in_specs=[smem] + [vmem] * 3,
        out_shape=(array((seqs, res, model_dim)), array(block)),
        compiler_params=params(),
        name="finish_rows",
    )(place, keep, shift(send, "c", 1), out_weight)
    return mixed, grad_query, grad_key, grad_value


def solution(mesh):
    grid = Mesh(mesh.devices.reshape(4, 4, 2, 4, 4), ("zh", "y", "c", "x", "zl"))
    placed = P(("zh", "y", "c"), ("x", "zl"), None)
    return jax.shard_map(
        on_device,
        mesh=grid,
        in_specs=(placed, placed, placed, P(), placed),
        out_specs=(placed, placed, placed, placed),
        check_vma=False,
    )
```

```python
import math

import jax
import jax.numpy as jnp
from jax import lax
from jax.experimental import pallas as pl
from jax.experimental.pallas import tpu as pltpu
from jax.sharding import Mesh, PartitionSpec as P

HEADS = 6
F32 = jnp.float32
BF16 = jnp.bfloat16
VMEM = 16 * 1024 * 1024


def params():
    return pltpu.CompilerParams(vmem_limit_bytes=VMEM)


def exchange(blocks, axis):
    return lax.all_to_all(blocks, axis, 0, 0, tiled=True)


def shift(block, axis, by):
    n = lax.axis_size(axis)
    return lax.ppermute(block, axis, [(i, (i + by) % n) for i in range(n)])


def halves(one, two):
    half = one.shape[1] // 2
    return (
        jnp.concatenate([one[:, :half], two[:, :half]], axis=1),
        jnp.concatenate([one[:, half:], two[:, half:]], axis=1),
    )


def swap(block, axis, bit):
    n = lax.axis_size(axis)
    return lax.ppermute(block, axis, [(i, i ^ bit) for i in range(n)])


def pack_kernel(
    place_ref, q_hbm, k_hbm, v_hbm, w_hbm, go_hbm, own_ref, send_ref, right_hbm, q_ref, k_ref, v_ref, w_ref, go_ref, kv_ref, sems
):
    loads = [
        pltpu.make_async_copy(src, dst, sems.at[n])
        for n, (src, dst) in enumerate(
            ((k_hbm, k_ref), (v_hbm, v_ref), (w_hbm, w_ref), (go_hbm, go_ref), (q_hbm, q_ref))
        )
    ]
    for load in loads:
        load.start()
    first = place_ref[0] == 0
    seqs, res, _ = q_ref.shape
    loads[0].wait()
    loads[1].wait()
    for s in range(seqs):
        kv_ref[0, s], kv_ref[1, s] = halves(k_ref[s], v_ref[s])
    stores = [pltpu.make_async_copy(kv_ref, right_hbm.at[n], sems.at[5 + n]) for n in range(4)]
    for store in stores:
        store.start()
    for load in loads[2:]:
        load.wait()
    grads = lax.dot_general(
        go_ref[...].reshape(seqs * res, go_ref.shape[2]),
        w_ref[...],
        (((1,), (1,)), ((), ())),
        preferred_element_type=F32,
    ).astype(BF16)
    for s in range(seqs):
        low, high = halves(q_ref[s], grads[s * res : (s + 1) * res])
        own_ref[s] = jnp.where(first, low, high)
        send_ref[s] = jnp.where(first, high, low)
    for store in stores:
        store.wait()


def slab(blocks, p):
    at = slice(p * 128, p * 128 + 128)
    rows = [
        jnp.concatenate([ref[s, :, at] for ref in row for s in range(ref.shape[0])], axis=1) for row in blocks
    ]
    return jnp.concatenate(rows, axis=0)


def lefts(own_ref, other_ref):
    return [(own_ref.at[n], other_ref.at[n]) for n in range(4)]


def rights(place_ref, ref):
    core = place_ref[0]
    x = [lax.rem(place_ref[1] + 4 - n, 4) for n in range(4)]
    return [(ref.at[x[n], core], ref.at[x[n], 1 - core]) for n in range(4)]


def odd_chunk(shape):
    return (lax.broadcasted_iota(jnp.int32, shape, 1) // 64) % 2 == 1


def two_terms(value):
    high = value.astype(BF16)
    return high, (value - high.astype(F32)).astype(BF16)


def product_kernel(place_ref, own_ref, other_ref, right_ref, out_ref):
    for p in range(3):
        left = slab(lefts(own_ref, other_ref), p)
        right = slab(rights(place_ref, right_ref), p)
        odd = odd_chunk(left.shape)
        zero = jnp.zeros_like(left)
        for parity, part in enumerate((jnp.where(odd, zero, left), jnp.where(odd, left, zero))):
            full = lax.dot_general(part, right, (((1,), (1,)), ((), ())), preferred_element_type=F32)
            chunk = 2 * p + parity
            for at, term in zip((chunk, chunk + 3) if chunk < 3 else (chunk + 3,), two_terms(full)):
                out_ref[:, at] = term.reshape(out_ref.shape[0], out_ref.shape[2], out_ref.shape[3])


def rows_kernel(part_ref, out_ref, rows_ref):
    def added(j):
        p = [part_ref[n, j].astype(F32) for n in range(4)]
        return (p[0] + p[1]) + (p[2] + p[3])

    for t in range(3):
        terms = [term.astype(F32) for term in two_terms(added(t) + added(t + 3))] + [added(t + 6)]
        for kind, term in enumerate(terms):
            for n in range(16):
                at = (kind * 3 + t) * 4
                rows_ref[n, at : at + 4] = term[n * 4 : n * 4 + 4, :128]
                rows_ref[n, 36 + at : 40 + at] = term[n * 4 : n * 4 + 4, 128:]
    for n in range(16):
        out_ref[n] = rows_ref[n].astype(BF16)


def softmax_kernel(scale, part_ref, out_ref):
    logits, grads = [], []
    for col in range(4):
        parts = [part_ref[n * 4 + col].astype(F32) for n in range(4)]
        total = (parts[0] + parts[1]) + (parts[2] + parts[3])
        for at in (0, 36):
            logits.append(total[at : at + 12] + total[at + 12 : at + 24])
            grads.append(total[at + 24 : at + 36])
    logits = jnp.concatenate(logits, axis=1) * scale
    grads = jnp.concatenate(grads, axis=1)
    expo = jnp.exp(logits - jnp.max(logits, axis=-1, keepdims=True))
    weights = expo / jnp.sum(expo, axis=-1, keepdims=True)
    scores = weights * (grads - jnp.sum(weights * grads, axis=-1, keepdims=True))
    full = jnp.concatenate([scores, weights], axis=0)
    for col in range(4):
        at = col * 256
        tile = jnp.concatenate([full[:, at : at + 128], full[:, at + 128 : at + 256]], axis=0).astype(BF16)
        for n in range(col, 16, 4):
            out_ref[n] = tile


def unpack_kernel(mats_ref, out_ref, rows_ref):
    for n in range(16):
        block = mats_ref[n].astype(F32)
        for j in range(6):
            rows_ref[j, n * 4 : n * 4 + 4, 0:128] = block[j * 4 : j * 4 + 4]
            rows_ref[j, n * 4 : n * 4 + 4, 128:256] = block[24 + j * 4 : 28 + j * 4]
    full = rows_ref[...].astype(BF16)
    for n in range(out_ref.shape[0]):
        out_ref[n] = full


def product(mats_ref, p, side, contract, scale):
    even, odd = (
        lax.dot_general(
            mats_ref[:, j].reshape(256, 256), side, (((contract,), (0,)), ((), ())), preferred_element_type=F32
        )
        for j in (2 * p, 2 * p + 1)
    )
    if 2 * p < 3:
        even = even * scale
    if 2 * p + 1 < 3:
        odd = odd * scale
    return jnp.where(odd_chunk(even.shape), odd, even).astype(BF16)


def put(refs, value, p):
    for n, ref in enumerate(refs):
        seqs, res, _ = ref.shape
        for s in range(seqs):
            ref[s, :, p * 128 : p * 128 + 128] = value[n * res : (n + 1) * res, s * 128 : s * 128 + 128]


def row_kernel(scale, place_ref, mats_ref, right_ref, own_hbm, near_hbm, mine_hbm, cross_hbm, mats_hbm, row_ref, sems):
    handed = pltpu.make_async_copy(mats_ref, mats_hbm, sems.at[0])
    handed.start()
    here = place_ref[2]
    near = here + 1 - 2 * lax.rem(here, 2)
    blocks = rights(place_ref, right_ref)
    copies = [handed]
    for slot in (1, 0):
        for p in range(3):
            side = slab([(pair[slot],) for pair in blocks], p)
            put([row_ref.at[slot, n] for n in range(4)], product(mats_ref, p, side, 1, scale), p)
        if slot == 1:
            moves = (
                (row_ref.at[1, near], near_hbm.at[0]),
                (row_ref.at[1, lax.rem(near + 2, 4)], near_hbm.at[1]),
                (row_ref.at[1, here], mine_hbm),
                (row_ref.at[1, lax.rem(here + 2, 4)], cross_hbm),
            )
        else:
            moves = ((row_ref.at[0], own_hbm),)
        for src, dst in moves:
            copy = pltpu.make_async_copy(src, dst, sems.at[len(copies)])
            copy.start()
            copies.append(copy)
    for copy in copies:
        copy.wait()


def cross_kernel(cross_ref, got_ref, out_ref):
    for s in range(out_ref.shape[0]):
        out_ref[s] = (cross_ref[s].astype(F32) + got_ref[1, s].astype(F32)).astype(BF16)


def other_rows_kernel(mine_ref, got_ref, crossed_ref, out_ref):
    for s in range(out_ref.shape[0]):
        total = mine_ref[s].astype(F32) + got_ref[0, s].astype(F32) + crossed_ref[s].astype(F32)
        out_ref[s] = total.astype(BF16)


def col_kernel(scale, mats_ref, own_ref, other_ref, *refs):
    col_hbms, col_ref, sems = refs[:4], refs[4], refs[5]
    for slot, ref in enumerate((own_ref, other_ref)):
        for p in range(3):
            side = slab([(ref.at[n],) for n in range(4)], p)
            put([col_ref.at[n, slot] for n in range(4)], product(mats_ref, p, side, 0, scale), p)
    copies = [pltpu.make_async_copy(col_ref.at[n], col_hbms[n], sems.at[n]) for n in range(4)]
    for copy in copies:
        copy.start()
    for copy in copies:
        copy.wait()


def four(refs, s):
    p = [ref[s].astype(F32) for ref in refs]
    return ((p[0] + p[1]) + (p[2] + p[3])).astype(BF16)


def total_kernel(zero_ref, one_ref, two_ref, three_ref, keep_ref, send_ref):
    refs = (zero_ref, one_ref, two_ref, three_ref)
    for s in range(keep_ref.shape[0]):
        keep_ref[s] = four([ref.at[0] for ref in refs], s)
        send_ref[s] = four([ref.at[1] for ref in refs], s)


def total_blocks_kernel(part_ref, out_ref):
    for s in range(out_ref.shape[0]):
        out_ref[s] = four([part_ref.at[n] for n in range(4)], s)


def unpacked(first, keep, got):
    return halves(jnp.where(first, keep, got), jnp.where(first, got, keep))


def finish_columns_kernel(place_ref, keep_ref, got_ref, gk_ref, gv_ref):
    first = place_ref[0] == 0
    for s in range(keep_ref.shape[0]):
        gk_ref[s], gv_ref[s] = unpacked(first, keep_ref[s], got_ref[s])


def finish_rows_kernel(place_ref, keep_ref, got_ref, w_ref, mixed_ref, gq_ref):
    seqs, res, width = keep_ref.shape
    keep, got = keep_ref[...].reshape(seqs * res, width), got_ref[...].reshape(seqs * res, width)
    grad_query, attended = unpacked(place_ref[0] == 0, keep, got)
    gq_ref[...] = grad_query.reshape(seqs, res, width)
    mixed = jnp.dot(attended, w_ref[...], preferred_element_type=F32).astype(BF16)
    mixed_ref[...] = mixed.reshape(mixed_ref.shape)


def on_device(queries, keys, values, out_weight, grad_out):
    seqs, res, width = queries.shape
    model_dim = out_weight.shape[1]
    scale = 1.0 / math.sqrt(width // HEADS * seqs * 32)
    place = jnp.stack([lax.axis_index(axis) for axis in ("c", "x", "zl")]).astype(jnp.int32)
    block = (seqs, res, width)
    smem = pl.BlockSpec(memory_space=pltpu.SMEM)
    vmem = pl.BlockSpec(memory_space=pltpu.VMEM)
    hbm = pl.BlockSpec(memory_space=pltpu.HBM)

    def array(shape, dtype=BF16):
        return jax.ShapeDtypeStruct(shape, dtype)

    args = (queries, keys, values, out_weight, grad_out)
    own, send, right = pl.pallas_call(
        pack_kernel,
        in_specs=[smem] + [hbm] * 5,
        out_specs=[vmem, vmem, hbm],
        out_shape=(array(block), array(block), pltpu.HBM((4, 2) + block, BF16)),
        scratch_shapes=[pltpu.VMEM(a.shape, BF16) for a in (queries, keys, values, out_weight, grad_out)]
        + [pltpu.VMEM((2,) + block, BF16), pltpu.SemaphoreType.DMA((9,))],
        compiler_params=params(),
        name="pack",
    )(place, *(pltpu.with_memory_space_constraint(arg, pltpu.HBM) for arg in args))
    right = exchange(right.reshape((8,) + block), ("x", "c")).reshape((4, 2) + block)
    other = shift(send, "c", 1)
    own = lax.all_gather(own, "zl")
    other = lax.all_gather(other, "zl")

    partial = pl.pallas_call(
        product_kernel,
        in_specs=[smem] + [vmem] * 3,
        out_shape=array((4, 9, 64, 256)),
        compiler_params=params(),
        name="products",
    )(place, own, other, right)
    partial = exchange(partial, "y")
    partial = pl.pallas_call(
        rows_kernel,
        out_shape=array((16, 72, 128)),
        scratch_shapes=[pltpu.VMEM((16, 72, 128), F32)],
        compiler_params=params(),
        name="rows",
    )(partial)
    partial = exchange(partial, ("zh", "zl"))
    mats = pl.pallas_call(
        lambda *refs: softmax_kernel(scale, *refs),
        out_shape=array((16, 48, 128)),
        compiler_params=params(),
        name="softmax",
    )(partial)
    mats = exchange(mats, ("zh", "zl"))
    mats = pl.pallas_call(
        unpack_kernel,
        out_shape=array((4, 6, 64, 256)),
        scratch_shapes=[pltpu.VMEM((6, 64, 256), F32)],
        compiler_params=params(),
        name="unpack",
    )(mats)
    mats = exchange(mats, "y")

    pair, single = pltpu.HBM((2,) + block, BF16), pltpu.HBM(block, BF16)
    row, near, mine, cross, mats = pl.pallas_call(
        lambda *refs: row_kernel(scale, *refs),
        in_specs=[smem] + [vmem] * 2,
        out_specs=[hbm] * 5,
        out_shape=(pltpu.HBM((4,) + block, BF16), pair, single, single, pltpu.HBM(mats.shape, BF16)),
        scratch_shapes=[pltpu.VMEM((2, 4) + block, BF16), pltpu.SemaphoreType.DMA((6,))],
        compiler_params=params(),
        name="row_products",
    )(place, mats, right)
    near = swap(near, "zl", 1)
    cols = pl.pallas_call(
        lambda *refs: col_kernel(scale, *refs),
        in_specs=[vmem] * 3,
        out_specs=[hbm] * 4,
        out_shape=(pltpu.HBM((2,) + block, BF16),) * 4,
        scratch_shapes=[pltpu.VMEM((4, 2) + block, BF16), pltpu.SemaphoreType.DMA((4,))],
        compiler_params=params(),
        name="col_products",
    )(mats, own, other)
    row = exchange(row, "zl")
    cols = [cols[0]] + [shift(cols[by], "x", -by) for by in (1, 2, 3)]
    cross = pl.pallas_call(cross_kernel, out_shape=array(block), compiler_params=params(), name="cross")(cross, near)
    send_rows = pl.pallas_call(
        other_rows_kernel, out_shape=array(block), compiler_params=params(), name="other_rows"
    )(mine, near, swap(cross, "zl", 2))
    got_rows, cols = lax.optimization_barrier((shift(send_rows, "c", 1), cols))
    keep, send = pl.pallas_call(
        total_kernel, out_shape=(array(block), array(block)), compiler_params=params(), name="total_columns"
    )(*cols)
    got_columns = shift(send, "c", 1)
    keep_rows = pl.pallas_call(
        total_blocks_kernel, out_shape=array(block), compiler_params=params(), name="total_rows"
    )(row)
    mixed, grad_query = pl.pallas_call(
        finish_rows_kernel,
        in_specs=[smem] + [vmem] * 3,
        out_shape=(array((seqs, res, model_dim)), array(block)),
        compiler_params=params(),
        name="finish_rows",
    )(place, keep_rows, got_rows, out_weight)
    got_columns, mixed, grad_query = lax.optimization_barrier((got_columns, mixed, grad_query))
    grad_key, grad_value = pl.pallas_call(
        finish_columns_kernel,
        in_specs=[smem, vmem, vmem],
        out_shape=(array(block), array(block)),
        compiler_params=params(),
        name="finish_columns",
    )(place, keep, got_columns)
    return mixed, grad_query, grad_key, grad_value


def solution(mesh):
    grid = Mesh(mesh.devices.reshape(4, 4, 2, 4, 4), ("zh", "y", "c", "x", "zl"))
    placed = P(("zh", "y", "c"), ("x", "zl"), None)
    return jax.shard_map(
        on_device,
        mesh=grid,
        in_specs=(placed, placed, placed, P(), placed),
        out_specs=(placed, placed, placed, placed),
        check_vma=False,
    )
```

```python
import math

import jax
import jax.numpy as jnp
from jax import lax
from jax.experimental import pallas as pl
from jax.experimental.pallas import tpu as pltpu
from jax.sharding import Mesh, PartitionSpec as P

HEADS = 6
F32 = jnp.float32
BF16 = jnp.bfloat16
VMEM = 16 * 1024 * 1024


def params():
    return pltpu.CompilerParams(vmem_limit_bytes=VMEM)


def exchange(blocks, axis):
    return lax.all_to_all(blocks, axis, 0, 0, tiled=True)


def shift(block, axis, by):
    n = lax.axis_size(axis)
    return lax.ppermute(block, axis, [(i, (i + by) % n) for i in range(n)])


def halves(one, two):
    half = one.shape[1] // 2
    return (
        jnp.concatenate([one[:, :half], two[:, :half]], axis=1),
        jnp.concatenate([one[:, half:], two[:, half:]], axis=1),
    )


def swap(block, axis, bit):
    n = lax.axis_size(axis)
    return lax.ppermute(block, axis, [(i, i ^ bit) for i in range(n)])


def pack_kernel(
    place_ref, q_hbm, k_hbm, v_hbm, w_hbm, go_hbm, own_ref, send_ref, right_hbm, q_ref, k_ref, v_ref, w_ref, go_ref, kv_ref, sems
):
    loads = [
        pltpu.make_async_copy(src, dst, sems.at[n])
        for n, (src, dst) in enumerate(
            ((k_hbm, k_ref), (v_hbm, v_ref), (w_hbm, w_ref), (go_hbm, go_ref), (q_hbm, q_ref))
        )
    ]
    for load in loads:
        load.start()
    first = place_ref[0] == 0
    seqs, res, _ = q_ref.shape
    loads[0].wait()
    loads[1].wait()
    for s in range(seqs):
        kv_ref[0, s], kv_ref[1, s] = halves(k_ref[s], v_ref[s])
    stores = [pltpu.make_async_copy(kv_ref, right_hbm.at[n], sems.at[5 + n]) for n in range(4)]
    for store in stores:
        store.start()
    for load in loads[2:]:
        load.wait()
    grads = lax.dot_general(
        go_ref[...].reshape(seqs * res, go_ref.shape[2]),
        w_ref[...],
        (((1,), (1,)), ((), ())),
        preferred_element_type=F32,
    ).astype(BF16)
    for s in range(seqs):
        low, high = halves(q_ref[s], grads[s * res : (s + 1) * res])
        own_ref[s] = jnp.where(first, low, high)
        send_ref[s] = jnp.where(first, high, low)
    for store in stores:
        store.wait()


def slab(blocks, p):
    at = slice(p * 128, p * 128 + 128)
    rows = [
        jnp.concatenate([ref[s, :, at] for ref in row for s in range(ref.shape[0])], axis=1) for row in blocks
    ]
    return jnp.concatenate(rows, axis=0)


def lefts(own_ref, other_ref):
    return [(own_ref.at[n], other_ref.at[n]) for n in range(4)]


def rights(place_ref, ref):
    core = place_ref[0]
    x = [lax.rem(place_ref[1] + 4 - n, 4) for n in range(4)]
    return [(ref.at[x[n], core], ref.at[x[n], 1 - core]) for n in range(4)]


def odd_chunk(shape):
    return (lax.broadcasted_iota(jnp.int32, shape, 1) // 64) % 2 == 1


def two_terms(value):
    high = value.astype(BF16)
    return high, (value - high.astype(F32)).astype(BF16)


def product_kernel(place_ref, own_ref, other_ref, right_ref, out_ref):
    for p in range(3):
        left = slab(lefts(own_ref, other_ref), p)
        right = slab(rights(place_ref, right_ref), p)
        odd = odd_chunk(left.shape)
        zero = jnp.zeros_like(left)
        for parity, part in enumerate((jnp.where(odd, zero, left), jnp.where(odd, left, zero))):
            full = lax.dot_general(part, right, (((1,), (1,)), ((), ())), preferred_element_type=F32)
            chunk = 2 * p + parity
            for at, term in zip((chunk, chunk + 3) if chunk < 3 else (chunk + 3,), two_terms(full)):
                out_ref[:, at] = term.reshape(out_ref.shape[0], out_ref.shape[2], out_ref.shape[3])


def rows_kernel(part_ref, out_ref, rows_ref):
    def added(j):
        p = [part_ref[n, j].astype(F32) for n in range(4)]
        return (p[0] + p[1]) + (p[2] + p[3])

    for t in range(3):
        terms = [term.astype(F32) for term in two_terms(added(t) + added(t + 3))] + [added(t + 6)]
        for kind, term in enumerate(terms):
            for n in range(16):
                at = (kind * 3 + t) * 4
                rows_ref[n, at : at + 4] = term[n * 4 : n * 4 + 4, :128]
                rows_ref[n, 36 + at : 40 + at] = term[n * 4 : n * 4 + 4, 128:]
    for n in range(16):
        out_ref[n] = rows_ref[n].astype(BF16)


def softmax_kernel(scale, part_ref, out_ref):
    logits, grads = [], []
    for col in range(4):
        parts = [part_ref[n * 4 + col].astype(F32) for n in range(4)]
        total = (parts[0] + parts[1]) + (parts[2] + parts[3])
        for at in (0, 36):
            logits.append(total[at : at + 12] + total[at + 12 : at + 24])
            grads.append(total[at + 24 : at + 36])
    logits = jnp.concatenate(logits, axis=1) * scale
    grads = jnp.concatenate(grads, axis=1)
    expo = jnp.exp(logits - jnp.max(logits, axis=-1, keepdims=True))
    weights = expo / jnp.sum(expo, axis=-1, keepdims=True)
    scores = weights * (grads - jnp.sum(weights * grads, axis=-1, keepdims=True))
    full = jnp.concatenate([scores, weights], axis=0)
    for col in range(4):
        at = col * 256
        tile = jnp.concatenate([full[:, at : at + 128], full[:, at + 128 : at + 256]], axis=0).astype(BF16)
        for n in range(col, 16, 4):
            out_ref[n] = tile


def unpack_kernel(mats_ref, out_ref, rows_ref):
    for n in range(16):
        block = mats_ref[n].astype(F32)
        for j in range(6):
            rows_ref[j, n * 4 : n * 4 + 4, 0:128] = block[j * 4 : j * 4 + 4]
            rows_ref[j, n * 4 : n * 4 + 4, 128:256] = block[24 + j * 4 : 28 + j * 4]
    full = rows_ref[...].astype(BF16)
    for n in range(out_ref.shape[0]):
        out_ref[n] = full


def product(mats_ref, p, side, contract, scale):
    even, odd = (
        lax.dot_general(
            mats_ref[:, j].reshape(256, 256), side, (((contract,), (0,)), ((), ())), preferred_element_type=F32
        )
        for j in (2 * p, 2 * p + 1)
    )
    if 2 * p < 3:
        even = even * scale
    if 2 * p + 1 < 3:
        odd = odd * scale
    return jnp.where(odd_chunk(even.shape), odd, even).astype(BF16)


def put(refs, value, p):
    for n, ref in enumerate(refs):
        seqs, res, _ = ref.shape
        for s in range(seqs):
            ref[s, :, p * 128 : p * 128 + 128] = value[n * res : (n + 1) * res, s * 128 : s * 128 + 128]


def row_kernel(scale, place_ref, mats_ref, right_ref, own_hbm, near_hbm, mine_hbm, cross_hbm, mats_hbm, row_ref, sems):
    handed = pltpu.make_async_copy(mats_ref, mats_hbm, sems.at[0])
    handed.start()
    here = place_ref[2]
    near = here + 1 - 2 * lax.rem(here, 2)
    blocks = rights(place_ref, right_ref)
    copies = [handed]
    for slot in (1, 0):
        for p in range(3):
            side = slab([(pair[slot],) for pair in blocks], p)
            put([row_ref.at[slot, n] for n in range(4)], product(mats_ref, p, side, 1, scale), p)
        if slot == 1:
            moves = (
                (row_ref.at[1, near], near_hbm.at[0]),
                (row_ref.at[1, lax.rem(near + 2, 4)], near_hbm.at[1]),
                (row_ref.at[1, here], mine_hbm),
                (row_ref.at[1, lax.rem(here + 2, 4)], cross_hbm),
            )
        else:
            moves = ((row_ref.at[0], own_hbm),)
        for src, dst in moves:
            copy = pltpu.make_async_copy(src, dst, sems.at[len(copies)])
            copy.start()
            copies.append(copy)
    for copy in copies:
        copy.wait()


def cross_kernel(cross_ref, got_ref, out_ref):
    for s in range(out_ref.shape[0]):
        out_ref[s] = (cross_ref[s].astype(F32) + got_ref[1, s].astype(F32)).astype(BF16)


def col_kernel(scale, mats_ref, own_ref, other_ref, *refs):
    col_hbms, col_ref, sems = refs[:4], refs[4], refs[5]
    for slot, ref in enumerate((own_ref, other_ref)):
        for p in range(3):
            side = slab([(ref.at[n],) for n in range(4)], p)
            put([col_ref.at[n, slot] for n in range(4)], product(mats_ref, p, side, 0, scale), p)
    copies = [pltpu.make_async_copy(col_ref.at[n], col_hbms[n], sems.at[n]) for n in range(4)]
    for copy in copies:
        copy.start()
    for copy in copies:
        copy.wait()


def four(refs, s):
    p = [ref[s].astype(F32) for ref in refs]
    return ((p[0] + p[1]) + (p[2] + p[3])).astype(BF16)


def trade_kernel(zero_ref, one_ref, two_ref, three_ref, mine_ref, got_ref, crossed_ref, keep_ref, send_ref):
    refs = (zero_ref, one_ref, two_ref, three_ref)
    for s in range(keep_ref.shape[0]):
        keep_ref[s] = four([ref.at[0] for ref in refs], s)
        send_ref[0, s] = four([ref.at[1] for ref in refs], s)
        total = mine_ref[s].astype(F32) + got_ref[0, s].astype(F32) + crossed_ref[s].astype(F32)
        send_ref[1, s] = total.astype(BF16)


def unpacked(first, keep, got):
    return halves(jnp.where(first, keep, got), jnp.where(first, got, keep))


def finish_kernel(place_ref, row_ref, keep_ref, got_ref, w_ref, mixed_ref, gq_ref, gk_ref, gv_ref):
    first = place_ref[0] == 0
    attended = []
    for s in range(keep_ref.shape[0]):
        gk_ref[s], gv_ref[s] = unpacked(first, keep_ref[s], got_ref[0, s])
        rows = four([row_ref.at[n] for n in range(4)], s)
        gq_ref[s], one = unpacked(first, rows, got_ref[1, s])
        attended.append(one)
    mixed = jnp.dot(jnp.concatenate(attended, axis=0), w_ref[...], preferred_element_type=F32).astype(BF16)
    mixed_ref[...] = mixed.reshape(mixed_ref.shape)


def on_device(queries, keys, values, out_weight, grad_out):
    seqs, res, width = queries.shape
    model_dim = out_weight.shape[1]
    scale = 1.0 / math.sqrt(width // HEADS * seqs * 32)
    place = jnp.stack([lax.axis_index(axis) for axis in ("c", "x", "zl")]).astype(jnp.int32)
    block = (seqs, res, width)
    smem = pl.BlockSpec(memory_space=pltpu.SMEM)
    vmem = pl.BlockSpec(memory_space=pltpu.VMEM)
    hbm = pl.BlockSpec(memory_space=pltpu.HBM)

    def array(shape, dtype=BF16):
        return jax.ShapeDtypeStruct(shape, dtype)

    args = (queries, keys, values, out_weight, grad_out)
    own, send, right = pl.pallas_call(
        pack_kernel,
        in_specs=[smem] + [hbm] * 5,
        out_specs=[vmem, vmem, hbm],
        out_shape=(array(block), array(block), pltpu.HBM((4, 2) + block, BF16)),
        scratch_shapes=[pltpu.VMEM(a.shape, BF16) for a in (queries, keys, values, out_weight, grad_out)]
        + [pltpu.VMEM((2,) + block, BF16), pltpu.SemaphoreType.DMA((9,))],
        compiler_params=params(),
        name="pack",
    )(place, *(pltpu.with_memory_space_constraint(arg, pltpu.HBM) for arg in args))
    right = exchange(right.reshape((8,) + block), ("x", "c")).reshape((4, 2) + block)
    other = shift(send, "c", 1)
    own = lax.all_gather(own, "zl")
    other = lax.all_gather(other, "zl")

    partial = pl.pallas_call(
        product_kernel,
        in_specs=[smem] + [vmem] * 3,
        out_shape=array((4, 9, 64, 256)),
        compiler_params=params(),
        name="products",
    )(place, own, other, right)
    partial = exchange(partial, "y")
    partial = pl.pallas_call(
        rows_kernel,
        out_shape=array((16, 72, 128)),
        scratch_shapes=[pltpu.VMEM((16, 72, 128), F32)],
        compiler_params=params(),
        name="rows",
    )(partial)
    partial = exchange(partial, ("zh", "zl"))
    mats = pl.pallas_call(
        lambda *refs: softmax_kernel(scale, *refs),
        out_shape=array((16, 48, 128)),
        compiler_params=params(),
        name="softmax",
    )(partial)
    mats = exchange(mats, ("zh", "zl"))
    mats = pl.pallas_call(
        unpack_kernel,
        out_shape=array((4, 6, 64, 256)),
        scratch_shapes=[pltpu.VMEM((6, 64, 256), F32)],
        compiler_params=params(),
        name="unpack",
    )(mats)
    mats = exchange(mats, "y")

    pair, single = pltpu.HBM((2,) + block, BF16), pltpu.HBM(block, BF16)
    row, near, mine, cross, mats = pl.pallas_call(
        lambda *refs: row_kernel(scale, *refs),
        in_specs=[smem] + [vmem] * 2,
        out_specs=[hbm] * 5,
        out_shape=(pltpu.HBM((4,) + block, BF16), pair, single, single, pltpu.HBM(mats.shape, BF16)),
        scratch_shapes=[pltpu.VMEM((2, 4) + block, BF16), pltpu.SemaphoreType.DMA((6,))],
        compiler_params=params(),
        name="row_products",
    )(place, mats, right)
    near = swap(near, "zl", 1)
    cols = pl.pallas_call(
        lambda *refs: col_kernel(scale, *refs),
        in_specs=[vmem] * 3,
        out_specs=[hbm] * 4,
        out_shape=(pltpu.HBM((2,) + block, BF16),) * 4,
        scratch_shapes=[pltpu.VMEM((4, 2) + block, BF16), pltpu.SemaphoreType.DMA((4,))],
        compiler_params=params(),
        name="col_products",
    )(mats, own, other)
    row = exchange(row, "zl")
    cols = [cols[0]] + [shift(cols[by], "x", -by) for by in (1, 2, 3)]
    cross = pl.pallas_call(cross_kernel, out_shape=array(block), compiler_params=params(), name="cross")(cross, near)
    keep, send = pl.pallas_call(
        trade_kernel, out_shape=(array(block), array((2,) + block)), compiler_params=params(), name="trade"
    )(*cols, mine, near, swap(cross, "zl", 2))
    return pl.pallas_call(
        finish_kernel,
        in_specs=[smem] + [vmem] * 4,
        out_shape=(array((seqs, res, model_dim)), array(block), array(block), array(block)),
        compiler_params=params(),
        name="finish",
    )(place, row, keep, shift(send, "c", 1), out_weight)


def solution(mesh):
    grid = Mesh(mesh.devices.reshape(4, 4, 2, 4, 4), ("zh", "y", "c", "x", "zl"))
    placed = P(("zh", "y", "c"), ("x", "zl"), None)
    return jax.shard_map(
        on_device,
        mesh=grid,
        in_specs=(placed, placed, placed, P(), placed),
        out_specs=(placed, placed, placed, placed),
        check_vma=False,
    )
```
